32 devices in a mesh: dp: 16 (over z, x, core), mp: 2 (over y).
Axes of the slice: x: 2, y: 2, z: 4, core: 2. Of those that a mesh axis runs over, the one named last changes fastest.
Arguments:
- tokens: bfloat16 [16384, 1024], P('dp'), may hold values from -6 to 6
- cotangent: bfloat16 [16384, 1024], P('dp')
- proj_qkv: float32 [3, 1024, 1024], P(None, 'dp', 'mp'), may hold values from -0.1875 to 0.1875
- proj_out: float32 [1024, 1024], P('mp', 'dp'), may hold values from -4 to 4
- proj_gate_up: float32 [2, 1024, 2816], P(None, 'dp', 'mp'), may hold values from -0.1875 to 0.1875
- proj_down: float32 [2816, 1024], P('mp', 'dp'), may hold values from -0.109375 to 0.109375
- norm_gains: float32 [2, 1024], P(None, 'dp'), may hold values from 0.5 to 1.5
- first_qkv: float32 [3, 1024, 1024], P(None, 'dp', 'mp'), may hold values from -160 to 160
- first_out: float32 [1024, 1024], P('mp', 'dp'), may hold values from -6 to 6
- first_gate_up: float32 [2, 1024, 2816], P(None, 'dp', 'mp'), may hold values from -48 to 48
- first_down: float32 [2816, 1024], P('mp', 'dp'), may hold values from -96 to 96
- first_gains: float32 [2, 1024], P(None, 'dp'), may hold values from -160 to 160
- second_qkv: float32 [3, 1024, 1024], P(None, 'dp', 'mp'), may hold values from 3440.64 to 13762.56
- second_out: float32 [1024, 1024], P('mp', 'dp'), may hold values from 6.72 to 27.2
- second_gate_up: float32 [2, 1024, 2816], P(None, 'dp', 'mp'), may hold values from 311.296 to 1245.184
- second_down: float32 [2816, 1024], P('mp', 'dp'), may hold values from 1048.576 to 4096
- second_gains: float32 [2, 1024], P(None, 'dp'), may hold values from 3440.64 to 13762.56
- cache: bfloat16 [16384, 2, 1024], P('dp', None, 'mp'), may hold values from -6 to 6
- doc_segments: int32 [3], replicated, may hold values from 1 to 4, as said below
- padding: int32 [16384], replicated, may hold values from 0 to 1, as said below
- retrieval: int32 [16, 128], P('dp'), may hold values from 0 to 1023
Outputs:
- block_out: bfloat16 [16384, 1024], P('dp')
- input_grad: bfloat16 [16384, 1024], P('dp')
- qkv_first: float32 [3, 1024, 1024], P(None, 'dp', 'mp')
- qkv_second: float32 [3, 1024, 1024], P(None, 'dp', 'mp')
- qkv_new: float32 [3, 1024, 1024], P(None, 'dp', 'mp')
- out_first: float32 [1024, 1024], P('mp', 'dp')
- out_second: float32 [1024, 1024], P('mp', 'dp')
- out_new: float32 [1024, 1024], P('mp', 'dp')
- gate_up_first: float32 [2, 1024, 2816], P(None, 'dp', 'mp')
- gate_up_second: float32 [2, 1024, 2816], P(None, 'dp', 'mp')
- gate_up_new: float32 [2, 1024, 2816], P(None, 'dp', 'mp')
- down_first: float32 [2816, 1024], P('mp', 'dp')
- down_second: float32 [2816, 1024], P('mp', 'dp')
- down_new: float32 [2816, 1024], P('mp', 'dp')
- gains_first: float32 [2, 1024], P(None, 'dp')
- gains_second: float32 [2, 1024], P(None, 'dp')
- gains_new: float32 [2, 1024], P(None, 'dp')
The draws below stay inside these ranges and needn't reach their ends.
Inputs may be any that keep to these rules, and one draw needn't show every extreme that they name: `doc_segments`: segment counts of 3 consecutive documents, summing to 8; one document has exactly 4. `padding`: zeros only at the tail of each document's last segment: 1 to 1024 tokens, at most half of that segment.
All inputs are finite; a program needn't handle non-finite values.
Results may differ from the reference program's by a relative error of at most 0.017.
The reference program's roundings to bfloat16 on the way count: a program that leaves them out, or rounds other values in their place, can miss the bound.
Values may be sent and summed in bfloat16 or wider, within the bound.
No kernel may reach another device: no remote copies, remote signals or barrier semaphores. Data moves between devices by JAX's collectives and lax.ppermute only.
A program may use at most 192 MiB of HBM per device.

```python
import math
import jax
import jax.numpy as jnp
from jax import lax

D = 1024
HEADS = 8
HEAD_DIM = 128
FF = 2816
TOK_DEV = 1024
CACHE_DEV = 1024
SEG = 2048
RETR = 128
STEP = 10
TOKENS = 16384
NSEG = 8
SPAN = 2
N_DP = 16


def doc_layout(key):
    base = jax.random.fold_in(key, 101)
    key_big, key_split, key_pads = jax.random.split(base, 3)
    longest = NSEG // 2
    remain = NSEG - longest
    biggest = jax.random.randint(key_big, (), 0, 3)
    first_share = jax.random.randint(key_split, (), 1, remain)
    places = jnp.arange(3, dtype=jnp.int32)
    order = places - (places > biggest).astype(jnp.int32)
    counts = jnp.where(places == biggest, longest, jnp.where(order == 0, first_share, remain - first_share))
    pads = jax.random.randint(key_pads, (3,), 1, SEG // 2 + 1)
    return (counts.astype(jnp.int32), pads.astype(jnp.int32))


def draw_doc_segments(key, part):
    counts, pads = doc_layout(key)
    return counts


def draw_padding(key, part):
    counts, pads = doc_layout(key)
    token_ids = jnp.arange(TOKENS, dtype=jnp.int32)
    segment = token_ids // SEG
    place = token_ids % SEG
    ends = jnp.cumsum(counts)
    document = jnp.sum((segment[:, None] >= ends[None, :]).astype(jnp.int32), axis=1)
    last_segment = ends[document] - 1
    pad_length = pads[document]
    padded = (segment == last_segment) & (place >= SEG - pad_length)
    return jnp.where(padded, 0, 1).astype(jnp.int32)


def draw_cotangent(key, part):
    key = jax.random.fold_in(key, 7)
    ramp = jnp.arange(TOKENS, dtype=jnp.float32)[:, None] / TOKENS
    values = jax.random.normal(key, (TOKENS, D), jnp.float32) * (1.0 + 2.0 * ramp)
    return values.astype(jnp.bfloat16)


def with_ends(result, rng, smallest, high):
    shape = result.shape
    index_at = [jax.random.randint(jax.random.fold_in(rng, axis), (), 0, shape[axis]) for axis in range(len(shape))]
    result = result.at[tuple(index_at)].set(smallest)
    longest = shape.index(max(shape))
    index_at[longest] = (index_at[longest] + 1) % shape[longest]
    return result.at[tuple(index_at)].set(high)


def block_scale(stream_key, dims, cuts, least, largest):
    def one(position, blocks):
        steps = jax.random.uniform(jax.random.fold_in(jax.random.fold_in(stream_key, 6), position), (blocks,), jnp.float32, least / len(cuts), largest / len(cuts))
        return jnp.repeat(jnp.exp(steps), dims[position] // blocks).reshape((-1,) + (1,) * (len(dims) - position - 1))

    loudness = one(*cuts[0])
    for cut in cuts[1:]:
        loudness = loudness * one(*cut)
    return loudness


def scatter_about(key, extent, deviation, most, cuts=(), held_as=jnp.bfloat16):
    drawn = jax.random.normal(key, extent, jnp.float32) * deviation
    if len(cuts) > 0:
        drawn = block_scale(key, extent, cuts, -0.22, 0.18) * drawn
    return jnp.clip(drawn, min=-most, max=most).astype(held_as)


def setup_inputs(seed: int = 0) -> dict:
    key_of = jax.random.split(jax.random.key(seed), 22)
    return {
        "tokens": scatter_about(key_of[0], (TOKENS, D), 1.0, 6.0, ((0, 16),)),
        "cotangent": draw_cotangent(jax.random.fold_in(key_of[21], 71), 0),
        "proj_qkv": scatter_about(key_of[2], (3, D, D), D ** -0.5, 0.1875, ((1, 16), (2, 2)), jnp.float32),
        "proj_out": scatter_about(key_of[3], (D, D), (max(1, 4 * D // SEG)) ** -0.5, 4.0, ((0, 2), (1, 16)), jnp.float32),
        "proj_gate_up": scatter_about(key_of[4], (2, D, FF), D ** -0.5, 0.1875, ((1, 16), (2, 2)), jnp.float32),
        "proj_down": scatter_about(key_of[5], (FF, D), FF ** -0.5, 0.109375, ((0, 2), (1, 16)), jnp.float32),
        "norm_gains": jnp.clip(1.0 + 0.1 * jax.random.normal(key_of[6], (2, D), jnp.float32), 0.5, 1.5),
        "first_qkv": scatter_about(key_of[7], (3, D, D), (0.22 * TOKENS ** 0.5), 160.0, ((1, 16), (2, 2)), jnp.float32),
        "first_out": scatter_about(key_of[8], (D, D), (0.44 * (TOKENS // SEG) ** 0.5), 6.0, ((0, 2), (1, 16)), jnp.float32),
        "first_gate_up": scatter_about(key_of[9], (2, D, FF), (0.067 * TOKENS ** 0.5), 48.0, ((1, 16), (2, 2)), jnp.float32),
        "first_down": scatter_about(key_of[10], (FF, D), (0.12 * TOKENS ** 0.5), 96.0, ((0, 2), (1, 16)), jnp.float32),
        "first_gains": scatter_about(key_of[11], (2, D), (0.22 * TOKENS ** 0.5), 160.0, ((1, 16),), jnp.float32),
        "second_qkv": jnp.clip(jnp.exp(math.log(13762.56) - 1.3862944 * jax.random.uniform(key_of[12], (3, D, D), jnp.float32) ** block_scale(key_of[12], (3, D, D), ((1, 16), (2, 2)), -0.2, 0.2)), 3440.64, 13762.56),
        "second_out": jnp.clip(jnp.exp(math.log(27.2) - 1.3981289 * jax.random.uniform(key_of[13], (D, D), jnp.float32) ** block_scale(key_of[13], (D, D), ((0, 2), (1, 16)), -0.2, 0.2)), 6.72, 27.2),
        "second_gate_up": jnp.clip(jnp.exp(math.log(1245.184) - 1.3862944 * jax.random.uniform(key_of[14], (2, D, FF), jnp.float32) ** block_scale(key_of[14], (2, D, FF), ((1, 16), (2, 2)), -0.2, 0.2)), 311.296, 1245.184),
        "second_down": jnp.clip(jnp.exp(math.log(4096.0) - 1.3625778 * jax.random.uniform(key_of[15], (FF, D), jnp.float32) ** block_scale(key_of[15], (FF, D), ((0, 2), (1, 16)), -0.2, 0.2)), 1048.576, 4096.0),
        "second_gains": jnp.clip(jnp.exp(math.log(13762.56) - 1.3862944 * jax.random.uniform(key_of[16], (2, D), jnp.float32) ** block_scale(key_of[16], (2, D), ((1, 16),), -0.2, 0.2)), 3440.64, 13762.56),
        "cache": scatter_about(key_of[17], (N_DP * CACHE_DEV, 2, D), 1.0, 6.0, ((0, 16), (2, 2))),
        "doc_segments": draw_doc_segments(jax.random.fold_in(key_of[21], 71), 0),
        "padding": draw_padding(jax.random.fold_in(key_of[21], 71), 0),
        "retrieval": with_ends(jax.random.randint(key_of[20], (N_DP, RETR), 0, CACHE_DEV), jax.random.fold_in(key_of[20], 1), 0, CACHE_DEV - 1).astype(jnp.int32),
    }


EPS = 1e-05
BETA_ONE = 0.9
BETA_TWO = 0.95
ADAM_EPS = 1e-08
DECAY = 0.1
NEGATIVE = -1e+30

@jax.custom_vjp
def low(v):
    return lax.optimization_barrier(v.astype(jnp.bfloat16)).astype(jnp.float32)

@jax.custom_vjp
def low_back(v):
    return v

def low_keep(v):
    return (low(v), None)

def low_pass(kept, grad):
    return (grad,)

def back_keep(v):
    return (v, None)

def back_low(kept, grad):
    return (low(grad),)
low.defvjp(low_keep, low_pass)
low_back.defvjp(back_keep, back_low)

def matmul(left, right):
    return jnp.dot(left, right, precision=lax.Precision.HIGHEST, preferred_element_type=jnp.float32)

def angles(places):
    half_dim = HEAD_DIM // 2
    freqs = 10000.0 ** (-(jnp.arange(half_dim, dtype=jnp.float32) / half_dim))
    phase = places.astype(jnp.float32)[:, None] * freqs[None, :]
    return (jnp.cos(phase), jnp.sin(phase))

def rotate(value, cosines, sine_table):
    half_dim = HEAD_DIM // 2
    first_half = value[..., :half_dim]
    second_half = value[..., half_dim:]
    cos_wide = cosines[:, None, :]
    sin_wide = sine_table[:, None, :]
    return jnp.concatenate([first_half * cos_wide - second_half * sin_wide, second_half * cos_wide + first_half * sin_wide], axis=-1)

def normalize(value):
    return value * lax.rsqrt(lax.optimization_barrier(jnp.mean(value * value, axis=-1, keepdims=True)) + EPS)

def segment_attention(pieces):
    queries, keys, values, mem_keys, mem_values, valid, memory_on = pieces
    scale_factor = HEAD_DIM ** (-0.5)
    local = low_back(scale_factor * jnp.einsum('qhd,khd->hqk', queries, keys, precision=lax.Precision.HIGHEST))
    places = jnp.arange(SEG, dtype=jnp.int32)
    allowed = (places[:, None] >= places[None, :]) & (valid[None, :] > 0)
    blocked = queries.reshape(SPAN, TOK_DEV, HEADS, HEAD_DIM)
    memory = low_back(scale_factor * jnp.einsum('bqhd,brhd->hbqr', blocked, mem_keys, precision=lax.Precision.HIGHEST)).reshape(HEADS, SEG, RETR)
    scores = jnp.concatenate([jnp.where(allowed[None], local, NEGATIVE), jnp.where(memory_on > 0, memory, NEGATIVE)], axis=-1)
    top = lax.optimization_barrier(jnp.max(scores, axis=-1, keepdims=True))
    exponent = jnp.exp(scores - top)
    probs = exponent / lax.optimization_barrier(jnp.sum(exponent, axis=-1, keepdims=True))
    weights_low = low(probs)
    local_out = jnp.einsum('hqk,khd->qhd', weights_low[..., :SEG], values, precision=lax.Precision.HIGHEST)
    memory_part = weights_low[..., SEG:].reshape(HEADS, SPAN, TOK_DEV, RETR)
    memory_out = jnp.einsum('hbqr,brhd->bqhd', memory_part, mem_values, precision=lax.Precision.HIGHEST).reshape(SEG, HEADS, HEAD_DIM)
    return local_out + memory_out

def adamw(weight, grad, first, second, rate):
    first_new = BETA_ONE * first + (1.0 - BETA_ONE) * grad
    second_new = BETA_TWO * second + (1.0 - BETA_TWO) * grad * grad
    first_hat = first_new / (1.0 - BETA_ONE ** STEP)
    second_hat = second_new / (1.0 - BETA_TWO ** STEP)
    updated = weight - rate * (first_hat / (jnp.sqrt(second_hat) + ADAM_EPS) + DECAY * weight)
    return (first_new, second_new, updated)

def reference(tokens, cotangent, proj_qkv, proj_out, proj_gate_up, proj_down, norm_gains, first_qkv, first_out, first_gate_up, first_down, first_gains, second_qkv, second_out, second_gate_up, second_down, second_gains, cache, doc_segments, padding, retrieval):
    cache_full = cache.astype(jnp.float32)
    row_index = retrieval + (jnp.arange(N_DP, dtype=jnp.int32) * CACHE_DEV)[:, None]
    fetched = cache_full[row_index]
    mem_keys = fetched[:, :, 0].reshape(NSEG, SPAN, RETR, HEADS, HEAD_DIM)
    mem_values = fetched[:, :, 1].reshape(NSEG, SPAN, RETR, HEADS, HEAD_DIM)
    starts = jnp.cumsum(doc_segments) - doc_segments
    segment_ids = jnp.arange(NSEG, dtype=jnp.int32)
    memory_on = jnp.where(jnp.any(segment_ids[:, None] == starts[None, :], axis=1), 0, 1).astype(jnp.int32)
    key_valid = padding.reshape(NSEG, SEG)
    places = jnp.arange(TOKENS, dtype=jnp.int32) % SEG
    cosines, sine_table = angles(places)
    shape = (NSEG, SEG, HEADS, HEAD_DIM)

    def forward(inputs, weight_qkv, weight_out, weight_gate_up, weight_down, gains):
        gains_low = low(gains)
        normed_one = low(normalize(inputs) * gains_low[0])
        qkv_low = low(weight_qkv)
        queries = low_back(matmul(normed_one, qkv_low[0])).reshape(TOKENS, HEADS, HEAD_DIM)
        keys = low_back(matmul(normed_one, qkv_low[1])).reshape(TOKENS, HEADS, HEAD_DIM)
        values = low(low_back(matmul(normed_one, qkv_low[2])))
        queries_rot = low(rotate(queries, cosines, sine_table))
        keys_rot = low(rotate(keys, cosines, sine_table))
        attended = lax.map(jax.checkpoint(segment_attention), (queries_rot.reshape(shape), keys_rot.reshape(shape), values.reshape(shape), mem_keys, mem_values, key_valid, memory_on))
        attended = low(low_back(attended.reshape(TOKENS, D)))
        middle = inputs + low_back(matmul(attended, low(weight_out)))
        normed_two = low(normalize(middle) * gains_low[1])
        gate_up_low = low(weight_gate_up)
        gate = low_back(matmul(normed_two, gate_up_low[0]))
        up_part = low_back(matmul(normed_two, gate_up_low[1]))
        hidden = low(gate * jax.nn.sigmoid(gate) * up_part)
        return middle + low_back(matmul(hidden, low(weight_down)))
    block, pullback = jax.vjp(forward, tokens.astype(jnp.float32), proj_qkv, proj_out, proj_gate_up, proj_down, norm_gains)
    grads = pullback(cotangent.astype(jnp.float32))
    qkv_first, qkv_second, qkv_new = adamw(proj_qkv, grads[1], first_qkv, second_qkv, 0.5 / math.sqrt(D))
    out_first, out_second, out_new = adamw(proj_out, grads[2], first_out, second_out, 0.5 / math.sqrt(max(1, 4 * D // SEG)))
    gate_up_first, gate_up_second, gate_up_new = adamw(proj_gate_up, grads[3], first_gate_up, second_gate_up, 0.5 / math.sqrt(D))
    down_first, down_second, down_new = adamw(proj_down, grads[4], first_down, second_down, 0.5 / math.sqrt(FF))
    gains_first, gains_second, gains_new = adamw(norm_gains, grads[5], first_gains, second_gains, 0.6)
    return (block.astype(jnp.bfloat16), grads[0].astype(jnp.bfloat16), qkv_first, qkv_second, qkv_new, out_first, out_second, out_new, gate_up_first, gate_up_second, gate_up_new, down_first, down_second, down_new, gains_first, gains_second, gains_new)
```

```python
import functools
import math

import jax
import jax.numpy as jnp
from jax import lax
from jax.experimental import pallas as pl
from jax.experimental.pallas import tpu as pltpu
from jax.sharding import PartitionSpec as P

D = 1024
HEAD_DIM = 128
FF = 2816
SEG = 2048
RETR = 128
STEP = 10

EPS = 1e-05
BETA_ONE = 0.9
BETA_TWO = 0.95
ADAM_EPS = 1e-08
DECAY = 0.1
NEGATIVE = -1e30
SCALE = HEAD_DIM**-0.5
SCALE_TWO = SCALE * math.log2(math.e)

BF = jnp.bfloat16
F32 = jnp.float32
MIB = 1024 * 1024
TILE = 256


def dot(left, right):
    return jnp.dot(left, right, preferred_element_type=F32)


def dot_nt(left, right):
    return lax.dot_general(left, right, (((1,), (1,)), ((), ())), preferred_element_type=F32)


def dot_tn(left, right):
    return lax.dot_general(left, right, (((0,), (0,)), ((), ())), preferred_element_type=F32)


def params(mib, axes=1):
    return pltpu.CompilerParams(
        dimension_semantics=("arbitrary",) * axes, vmem_limit_bytes=mib * MIB
    )


def cost(flops, moved, trans=0):
    return pl.CostEstimate(flops=int(flops), bytes_accessed=int(moved), transcendentals=int(trans))


def rope_tables(count):
    half_dim = HEAD_DIM // 2
    freqs = 10000.0 ** (-(jnp.arange(half_dim, dtype=F32) / half_dim))
    phase = jnp.arange(count, dtype=jnp.int32).astype(F32)[:, None] * freqs[None, :]
    cosines, sines = jnp.cos(phase), jnp.sin(phase)
    return jnp.concatenate([cosines, cosines], 1), jnp.concatenate([-sines, sines], 1)


def turn(value, cosines, sines):
    return value * cosines + pltpu.roll(value, HEAD_DIM // 2, 1) * sines


def adamw(weight, grad, first, second, rate):
    first_new = BETA_ONE * first + (1.0 - BETA_ONE) * grad
    second_new = BETA_TWO * second + (1.0 - BETA_TWO) * grad * grad
    first_hat = first_new / (1.0 - BETA_ONE**STEP)
    second_hat = second_new / (1.0 - BETA_TWO**STEP)
    updated = weight - rate * (first_hat / (jnp.sqrt(second_hat) + ADAM_EPS) + DECAY * weight)
    return (first_new, second_new, updated)


def qkv_kernel(info, normed, weight, cosines, sines, out):
    result = dot(normed[...], weight[...])
    part = pl.program_id(0)
    for head in range(2):
        value = result[:, head * HEAD_DIM : (head + 1) * HEAD_DIM]

        @pl.when(part < 2)
        def _():
            out[0, head] = turn(value, cosines[...], sines[...]).astype(BF)

        @pl.when(part == 2)
        def _():
            out[0, head] = value.astype(BF)


def project_pair(info, normed, weights, cosines, sines, slot):
    rows = normed.shape[0]
    return pl.pallas_call(
        qkv_kernel,
        out_shape=jax.ShapeDtypeStruct((3, 2, rows, HEAD_DIM), BF),
        grid_spec=pltpu.PrefetchScalarGridSpec(
            num_scalar_prefetch=1,
            grid=(3,),
            in_specs=[
                pl.BlockSpec((rows, D), lambda j, info: (0, 0)),
                pl.BlockSpec((D, 256), lambda j, info: (0, 2 * j + info[slot])),
                pl.BlockSpec((rows, HEAD_DIM), lambda j, info: (info[0], 0)),
                pl.BlockSpec((rows, HEAD_DIM), lambda j, info: (info[0], 0)),
            ],
            out_specs=pl.BlockSpec((1, 2, rows, HEAD_DIM), lambda j, info: (j, 0, 0, 0)),
        ),
        compiler_params=params(40),
        cost_estimate=cost(2 * rows * D * 768, 6 * MIB),
        name="project_pair",
    )(info, normed, weights, cosines, sines)


def place(scratch, own, other, rank, rows):
    scratch[pl.ds(pl.multiple_of(rank * rows, rows), rows), :] = own
    scratch[pl.ds(pl.multiple_of((1 - rank) * rows, rows), rows), :] = other


def chunks_of(tile, step):
    end = tile * TILE
    spans = [(start, min(step, end - start)) for start in range(0, end, step)]
    return spans + [(end, TILE)]


def causal(scores):
    rows = lax.broadcasted_iota(jnp.int32, scores.shape, 0)
    columns = lax.broadcasted_iota(jnp.int32, scores.shape, 1)
    return jnp.where(rows <= columns, scores, NEGATIVE)


def forward_kernel(
    info, own, other, mem_own, mem_other, bias, keep, send, turned, logs,
    q_s, k_s, v_s, vt_s, mem_s, s_s, out_s,
):
    rank = info[0]
    rows = own.shape[2]
    mem_bias = jnp.where(info[2] > 0, 0.0, NEGATIVE).astype(F32)
    place(q_s, own[0, 0], other[0, 0], rank, rows)
    place(k_s, own[1, 0], other[1, 0], rank, rows)
    place(v_s, own[2, 0], other[2, 0], rank, rows)
    mem_s[rank] = mem_own[:, 0]
    mem_s[1 - rank] = mem_other[:, 0]
    vt_s[...] = v_s[...].astype(F32).T.astype(BF)
    ones = (lax.broadcasted_iota(jnp.int32, (TILE, HEAD_DIM), 1) == 0).astype(BF)
    for tile in range(SEG // TILE):
        here = slice(tile * TILE, (tile + 1) * TILE)
        block = tile * TILE // rows
        query = q_s[here, :]
        wide = jnp.concatenate([query, ones], axis=1)
        spans = chunks_of(tile, 512)
        scores = dot_nt(mem_s[block, 0], query) + mem_bias
        s_s[SEG : SEG + RETR, :] = scores
        top = jnp.max(scores, axis=0, keepdims=True)
        for start, size in spans:
            span = slice(start, start + size)
            if start + size > SEG // 2:
                scores = dot_nt(jnp.concatenate([k_s[span, :], bias[span, :]], axis=1), wide)
            else:
                scores = dot_nt(k_s[span, :], query)
            if start == tile * TILE:
                scores = causal(scores)
            s_s[span, :] = scores
            top = jnp.maximum(top, jnp.max(scores, axis=0, keepdims=True))
        shift = top * SCALE_TWO
        exponent = jnp.exp2(s_s[SEG : SEG + RETR, :] * SCALE_TWO - shift)
        total = jnp.sum(exponent, axis=0, keepdims=True)
        result = dot(mem_s[block, 1].astype(F32).T.astype(BF), exponent.astype(BF))
        for start, size in spans:
            span = slice(start, start + size)
            exponent = jnp.exp2(s_s[span, :] * SCALE_TWO - shift)
            total = total + jnp.sum(exponent, axis=0, keepdims=True)
            result = result + dot(vt_s[:, span], exponent.astype(BF))
        result = result * (1.0 / total)
        turned[0, :, here] = result
        logs[0, :, here] = shift + jnp.log2(total)
        out_s[here, :] = result.T.astype(BF)
    keep[0] = out_s[pl.ds(pl.multiple_of(rank * rows, rows), rows), :]
    send[0] = out_s[pl.ds(pl.multiple_of((1 - rank) * rows, rows), rows), :]


def attend_forward(info, own, other, mem_own, mem_other, bias):
    rows = own.shape[2]
    part = pl.BlockSpec((3, 1, rows, HEAD_DIM), lambda h, info: (0, h, 0, 0))
    mem = pl.BlockSpec((2, 1, RETR, HEAD_DIM), lambda h, info: (0, h, 0, 0))
    half = pl.BlockSpec((1, rows, HEAD_DIM), lambda h, info: (h, 0, 0))
    return pl.pallas_call(
        forward_kernel,
        out_shape=(
            jax.ShapeDtypeStruct((2, rows, HEAD_DIM), BF),
            jax.ShapeDtypeStruct((2, rows, HEAD_DIM), BF),
            jax.ShapeDtypeStruct((2, HEAD_DIM, SEG), F32),
            jax.ShapeDtypeStruct((2, 1, SEG), F32),
        ),
        grid_spec=pltpu.PrefetchScalarGridSpec(
            num_scalar_prefetch=1,
            grid=(2,),
            in_specs=[
                part,
                part,
                mem,
                mem,
                pl.BlockSpec((SEG, HEAD_DIM), lambda h, info: (0, 0)),
            ],
            out_specs=(
                half,
                half,
                pl.BlockSpec((1, HEAD_DIM, SEG), lambda h, info: (h, 0, 0)),
                pl.BlockSpec((1, 1, SEG), lambda h, info: (h, 0, 0)),
            ),
            scratch_shapes=[
                pltpu.VMEM((SEG, HEAD_DIM), BF),
                pltpu.VMEM((SEG, HEAD_DIM), BF),
                pltpu.VMEM((SEG, HEAD_DIM), BF),
                pltpu.VMEM((HEAD_DIM, SEG), BF),
                pltpu.VMEM((2, 2, RETR, HEAD_DIM), BF),
                pltpu.VMEM((SEG + RETR, TILE), F32),
                pltpu.VMEM((SEG, HEAD_DIM), BF),
            ],
        ),
        compiler_params=params(48),
        cost_estimate=cost(5e9, 8 * MIB, 5e6),
        name="attend_forward",
    )(info, own, other, mem_own, mem_other, bias)


def backward_kernel(
    info, own, other, mem_own, mem_other, bias, grad_own, grad_other, turned, logs, cosines, sines,
    keep, send,
    q_s, k_s, v_s, g_s, kt_s, mem_s, dots_s, dq_s, dk_s, dv_s,
):
    rank = info[0]
    rows = own.shape[2]
    mem_bias = jnp.where(info[2] > 0, 0.0, NEGATIVE).astype(F32)
    place(q_s, own[0, 0], other[0, 0], rank, rows)
    place(k_s, own[1, 0], other[1, 0], rank, rows)
    place(v_s, own[2, 0], other[2, 0], rank, rows)
    place(g_s, grad_own[0], grad_other[0], rank, rows)
    mem_s[rank] = mem_own[:, 0]
    mem_s[1 - rank] = mem_other[:, 0]
    kt_s[...] = k_s[...].astype(F32).T.astype(BF)
    dots_s[...] = jnp.sum(g_s[...].astype(F32).T * turned[0], axis=0, keepdims=True)
    dk_s[...] = jnp.zeros_like(dk_s)
    dv_s[...] = jnp.zeros_like(dv_s)
    ones = (lax.broadcasted_iota(jnp.int32, (TILE, HEAD_DIM), 1) == 0).astype(BF)
    for tile in range(SEG // TILE):
        here = slice(tile * TILE, (tile + 1) * TILE)
        block = tile * TILE // rows
        query = q_s[here, :]
        wide = jnp.concatenate([query, ones], axis=1)
        grad = g_s[here, :]
        log = logs[0, :, here]
        dots = dots_s[:, here]
        scores = dot_nt(mem_s[block, 0], query) + mem_bias
        probs = jnp.exp2(scores * SCALE_TWO - log)
        change = (probs * (dot_nt(mem_s[block, 1], grad) - dots)).astype(BF)
        result = dot(mem_s[block, 0].astype(F32).T.astype(BF), change)
        for start, size in chunks_of(tile, 512):
            span = slice(start, start + size)
            keys = k_s[span, :]
            if start + size > SEG // 2:
                scores = dot_nt(jnp.concatenate([keys, bias[span, :]], axis=1), wide)
            else:
                scores = dot_nt(keys, query)
            if start == tile * TILE:
                scores = causal(scores)
            probs = jnp.exp2(scores * SCALE_TWO - log)
            change = (probs * (dot_nt(v_s[span, :], grad) - dots)).astype(BF)
            dv_s[span, :] += dot(probs.astype(BF), grad)
            dk_s[span, :] += dot(change, query)
            result = result + dot(kt_s[:, span], change)
        dq_s[here, :] = turn(result.T * SCALE, cosines[here, :], -sines[here, :]).astype(BF)
    for index in range(2):
        held = pl.ds(pl.multiple_of((rank if index == 0 else 1 - rank) * rows, rows), rows)
        out = keep if index == 0 else send
        out[0, 0] = dq_s[held, :]
        out[1, 0] = turn(dk_s[held, :] * SCALE, cosines[held, :], -sines[held, :]).astype(BF)
        out[2, 0] = dv_s[held, :].astype(BF)


def attend_backward(
    info, own, other, mem_own, mem_other, bias, grad_own, grad_other, turned, logs, cosines, sines
):
    rows = own.shape[2]
    part = pl.BlockSpec((3, 1, rows, HEAD_DIM), lambda h, info: (0, h, 0, 0))
    mem = pl.BlockSpec((2, 1, RETR, HEAD_DIM), lambda h, info: (0, h, 0, 0))
    half = pl.BlockSpec((1, rows, HEAD_DIM), lambda h, info: (h, 0, 0))
    table = pl.BlockSpec((SEG, HEAD_DIM), lambda h, info: (0, 0))
    return pl.pallas_call(
        backward_kernel,
        out_shape=(jax.ShapeDtypeStruct((3, 2, rows, HEAD_DIM), BF),) * 2,
        grid_spec=pltpu.PrefetchScalarGridSpec(
            num_scalar_prefetch=1,
            grid=(2,),
            in_specs=[
                part,
                part,
                mem,
                mem,
                table,
                half,
                half,
                pl.BlockSpec((1, HEAD_DIM, SEG), lambda h, info: (h, 0, 0)),
                pl.BlockSpec((1, 1, SEG), lambda h, info: (h, 0, 0)),
                table,
                table,
            ],
            out_specs=(part, part),
            scratch_shapes=[pltpu.VMEM((SEG, HEAD_DIM), BF)] * 4
            + [
                pltpu.VMEM((HEAD_DIM, SEG), BF),
                pltpu.VMEM((2, 2, RETR, HEAD_DIM), BF),
                pltpu.VMEM((1, SEG), F32),
                pltpu.VMEM((SEG, HEAD_DIM), BF),
                pltpu.VMEM((SEG, HEAD_DIM), F32),
                pltpu.VMEM((SEG, HEAD_DIM), F32),
            ],
        ),
        compiler_params=params(48),
        cost_estimate=cost(12e9, 16 * MIB, 5e6),
        name="attend_backward",
    )(info, own, other, mem_own, mem_other, bias, grad_own, grad_other, turned, logs, cosines, sines)


def middle_kernel(info, one, two, three, four, tokens, weight, gain, middle, normed, o_s):
    rank, group = info[0], info[1]
    pieces = ((one, group, rank), (two, group, 1 - rank), (three, 1 - group, rank), (four, 1 - group, 1 - rank))
    for piece, side, pair in pieces:
        for head in range(2):
            column = pl.multiple_of((side * 4 + pair * 2 + head) * HEAD_DIM, HEAD_DIM)
            o_s[:, pl.ds(column, HEAD_DIM)] = piece[head]
    value = tokens[...].astype(F32) + dot_nt(o_s[...], weight[...])
    middle[...] = value
    inverse = lax.rsqrt(jnp.mean(value * value, axis=1, keepdims=True) + EPS)
    normed[...] = (value * inverse * gain[...]).astype(BF)


def middle_call(info, pieces, tokens, weight, gain):
    rows = tokens.shape[0]
    piece = pl.BlockSpec((2, TILE, HEAD_DIM), lambda i, info: (0, i, 0))
    wide = pl.BlockSpec((TILE, D), lambda i, info: (i, 0))
    return pl.pallas_call(
        middle_kernel,
        out_shape=(
            jax.ShapeDtypeStruct((rows, D), F32),
            jax.ShapeDtypeStruct((rows, D), BF),
        ),
        grid_spec=pltpu.PrefetchScalarGridSpec(
            num_scalar_prefetch=1,
            grid=(rows // TILE,),
            in_specs=[piece] * 4
            + [
                wide,
                pl.BlockSpec((D, D), lambda i, info: (0, 0)),
                pl.BlockSpec((1, D), lambda i, info: (0, 0)),
            ],
            out_specs=(wide, wide),
            scratch_shapes=[pltpu.VMEM((TILE, D), BF)],
        ),
        compiler_params=params(40),
        cost_estimate=cost(2 * rows * D * D, 12 * MIB),
        name="middle",
    )(info, *pieces, tokens, weight, gain)


def feed_kernel(normed, upstream, gate_w, up_w, down_w, hidden, gate_grad, up_grad, back):
    gate = dot(normed[...], gate_w[...])
    up_part = dot(normed[...], up_w[...])
    sigma = jax.nn.sigmoid(gate)
    silu = gate * sigma
    hidden[...] = (silu * up_part).astype(BF)
    grad = dot(upstream[...], down_w[...])
    grad_gate = (grad * up_part * sigma * (1.0 + gate * (1.0 - sigma))).astype(BF)
    grad_up = (grad * silu).astype(BF)
    gate_grad[...] = grad_gate
    up_grad[...] = grad_up
    back[...] = (dot_nt(grad_gate, gate_w[...]) + dot_nt(grad_up, up_w[...])).astype(BF)


def feed_call(normed, upstream, weights, first, count):
    width = weights.shape[1] // 3
    whole = lambda index: pl.BlockSpec((D, width), lambda i: (0, index), pipeline_mode=pl.Buffered(1))
    source = pl.BlockSpec((TILE, D), lambda i: (i + first // TILE, 0))
    narrow = pl.BlockSpec((TILE, width), lambda i: (i, 0))
    return pl.pallas_call(
        feed_kernel,
        out_shape=(jax.ShapeDtypeStruct((count, width), BF),) * 3
        + (jax.ShapeDtypeStruct((count, D), BF),),
        grid=(count // TILE,),
        in_specs=[source, source, whole(0), whole(1), whole(2)],
        out_specs=(narrow, narrow, narrow, pl.BlockSpec((TILE, D), lambda i: (i, 0))),
        compiler_params=params(48),
        cost_estimate=cost(10 * count * D * width, 9 * MIB + 16 * count * D),
        name="feed",
    )(normed, upstream, weights, weights, weights)


def out_kernel(hidden, down_w, out):
    out[...] = dot_nt(hidden[...], down_w[...]).astype(BF)


def out_call(hidden, weights):
    count, width = hidden.shape
    return pl.pallas_call(
        out_kernel,
        out_shape=jax.ShapeDtypeStruct((count, D), BF),
        grid=(count // TILE,),
        in_specs=[
            pl.BlockSpec((TILE, width), lambda i: (i, 0)),
            pl.BlockSpec((D, width), lambda i: (0, 2), pipeline_mode=pl.Buffered(1)),
        ],
        out_specs=pl.BlockSpec((TILE, D), lambda i: (i, 0)),
        compiler_params=params(40),
        cost_estimate=cost(2 * count * D * width, 6 * MIB),
        name="feed_out",
    )(hidden, weights)


def feed_weight_kernel(normed, upstream, hidden, gate_grad, up_grad, out):
    width = hidden.shape[1]
    left = normed[...].astype(F32).T.astype(BF)
    out[:, :width] = dot(left, gate_grad[...]).astype(BF)
    out[:, width : 2 * width] = dot(left, up_grad[...]).astype(BF)
    left = upstream[...].astype(F32).T.astype(BF)
    out[:, 2 * width :] = dot(left, hidden[...]).astype(BF)


def feed_weight_call(normed, upstream, hidden, gate_grad, up_grad):
    rows, width = hidden.shape
    left = pl.BlockSpec((rows, TILE), lambda i: (0, i))
    whole = pl.BlockSpec((rows, width), lambda i: (0, 0), pipeline_mode=pl.Buffered(1))
    return pl.pallas_call(
        feed_weight_kernel,
        out_shape=jax.ShapeDtypeStruct((D, 3 * width), BF),
        grid=(D // TILE,),
        in_specs=[left, left, whole, whole, whole],
        out_specs=pl.BlockSpec((TILE, 3 * width), lambda i: (i, 0)),
        compiler_params=params(48),
        cost_estimate=cost(6 * rows * D * width, 22 * MIB),
        name="feed_weights",
    )(normed, upstream, hidden, gate_grad, up_grad)


def residual_kernel(info, middle, back_own, back_other, upstream, gain, weight, grad, low, keep, send, gain_grad):
    rank = info[0]
    value = middle[...]
    back = back_own[...].astype(F32) + back_other[...].astype(F32)
    inverse = lax.rsqrt(jnp.mean(value * value, axis=1, keepdims=True) + EPS)
    scaled = gain[...] * back
    inner = jnp.mean(scaled * value, axis=1, keepdims=True)
    total = upstream[...].astype(F32) + inverse * scaled - value * (inverse**3 * inner)
    grad[...] = total
    branch = total.astype(BF)
    low[...] = branch

    @pl.when(pl.program_id(0) == 0)
    def _():
        gain_grad[...] = jnp.zeros_like(gain_grad)

    gain_grad[...] += jnp.sum(back * value * inverse, axis=0, keepdims=True)
    for out, pair in ((keep, rank), (send, 1 - rank)):
        column = pl.multiple_of(pair * 2 * HEAD_DIM, 2 * HEAD_DIM)
        result = dot(branch, weight[:, pl.ds(column, 2 * HEAD_DIM)]).astype(BF)
        for head in range(2):
            out[head] = result[:, head * HEAD_DIM : (head + 1) * HEAD_DIM]


def residual_call(info, middle, back_own, back_other, upstream, gain, weight):
    rows = middle.shape[0]
    half = weight.shape[1] // 2
    wide = pl.BlockSpec((TILE, D), lambda i, info: (i, 0))
    row = pl.BlockSpec((1, D), lambda i, info: (0, 0))
    piece = pl.BlockSpec((2, TILE, HEAD_DIM), lambda i, info: (0, i, 0))
    return pl.pallas_call(
        residual_kernel,
        out_shape=(
            jax.ShapeDtypeStruct((rows, D), F32),
            jax.ShapeDtypeStruct((rows, D), BF),
            jax.ShapeDtypeStruct((2, rows, HEAD_DIM), BF),
            jax.ShapeDtypeStruct((2, rows, HEAD_DIM), BF),
            jax.ShapeDtypeStruct((1, D), F32),
        ),
        grid_spec=pltpu.PrefetchScalarGridSpec(
            num_scalar_prefetch=1,
            grid=(rows // TILE,),
            in_specs=[
                wide,
                wide,
                wide,
                wide,
                row,
                pl.BlockSpec((D, half), lambda i, info: (0, info[1])),
            ],
            out_specs=(wide, wide, piece, piece, row),
        ),
        compiler_params=params(40),
        cost_estimate=cost(2 * rows * D * half, 18 * MIB),
        name="residual",
    )(info, middle, back_own, back_other, upstream, gain, weight)


def back_kernel(info, own, other, weight, tokens, out, joined, gain_grad):
    rank = info[0]
    for piece, pair in ((own, rank), (other, 1 - rank)):
        for part in range(3):
            for head in range(2):
                column = pl.multiple_of((part * 4 + pair * 2 + head) * HEAD_DIM, HEAD_DIM)
                joined[:, pl.ds(column, HEAD_DIM)] = piece[part, head]
    back = dot_nt(joined[...], weight[...])
    out[...] = back.astype(BF)

    @pl.when(pl.program_id(0) == 0)
    def _():
        gain_grad[...] = jnp.zeros_like(gain_grad)

    value = tokens[...].astype(F32)
    inverse = lax.rsqrt(jnp.mean(value * value, axis=1, keepdims=True) + EPS)
    gain_grad[...] += jnp.sum(back * value * inverse, axis=0, keepdims=True)


def back_call(info, own, other, weights, tokens):
    rows = tokens.shape[0]
    width = 3 * 4 * HEAD_DIM
    piece = pl.BlockSpec((3, 2, TILE, HEAD_DIM), lambda i, info: (0, 0, i, 0))
    wide = pl.BlockSpec((TILE, D), lambda i, info: (i, 0))
    return pl.pallas_call(
        back_kernel,
        out_shape=(
            jax.ShapeDtypeStruct((rows, D), BF),
            jax.ShapeDtypeStruct((rows, width), BF),
            jax.ShapeDtypeStruct((1, D), F32),
        ),
        grid_spec=pltpu.PrefetchScalarGridSpec(
            num_scalar_prefetch=1,
            grid=(rows // TILE,),
            in_specs=[
                piece,
                piece,
                pl.BlockSpec((D, width), lambda i, info: (0, 0)),
                wide,
            ],
            out_specs=(
                wide,
                pl.BlockSpec((TILE, width), lambda i, info: (i, 0)),
                pl.BlockSpec((1, D), lambda i, info: (0, 0)),
            ),
        ),
        compiler_params=params(40),
        cost_estimate=cost(2 * rows * D * width, 13 * MIB),
        name="back",
    )(info, own, other, weights, tokens)


def attend_weight_kernel(info, normed, joined, low, one, two, out, o_s):
    @pl.when(pl.program_id(0) == 0)
    def _():
        for piece, pair in ((one, info[0]), (two, 1 - info[0])):
            for head in range(2):
                column = pl.multiple_of((pair * 2 + head) * HEAD_DIM, HEAD_DIM)
                o_s[:, pl.ds(column, HEAD_DIM)] = piece[head]

    width = joined.shape[1]
    left = normed[...].astype(F32).T.astype(BF)
    out[:, :width] = dot(left, joined[...]).astype(BF)
    left = low[...].astype(F32).T.astype(BF)
    out[:, width:] = dot(left, o_s[...]).astype(BF)


def attend_weight_call(info, normed, joined, low, one, two):
    rows, width = joined.shape
    half = 4 * HEAD_DIM
    left = pl.BlockSpec((rows, TILE), lambda i, info: (0, i))
    piece = pl.BlockSpec((2, rows, HEAD_DIM), lambda i, info: (0, 0, 0))
    return pl.pallas_call(
        attend_weight_kernel,
        out_shape=jax.ShapeDtypeStruct((D, width + half), BF),
        grid_spec=pltpu.PrefetchScalarGridSpec(
            num_scalar_prefetch=1,
            grid=(D // TILE,),
            in_specs=[
                left,
                pl.BlockSpec((rows, width), lambda i, info: (0, 0)),
                left,
                piece,
                piece,
            ],
            out_specs=pl.BlockSpec((TILE, width + half), lambda i, info: (i, 0)),
            scratch_shapes=[pltpu.VMEM((rows, half), BF)],
        ),
        compiler_params=params(40),
        cost_estimate=cost(2 * rows * D * (width + half), 13 * MIB),
        name="attend_weights",
    )(info, normed, joined, low, one, two)


def input_kernel(grad, back_own, back_other, tokens, gain, out):
    value = tokens[...].astype(F32)
    back = back_own[...].astype(F32) + back_other[...].astype(F32)
    inverse = lax.rsqrt(jnp.mean(value * value, axis=1, keepdims=True) + EPS)
    scaled = gain[...] * back
    inner = jnp.mean(scaled * value, axis=1, keepdims=True)
    out[...] = (grad[...] + inverse * scaled - value * (inverse**3 * inner)).astype(BF)


def input_call(grad, back_own, back_other, tokens, gain):
    rows = tokens.shape[0]
    wide = pl.BlockSpec((TILE, D), lambda i: (i, 0))
    return pl.pallas_call(
        input_kernel,
        out_shape=jax.ShapeDtypeStruct((rows, D), BF),
        grid=(rows // TILE,),
        in_specs=[wide, wide, wide, wide, pl.BlockSpec((1, D), lambda i: (0, 0))],
        out_specs=wide,
        compiler_params=params(32),
        cost_estimate=cost(12 * rows * D, 12 * MIB),
        name="input_grad",
    )(grad, back_own, back_other, tokens, gain)


def body(
    tokens,
    cotangent,
    proj_qkv,
    proj_out,
    proj_gate_up,
    proj_down,
    norm_gains,
    first_qkv,
    first_out,
    first_gate_up,
    first_down,
    first_gains,
    second_qkv,
    second_out,
    second_gate_up,
    second_down,
    second_gains,
    cache,
    doc_segments,
    padding,
    retrieval,
):
    rows = tokens.shape[0]
    count = lax.axis_size("dp")
    device = lax.axis_index("dp")
    group = lax.axis_index("mp")
    rank = device % 2
    segment = device // 2
    shard = proj_qkv.shape[1]
    local = proj_qkv.shape[2]
    hidden_here = proj_gate_up.shape[2]
    core_pairs = [(i, i ^ 1) for i in range(count)]

    def across(value):
        return lax.ppermute(value, "mp", [(0, 1), (1, 0)])

    def beside(value):
        return lax.ppermute(value, "dp", core_pairs)

    gain_columns = jnp.pad(norm_gains.astype(BF).T, ((0, 0), (0, HEAD_DIM - 2)))
    shard_one = jnp.concatenate(
        [proj_qkv[part].astype(BF) for part in range(3)] + [gain_columns], axis=1
    )
    out_own = proj_out.astype(BF).T
    out_other = across(out_own)
    out_both = [
        jnp.where(group == 0, out_own, out_other),
        jnp.where(group == 0, out_other, out_own),
    ]
    shard_two = jnp.concatenate(
        [proj_gate_up[0].astype(BF), proj_gate_up[1].astype(BF), proj_down.astype(BF).T], axis=1
    )
    weights_one = lax.all_gather(shard_one, "dp", axis=0, tiled=True)
    weights_two = lax.all_gather(shard_two, "dp", axis=0, tiled=True)
    weights_out = lax.all_gather(jnp.concatenate(out_both, axis=1), "dp", axis=0, tiled=True)
    gains = weights_one[:, 3 * local : 3 * local + 2].astype(F32).T
    gain_one, gain_two = gains[0:1], gains[1:2]

    starts = jnp.cumsum(doc_segments) - doc_segments
    memory_on = jnp.logical_not(jnp.any(starts == segment))
    info = jnp.stack(
        [rank, group, memory_on.astype(jnp.int32), 1 - rank]
    ).astype(jnp.int32)
    cosines, sines = rope_tables(SEG)
    valid = lax.dynamic_slice_in_dim(padding, segment * SEG, SEG)
    lane = jnp.arange(HEAD_DIM, dtype=jnp.int32)[None, :]
    bias = jnp.where((valid[:, None] == 0) & (lane == 0), NEGATIVE, 0.0).astype(BF)
    fetched = cache[retrieval[0]].reshape(RETR, 2, 2, 2, HEAD_DIM).transpose(2, 1, 3, 0, 4)
    mem_own = lax.dynamic_index_in_dim(fetched, rank, keepdims=False)
    mem_other = beside(lax.dynamic_index_in_dim(fetched, 1 - rank, keepdims=False))

    inputs = tokens.astype(F32)
    inverse_one = lax.rsqrt(jnp.mean(inputs * inputs, axis=-1, keepdims=True) + EPS)
    normed_one = (inputs * inverse_one * gain_one).astype(BF)

    send = project_pair(info, normed_one, weights_one, cosines, sines, 3)
    other = beside(send)
    own = project_pair(info, normed_one, weights_one, cosines, sines, 0)
    out_keep, out_send, turned, logs = attend_forward(info, own, other, mem_own, mem_other, bias)
    out_recv = beside(out_send)
    pieces = (out_keep, out_recv, across(out_keep), across(out_recv))
    middle, normed_two = middle_call(info, pieces, tokens, weights_out, gain_two)

    half = rows // 2
    feeds = [feed_call(normed_two, cotangent, weights_two, first, half) for first in (0, half)]
    backs = [feed[3] for feed in feeds]
    backs_other = [across(back) for back in backs]
    hidden, grad_gate, grad_up = (
        jnp.concatenate([feed[index] for feed in feeds], axis=0) for index in range(3)
    )
    feed_part = out_call(hidden, weights_two)
    feed_other = across(feed_part)
    feed_grads = feed_weight_call(normed_two, cotangent, hidden, grad_gate, grad_up)
    back_two = jnp.concatenate(backs, axis=0)
    back_two_other = jnp.concatenate(backs_other, axis=0)
    grad_middle, grad_low, grad_keep, grad_send, gain_two_grad = residual_call(
        info, middle, back_two, back_two_other, cotangent, gain_two, weights_out
    )
    grad_other = beside(grad_send)
    block_out = (middle + (feed_part.astype(F32) + feed_other.astype(F32))).astype(BF)

    d_keep, d_send = attend_backward(
        info, own, other, mem_own, mem_other, bias, grad_keep, grad_other, turned, logs, cosines, sines
    )
    d_other = beside(d_send)
    back_one, joined, gain_one_grad = back_call(info, d_keep, d_other, weights_one, tokens)
    back_one_other = across(back_one)
    attend_grads = attend_weight_call(info, normed_one, joined, grad_low, out_keep, out_recv)
    gain_grads = jnp.pad(
        jnp.concatenate([gain_one_grad, gain_two_grad], axis=0).astype(BF).T,
        ((0, 0), (0, HEAD_DIM - 2)),
    )
    input_grad = input_call(grad_middle, back_one, back_one_other, tokens, gain_one)

    feed_sum = lax.psum_scatter(feed_grads, "dp", scatter_dimension=0, tiled=True)
    attend_sum = lax.psum_scatter(
        jnp.concatenate([attend_grads, gain_grads], axis=1), "dp", scatter_dimension=0, tiled=True
    )
    feed_sum, attend_sum = feed_sum.astype(F32), attend_sum.astype(F32)
    gate_up_sum = jnp.stack([feed_sum[:, :hidden_here], feed_sum[:, hidden_here : 2 * hidden_here]])
    down_sum = feed_sum[:, 2 * hidden_here :].T
    qkv_sum = jnp.stack([attend_sum[:, part * local : (part + 1) * local] for part in range(3)])
    out_sum = attend_sum[:, 3 * local : 4 * local].T
    gains_sum = attend_sum[:, 4 * local : 4 * local + 2].T
    gains_sum = jnp.concatenate([gains_sum[0:1] + across(gains_sum[0:1]), gains_sum[1:2]], axis=0)

    qkv_first, qkv_second, qkv_new = adamw(
        proj_qkv, qkv_sum, first_qkv, second_qkv, 0.5 / math.sqrt(D)
    )
    out_first, out_second, out_new = adamw(
        proj_out, out_sum, first_out, second_out, 0.5 / math.sqrt(max(1, 4 * D // SEG))
    )
    gate_up_first, gate_up_second, gate_up_new = adamw(
        proj_gate_up, gate_up_sum, first_gate_up, second_gate_up, 0.5 / math.sqrt(D)
    )
    down_first, down_second, down_new = adamw(
        proj_down, down_sum, first_down, second_down, 0.5 / math.sqrt(FF)
    )
    gains_first, gains_second, gains_new = adamw(
        norm_gains, gains_sum, first_gains, second_gains, 0.6
    )
    return (
        block_out,
        input_grad,
        qkv_first,
        qkv_second,
        qkv_new,
        out_first,
        out_second,
        out_new,
        gate_up_first,
        gate_up_second,
        gate_up_new,
        down_first,
        down_second,
        down_new,
        gains_first,
        gains_second,
        gains_new,
    )


def solution(mesh):
    return jax.shard_map(
        body,
        mesh=mesh,
        in_specs=(
            P("dp", None),
            P("dp", None),
            P(None, "dp", "mp"),
            P("mp", "dp"),
            P(None, "dp", "mp"),
            P("mp", "dp"),
            P(None, "dp"),
            P(None, "dp", "mp"),
            P("mp", "dp"),
            P(None, "dp", "mp"),
            P("mp", "dp"),
            P(None, "dp"),
            P(None, "dp", "mp"),
            P("mp", "dp"),
            P(None, "dp", "mp"),
            P("mp", "dp"),
            P(None, "dp"),
            P("dp", None, "mp"),
            P(),
            P(),
            P("dp", None),
        ),
        out_specs=(
            P("dp", None),
            P("dp", None),
            P(None, "dp", "mp"),
            P(None, "dp", "mp"),
            P(None, "dp", "mp"),
            P("mp", "dp"),
            P("mp", "dp"),
            P("mp", "dp"),
            P(None, "dp", "mp"),
            P(None, "dp", "mp"),
            P(None, "dp", "mp"),
            P("mp", "dp"),
            P("mp", "dp"),
            P("mp", "dp"),
            P(None, "dp"),
            P(None, "dp"),
            P(None, "dp"),
        ),
        check_vma=False,
    )
```

```python
import functools
import math

import jax
import jax.numpy as jnp
from jax import lax
from jax.experimental import pallas as pl
from jax.experimental.pallas import tpu as pltpu
from jax.sharding import PartitionSpec as P

D = 1024
HEAD_DIM = 128
FF = 2816
SEG = 2048
RETR = 128
STEP = 10

EPS = 1e-05
BETA_ONE = 0.9
BETA_TWO = 0.95
ADAM_EPS = 1e-08
DECAY = 0.1
NEGATIVE = -1e30
SCALE = HEAD_DIM**-0.5
SCALE_TWO = SCALE * math.log2(math.e)

BF = jnp.bfloat16
F32 = jnp.float32
MIB = 1024 * 1024
TILE = 256
VMEM = 26
WEIGH = 1.0


def dot(left, right):
    return jnp.dot(left, right, preferred_element_type=F32)


def dot_nt(left, right):
    return lax.dot_general(left, right, (((1,), (1,)), ((), ())), preferred_element_type=F32)


def dot_tn(left, right):
    return lax.dot_general(left, right, (((0,), (0,)), ((), ())), preferred_element_type=F32)


def params(mib, axes=1):
    return pltpu.CompilerParams(
        dimension_semantics=("arbitrary",) * axes, vmem_limit_bytes=mib * MIB
    )


def cost(flops, moved, trans=0):
    return pl.CostEstimate(flops=int(flops * WEIGH), bytes_accessed=int(moved * WEIGH), transcendentals=int(trans))


def rope_tables(places):
    half_dim = HEAD_DIM // 2
    freqs = 10000.0 ** (-(jnp.arange(half_dim, dtype=F32) / half_dim))
    phase = places.astype(F32)[:, None] * freqs[None, :]
    cosines, sines = jnp.cos(phase), jnp.sin(phase)
    return jnp.concatenate([cosines, cosines], 1), jnp.concatenate([-sines, sines], 1)


def turn(value, cosines, sines):
    return value * cosines + pltpu.roll(value, HEAD_DIM // 2, 1) * sines


def adamw(weight, grad, first, second, rate):
    first_new = BETA_ONE * first + (1.0 - BETA_ONE) * grad
    second_new = BETA_TWO * second + (1.0 - BETA_TWO) * grad * grad
    first_hat = first_new / (1.0 - BETA_ONE**STEP)
    second_hat = second_new / (1.0 - BETA_TWO**STEP)
    updated = weight - rate * (first_hat / (jnp.sqrt(second_hat) + ADAM_EPS) + DECAY * weight)
    return (first_new, second_new, updated)


def rotate_out(result, part, cosines, sines, out):
    for head in range(2):
        value = result[:, head * HEAD_DIM : (head + 1) * HEAD_DIM]

        @pl.when(part < 2)
        def _():
            out[0, head] = turn(value, cosines[...], sines[...]).astype(BF)

        @pl.when(part == 2)
        def _():
            out[0, head] = value.astype(BF)


def first_kernel(info, tokens, gain_columns, weight, cosines, sines, out, normed, gains):
    part = pl.program_id(0)

    @pl.when(part == 0)
    def _():
        rows = gain_columns[...].astype(F32).T[:8, :]
        gains[...] = rows
        value = tokens[...].astype(F32)
        inverse = lax.rsqrt(jnp.mean(value * value, axis=1, keepdims=True) + EPS)
        normed[...] = (value * inverse * rows[0:1, :]).astype(BF)

    rotate_out(dot(normed[...], weight[...]), part, cosines, sines, out)


def second_kernel(info, normed, weight, cosines, sines, out):
    rotate_out(dot(normed[...], weight[...]), pl.program_id(0), cosines, sines, out)


def project_first(info, tokens, weights, cosines, sines):
    rows = tokens.shape[0]
    return pl.pallas_call(
        first_kernel,
        out_shape=(
            jax.ShapeDtypeStruct((3, 2, rows, HEAD_DIM), BF),
            jax.ShapeDtypeStruct((rows, D), BF),
            jax.ShapeDtypeStruct((8, D), F32),
        ),
        grid_spec=pltpu.PrefetchScalarGridSpec(
            num_scalar_prefetch=1,
            grid=(3,),
            in_specs=[
                pl.BlockSpec((rows, D), lambda j, info: (0, 0)),
                pl.BlockSpec((D, HEAD_DIM), lambda j, info: (0, 12)),
                pl.BlockSpec((D, 256), lambda j, info: (0, 2 * j + 1 - info[0])),
                pl.BlockSpec((rows, HEAD_DIM), lambda j, info: (info[0], 0)),
                pl.BlockSpec((rows, HEAD_DIM), lambda j, info: (info[0], 0)),
            ],
            out_specs=(
                pl.BlockSpec((1, 2, rows, HEAD_DIM), lambda j, info: (j, 0, 0, 0)),
                pl.BlockSpec((rows, D), lambda j, info: (0, 0)),
                pl.BlockSpec((8, D), lambda j, info: (0, 0)),
            ),
        ),
        compiler_params=params(VMEM),
        cost_estimate=cost(0, 0),
        name="project_first",
    )(info, tokens, weights, weights, cosines, sines)


def project_second(info, normed, weights, cosines, sines):
    rows = normed.shape[0]
    return pl.pallas_call(
        second_kernel,
        out_shape=jax.ShapeDtypeStruct((3, 2, rows, HEAD_DIM), BF),
        grid_spec=pltpu.PrefetchScalarGridSpec(
            num_scalar_prefetch=1,
            grid=(3,),
            in_specs=[
                pl.BlockSpec((rows, D), lambda j, info: (0, 0)),
                pl.BlockSpec((D, 256), lambda j, info: (0, 2 * j + info[0])),
                pl.BlockSpec((rows, HEAD_DIM), lambda j, info: (info[0], 0)),
                pl.BlockSpec((rows, HEAD_DIM), lambda j, info: (info[0], 0)),
            ],
            out_specs=pl.BlockSpec((1, 2, rows, HEAD_DIM), lambda j, info: (j, 0, 0, 0)),
        ),
        compiler_params=params(VMEM),
        cost_estimate=cost(0, 0),
        name="project_second",
    )(info, normed, weights, cosines, sines)


def place(scratch, own, other, rank, rows):
    scratch[pl.ds(pl.multiple_of(rank * rows, rows), rows), :] = own
    scratch[pl.ds(pl.multiple_of((1 - rank) * rows, rows), rows), :] = other


def chunks_of(tile, step):
    end = tile * TILE
    spans = [(start, min(step, end - start)) for start in range(0, end, step)]
    return spans + [(end, TILE)]


def causal(scores):
    rows = lax.broadcasted_iota(jnp.int32, scores.shape, 0)
    columns = lax.broadcasted_iota(jnp.int32, scores.shape, 1)
    return jnp.where(rows <= columns, scores, NEGATIVE)


def forward_kernel(
    info, own, other, mem_own, mem_other, bias, keep, send, turned, logs,
    q_s, k_s, v_s, vt_s, mem_s, s_s, out_s,
):
    rank = info[0]
    rows = own.shape[2]
    mem_bias = jnp.where(info[2] > 0, 0.0, NEGATIVE).astype(F32)
    place(q_s, own[0, 0], other[0, 0], rank, rows)
    place(k_s, own[1, 0], other[1, 0], rank, rows)
    place(v_s, own[2, 0], other[2, 0], rank, rows)
    mem_s[rank] = mem_own[:, 0]
    mem_s[1 - rank] = mem_other[:, 0]
    vt_s[...] = v_s[...].astype(F32).T.astype(BF)
    ones = (lax.broadcasted_iota(jnp.int32, (TILE, HEAD_DIM), 1) == 0).astype(BF)
    for tile in range(SEG // TILE):
        here = slice(tile * TILE, (tile + 1) * TILE)
        block = tile * TILE // rows
        query = q_s[here, :]
        wide = jnp.concatenate([query, ones], axis=1)
        spans = chunks_of(tile, 512)
        scores = dot_nt(mem_s[block, 0], query) + mem_bias
        s_s[SEG : SEG + RETR, :] = scores
        top = jnp.max(scores, axis=0, keepdims=True)
        for start, size in spans:
            span = slice(start, start + size)
            if start + size > SEG // 2:
                scores = dot_nt(jnp.concatenate([k_s[span, :], bias[span, :]], axis=1), wide)
            else:
                scores = dot_nt(k_s[span, :], query)
            if start == tile * TILE:
                scores = causal(scores)
            s_s[span, :] = scores
            top = jnp.maximum(top, jnp.max(scores, axis=0, keepdims=True))
        shift = top * SCALE_TWO
        exponent = jnp.exp2(s_s[SEG : SEG + RETR, :] * SCALE_TWO - shift)
        total = jnp.sum(exponent, axis=0, keepdims=True)
        result = dot(mem_s[block, 1].astype(F32).T.astype(BF), exponent.astype(BF))
        for start, size in spans:
            span = slice(start, start + size)
            exponent = jnp.exp2(s_s[span, :] * SCALE_TWO - shift)
            total = total + jnp.sum(exponent, axis=0, keepdims=True)
            result = result + dot(vt_s[:, span], exponent.astype(BF))
        result = result * (1.0 / total)
        turned[0, :, here] = result
        logs[0, :, here] = shift + jnp.log2(total)
        out_s[here, :] = result.T.astype(BF)
    keep[0] = out_s[pl.ds(pl.multiple_of(rank * rows, rows), rows), :]
    send[0] = out_s[pl.ds(pl.multiple_of((1 - rank) * rows, rows), rows), :]


def attend_forward(info, own, other, mem_own, mem_other, bias):
    rows = own.shape[2]
    part = pl.BlockSpec((3, 1, rows, HEAD_DIM), lambda h, info: (0, h, 0, 0))
    mem = pl.BlockSpec((2, 1, RETR, HEAD_DIM), lambda h, info: (0, h, 0, 0))
    half = pl.BlockSpec((1, rows, HEAD_DIM), lambda h, info: (h, 0, 0))
    return pl.pallas_call(
        forward_kernel,
        out_shape=(
            jax.ShapeDtypeStruct((2, rows, HEAD_DIM), BF),
            jax.ShapeDtypeStruct((2, rows, HEAD_DIM), BF),
            jax.ShapeDtypeStruct((2, HEAD_DIM, SEG), F32),
            jax.ShapeDtypeStruct((2, 1, SEG), F32),
        ),
        grid_spec=pltpu.PrefetchScalarGridSpec(
            num_scalar_prefetch=1,
            grid=(2,),
            in_specs=[
                part,
                part,
                mem,
                mem,
                pl.BlockSpec((SEG, HEAD_DIM), lambda h, info: (0, 0)),
            ],
            out_specs=(
                half,
                half,
                pl.BlockSpec((1, HEAD_DIM, SEG), lambda h, info: (h, 0, 0)),
                pl.BlockSpec((1, 1, SEG), lambda h, info: (h, 0, 0)),
            ),
            scratch_shapes=[
                pltpu.VMEM((SEG, HEAD_DIM), BF),
                pltpu.VMEM((SEG, HEAD_DIM), BF),
                pltpu.VMEM((SEG, HEAD_DIM), BF),
                pltpu.VMEM((HEAD_DIM, SEG), BF),
                pltpu.VMEM((2, 2, RETR, HEAD_DIM), BF),
                pltpu.VMEM((SEG + RETR, TILE), F32),
                pltpu.VMEM((SEG, HEAD_DIM), BF),
            ],
        ),
        compiler_params=params(VMEM),
        cost_estimate=cost(0, 0),
        name="attend_forward",
    )(info, own, other, mem_own, mem_other, bias)


def backward_kernel(
    info, own, other, mem_own, mem_other, bias, grad_own, grad_other, turned, logs, cosines, sines,
    keep, send,
    q_s, k_s, v_s, g_s, kt_s, mem_s, dots_s, dq_s, dk_s, dv_s,
):
    rank = info[0]
    rows = own.shape[2]
    mem_bias = jnp.where(info[2] > 0, 0.0, NEGATIVE).astype(F32)
    place(q_s, own[0, 0], other[0, 0], rank, rows)
    place(k_s, own[1, 0], other[1, 0], rank, rows)
    place(v_s, own[2, 0], other[2, 0], rank, rows)
    place(g_s, grad_own[0], grad_other[0], rank, rows)
    mem_s[rank] = mem_own[:, 0]
    mem_s[1 - rank] = mem_other[:, 0]
    kt_s[...] = k_s[...].astype(F32).T.astype(BF)
    dots_s[...] = jnp.sum(g_s[...].astype(F32).T * turned[0], axis=0, keepdims=True)
    dk_s[...] = jnp.zeros_like(dk_s)
    dv_s[...] = jnp.zeros_like(dv_s)
    ones = (lax.broadcasted_iota(jnp.int32, (TILE, HEAD_DIM), 1) == 0).astype(BF)
    for tile in range(SEG // TILE):
        here = slice(tile * TILE, (tile + 1) * TILE)
        block = tile * TILE // rows
        query = q_s[here, :]
        wide = jnp.concatenate([query, ones], axis=1)
        grad = g_s[here, :]
        log = logs[0, :, here]
        dots = dots_s[:, here]
        scores = dot_nt(mem_s[block, 0], query) + mem_bias
        probs = jnp.exp2(scores * SCALE_TWO - log)
        change = (probs * (dot_nt(mem_s[block, 1], grad) - dots)).astype(BF)
        result = dot(mem_s[block, 0].astype(F32).T.astype(BF), change)
        for start, size in chunks_of(tile, 512):
            span = slice(start, start + size)
            keys = k_s[span, :]
            if start + size > SEG // 2:
                scores = dot_nt(jnp.concatenate([keys, bias[span, :]], axis=1), wide)
            else:
                scores = dot_nt(keys, query)
            if start == tile * TILE:
                scores = causal(scores)
            probs = jnp.exp2(scores * SCALE_TWO - log)
            change = (probs * (dot_nt(v_s[span, :], grad) - dots)).astype(BF)
            dv_s[span, :] += dot(probs.astype(BF), grad)
            dk_s[span, :] += dot(change, query)
            result = result + dot(kt_s[:, span], change)
        dq_s[here, :] = turn(result.T * SCALE, cosines[here, :], -sines[here, :]).astype(BF)
    for index in range(2):
        held = pl.ds(pl.multiple_of((rank if index == 0 else 1 - rank) * rows, rows), rows)
        out = keep if index == 0 else send
        out[0, 0] = dq_s[held, :]
        out[1, 0] = turn(dk_s[held, :] * SCALE, cosines[held, :], -sines[held, :]).astype(BF)
        out[2, 0] = dv_s[held, :].astype(BF)


def attend_backward(
    info, own, other, mem_own, mem_other, bias, grad_own, grad_other, turned, logs, cosines, sines, head
):
    rows = own.shape[2]
    part = pl.BlockSpec((3, 1, rows, HEAD_DIM), lambda h, info: (0, head, 0, 0))
    mem = pl.BlockSpec((2, 1, RETR, HEAD_DIM), lambda h, info: (0, head, 0, 0))
    half = pl.BlockSpec((1, rows, HEAD_DIM), lambda h, info: (head, 0, 0))
    table = pl.BlockSpec((SEG, HEAD_DIM), lambda h, info: (0, 0))
    return pl.pallas_call(
        backward_kernel,
        out_shape=(jax.ShapeDtypeStruct((3, 1, rows, HEAD_DIM), BF),) * 2,
        grid_spec=pltpu.PrefetchScalarGridSpec(
            num_scalar_prefetch=1,
            grid=(1,),
            in_specs=[
                part,
                part,
                mem,
                mem,
                table,
                half,
                half,
                pl.BlockSpec((1, HEAD_DIM, SEG), lambda h, info: (head, 0, 0)),
                pl.BlockSpec((1, 1, SEG), lambda h, info: (head, 0, 0)),
                table,
                table,
            ],
            out_specs=(pl.BlockSpec((3, 1, rows, HEAD_DIM), lambda h, info: (0, 0, 0, 0)),) * 2,
            scratch_shapes=[pltpu.VMEM((SEG, HEAD_DIM), BF)] * 4
            + [
                pltpu.VMEM((HEAD_DIM, SEG), BF),
                pltpu.VMEM((2, 2, RETR, HEAD_DIM), BF),
                pltpu.VMEM((1, SEG), F32),
                pltpu.VMEM((SEG, HEAD_DIM), BF),
                pltpu.VMEM((SEG, HEAD_DIM), F32),
                pltpu.VMEM((SEG, HEAD_DIM), F32),
            ],
        ),
        compiler_params=params(VMEM),
        cost_estimate=cost(0, 0),
        name="attend_backward",
    )(
        info, own, other, mem_own, mem_other, bias, grad_own, grad_other, turned, logs, cosines, sines
    )


OUT_AT = 3 * 4 * HEAD_DIM + HEAD_DIM


def columns(width, start):
    return pl.BlockSpec(
        (pl.Element(D), pl.Element(width)),
        lambda *indices: (0, start),
        pipeline_mode=pl.Buffered(1),
    )


def attend_out_kernel(info, own, other, weight, out, joined):
    for piece, pair in ((own, info[0]), (other, 1 - info[0])):
        for head in range(2):
            column = pl.multiple_of((pair * 2 + head) * HEAD_DIM, HEAD_DIM)
            joined[:, pl.ds(column, HEAD_DIM)] = piece[head]
    out[...] = dot_nt(joined[...], weight[...]).astype(BF)


def attend_out_call(info, own, other, weights):
    rows, half = own.shape[1], 4 * HEAD_DIM
    piece = pl.BlockSpec((2, TILE, HEAD_DIM), lambda i, info: (0, i, 0))
    return pl.pallas_call(
        attend_out_kernel,
        out_shape=(jax.ShapeDtypeStruct((rows, D), BF), jax.ShapeDtypeStruct((rows, half), BF)),
        grid_spec=pltpu.PrefetchScalarGridSpec(
            num_scalar_prefetch=1,
            grid=(rows // TILE,),
            in_specs=[piece, piece, columns(half, OUT_AT)],
            out_specs=(
                pl.BlockSpec((TILE, D), lambda i, info: (i, 0)),
                pl.BlockSpec((TILE, half), lambda i, info: (i, 0)),
            ),
        ),
        compiler_params=params(VMEM),
        cost_estimate=cost(0, 0),
        name="attend_out",
    )(info, own, other, weights)


def middle_kernel(tokens, own, other, gain, middle, normed):
    value = tokens[...].astype(F32) + (own[...].astype(F32) + other[...].astype(F32))
    middle[...] = value
    inverse = lax.rsqrt(jnp.mean(value * value, axis=1, keepdims=True) + EPS)
    normed[...] = (value * inverse * gain[...]).astype(BF)


def middle_call(tokens, own, other, gain):
    rows = tokens.shape[0]
    wide = pl.BlockSpec((TILE, D), lambda i: (i, 0))
    return pl.pallas_call(
        middle_kernel,
        out_shape=(jax.ShapeDtypeStruct((rows, D), F32), jax.ShapeDtypeStruct((rows, D), BF)),
        grid=(rows // TILE,),
        in_specs=[wide, wide, wide, pl.BlockSpec((1, D), lambda i: (0, 0))],
        out_specs=(wide, wide),
        compiler_params=params(VMEM),
        cost_estimate=cost(0, 0),
        name="middle",
    )(tokens, own, other, gain)


def feed_kernel(normed, upstream, gate_w, up_w, down_w, *refs):
    hidden, gate_grad, up_grad, back = refs[-4:]
    gate = dot(normed[...], gate_w[...])
    up_part = dot(normed[...], up_w[...])
    sigma = jax.nn.sigmoid(gate)
    silu = gate * sigma
    hidden[...] = (silu * up_part).astype(BF)
    grad = dot(upstream[...], down_w[...])
    grad_gate = (grad * up_part * sigma * (1.0 + gate * (1.0 - sigma))).astype(BF)
    grad_up = (grad * silu).astype(BF)
    gate_grad[...] = grad_gate
    up_grad[...] = grad_up
    back[...] = (dot_nt(grad_gate, gate_w[...]) + dot_nt(grad_up, up_w[...])).astype(BF)


def feed_call(normed, upstream, weights, first, count, earlier):
    rows = normed.shape[0]
    width = FF // 2
    whole = lambda index: pl.BlockSpec((D, width), lambda i: (0, index), pipeline_mode=pl.Buffered(1))
    source = pl.BlockSpec((TILE, D), lambda i: (i + first // TILE, 0))
    narrow = pl.BlockSpec((TILE, width), lambda i: (i + first // TILE, 0))
    return pl.pallas_call(
        feed_kernel,
        out_shape=(jax.ShapeDtypeStruct((rows, width), BF),) * 3
        + (jax.ShapeDtypeStruct((count, D), BF),),
        grid=(count // TILE,),
        in_specs=[source, source, whole(0), whole(1), whole(2)]
        + [pl.BlockSpec(memory_space=pl.ANY)] * len(earlier),
        out_specs=(narrow, narrow, narrow, pl.BlockSpec((TILE, D), lambda i: (i, 0))),
        input_output_aliases={5 + index: index for index in range(len(earlier))},
        compiler_params=params(VMEM),
        cost_estimate=cost(5e7, 0),
        name="feed",
    )(normed, upstream, weights, weights, weights, *earlier)


def out_kernel(hidden, down_w, out):
    out[...] = dot_nt(hidden[...], down_w[...]).astype(BF)


def out_call(hidden, weights):
    count, width = hidden.shape
    return pl.pallas_call(
        out_kernel,
        out_shape=jax.ShapeDtypeStruct((count, D), BF),
        grid=(count // TILE,),
        in_specs=[
            pl.BlockSpec((TILE, width), lambda i: (i, 0)),
            pl.BlockSpec((D, width), lambda i: (0, 2), pipeline_mode=pl.Buffered(1)),
        ],
        out_specs=pl.BlockSpec((TILE, D), lambda i: (i, 0)),
        compiler_params=params(VMEM),
        cost_estimate=cost(5e7, 0),
        name="feed_out",
    )(hidden, weights)


def feed_weight_kernel(normed, upstream, hidden, gate_grad, up_grad, out):
    width = hidden.shape[1]
    left = normed[...].astype(F32).T.astype(BF)
    out[:, :width] = dot(left, gate_grad[...]).astype(BF)
    out[:, width : 2 * width] = dot(left, up_grad[...]).astype(BF)
    left = upstream[...].astype(F32).T.astype(BF)
    out[:, 2 * width :] = dot(left, hidden[...]).astype(BF)


def feed_weight_call(normed, upstream, hidden, gate_grad, up_grad):
    rows, width = hidden.shape
    left = pl.BlockSpec((rows, TILE), lambda i: (0, i))
    whole = pl.BlockSpec((rows, width), lambda i: (0, 0), pipeline_mode=pl.Buffered(1))
    return pl.pallas_call(
        feed_weight_kernel,
        out_shape=pltpu.HBM((D, 3 * width), BF),
        grid=(D // TILE,),
        in_specs=[left, left, whole, whole, whole],
        out_specs=pl.BlockSpec((TILE, 3 * width), lambda i: (i, 0)),
        compiler_params=params(VMEM),
        cost_estimate=cost(5e7, 0),
        name="feed_weights",
    )(normed, upstream, hidden, gate_grad, up_grad)


def residual_kernel(info, middle, back_own, back_other, upstream, gain, weight, *refs):
    grad, low, keep, send, gain_grad = refs[-5:]
    rank = info[0]
    value = middle[...]
    back = back_own[...].astype(F32) + back_other[...].astype(F32)
    inverse = lax.rsqrt(jnp.mean(value * value, axis=1, keepdims=True) + EPS)
    scaled = gain[...] * back
    inner = jnp.mean(scaled * value, axis=1, keepdims=True)
    total = upstream[...].astype(F32) + inverse * scaled - value * (inverse**3 * inner)
    grad[...] = total
    branch = total.astype(BF)
    low[...] = branch

    @pl.when(pl.program_id(0) == 0)
    def _():
        gain_grad[...] = jnp.zeros_like(gain_grad)

    gain_grad[...] += jnp.sum(back * value * inverse, axis=0, keepdims=True)
    for out, pair in ((keep, rank), (send, 1 - rank)):
        column = pl.multiple_of(pair * 2 * HEAD_DIM, 2 * HEAD_DIM)
        result = dot(branch, weight[:, pl.ds(column, 2 * HEAD_DIM)]).astype(BF)
        for head in range(2):
            out[head] = result[:, head * HEAD_DIM : (head + 1) * HEAD_DIM]


def residual_call(info, middle, back_own, back_other, upstream, gain, weights, first, earlier):
    rows, count = middle.shape[0], back_own.shape[0]
    start = first // TILE
    wide = pl.BlockSpec((TILE, D), lambda i, info: (i + start, 0))
    part = pl.BlockSpec((TILE, D), lambda i, info: (i, 0))
    row = pl.BlockSpec((1, D), lambda i, info: (0, 0))
    piece = pl.BlockSpec((2, TILE, HEAD_DIM), lambda i, info: (0, i + start, 0))
    return pl.pallas_call(
        residual_kernel,
        out_shape=(
            jax.ShapeDtypeStruct((rows, D), F32),
            jax.ShapeDtypeStruct((rows, D), BF),
            jax.ShapeDtypeStruct((2, rows, HEAD_DIM), BF),
            jax.ShapeDtypeStruct((2, rows, HEAD_DIM), BF),
            jax.ShapeDtypeStruct((1, D), F32),
        ),
        grid_spec=pltpu.PrefetchScalarGridSpec(
            num_scalar_prefetch=1,
            grid=(count // TILE,),
            in_specs=[wide, part, part, wide, row, columns(4 * HEAD_DIM, OUT_AT)]
            + [pl.BlockSpec(memory_space=pl.ANY)] * len(earlier),
            out_specs=(wide, wide, piece, piece, row),
        ),
        input_output_aliases={7 + index: index for index in range(len(earlier))},
        compiler_params=params(VMEM),
        cost_estimate=cost(5e7 if first + count < rows else 3e11, 0),
        name="residual",
    )(info, middle, back_own, back_other, upstream, gain, weights, *earlier)


def back_kernel(info, own_one, own_two, other_one, other_two, weight, tokens, out, joined, gain_grad):
    rank = info[0]
    for index, piece in enumerate((own_one, own_two, other_one, other_two)):
        pair = (rank, 1 - rank)[index // 2]
        for part in range(3):
            column = pl.multiple_of((part * 4 + pair * 2 + index % 2) * HEAD_DIM, HEAD_DIM)
            joined[:, pl.ds(column, HEAD_DIM)] = piece[part, 0]
    back = dot_nt(joined[...], weight[...])
    out[...] = back.astype(BF)

    @pl.when(pl.program_id(0) == 0)
    def _():
        gain_grad[...] = jnp.zeros_like(gain_grad)

    value = tokens[...].astype(F32)
    inverse = lax.rsqrt(jnp.mean(value * value, axis=1, keepdims=True) + EPS)
    gain_grad[...] += jnp.sum(back * value * inverse, axis=0, keepdims=True)


def back_call(info, pieces, weights, tokens):
    rows = tokens.shape[0]
    width = 3 * 4 * HEAD_DIM
    piece = pl.BlockSpec((3, 1, TILE, HEAD_DIM), lambda i, info: (0, 0, i, 0))
    wide = pl.BlockSpec((TILE, D), lambda i, info: (i, 0))
    return pl.pallas_call(
        back_kernel,
        out_shape=(
            jax.ShapeDtypeStruct((rows, D), BF),
            jax.ShapeDtypeStruct((rows, width), BF),
            jax.ShapeDtypeStruct((1, D), F32),
        ),
        grid_spec=pltpu.PrefetchScalarGridSpec(
            num_scalar_prefetch=1,
            grid=(rows // TILE,),
            in_specs=[
                piece,
                piece,
                piece,
                piece,
                pl.BlockSpec((D, width), lambda i, info: (0, 0)),
                wide,
            ],
            out_specs=(
                wide,
                pl.BlockSpec((TILE, width), lambda i, info: (i, 0)),
                pl.BlockSpec((1, D), lambda i, info: (0, 0)),
            ),
        ),
        compiler_params=params(VMEM),
        cost_estimate=cost(5e7, 0),
        name="back",
    )(info, *pieces, weights, tokens)


def attend_weight_kernel(info, normed, joined, low, attended, gain_one, gain_two, *refs):
    outs, out = refs[:-1], refs[-1]
    step = pl.program_id(0)
    count = len(outs) // 2

    tile, width, half = normed.shape[1], joined.shape[1], attended.shape[1]
    left = normed[...].astype(F32).T.astype(BF)
    out[:, :width] = dot(left, joined[...]).astype(BF)
    left = low[...].astype(F32).T.astype(BF)
    out[:, width : width + half] = dot(left, attended[...]).astype(BF)
    both = jnp.concatenate([gain_one[...], gain_two[...], jnp.zeros((HEAD_DIM - 2, tile), F32)])
    out[:, width + half :] = both.T.astype(BF)
    size = outs[0].shape[1]
    for line in range(tile // (4 * size)):
        place_ = step * (tile // (4 * size)) + line
        for slot in range(count):

            @pl.when(count - 1 - (place_ ^ info[4]) == slot)
            def _():
                for column in range(2):
                    for target, core in ((outs[slot], info[0]), (outs[count + slot], 1 - info[0])):
                        side = info[3] if column == 0 else 1 - info[3]
                        start = pl.multiple_of((line * 4 + side * 2 + core) * size, size)
                        target[column] = out[pl.ds(start, size), :]


def attend_weight_call(info, normed, joined, low, attended, gain_one, gain_two, size):
    rows, width = joined.shape
    half = 4 * HEAD_DIM
    total = width + half + HEAD_DIM
    tile, count = TILE, D // (4 * size)
    left = pl.BlockSpec((rows, tile), lambda i, info: (0, i))
    row = pl.BlockSpec((1, tile), lambda i, info: (0, i))
    return pl.pallas_call(
        attend_weight_kernel,
        out_shape=(jax.ShapeDtypeStruct((2, size, total), BF),) * (2 * count),
        grid_spec=pltpu.PrefetchScalarGridSpec(
            num_scalar_prefetch=1,
            grid=(D // tile,),
            in_specs=[
                left,
                pl.BlockSpec((rows, width), lambda i, info: (0, 0)),
                left,
                pl.BlockSpec((rows, half), lambda i, info: (0, 0)),
                row,
                row,
            ],
            out_specs=(pl.BlockSpec((2, size, total), lambda i, info: (0, 0, 0)),) * (2 * count),
            scratch_shapes=[pltpu.VMEM((tile, total), BF)],
        ),
        compiler_params=params(VMEM),
        cost_estimate=cost(0, 0),
        name="attend_weights",
    )(info, normed, joined, low, attended, gain_one, gain_two)


def input_kernel(grad, back_own, back_other, tokens, gain, out):
    value = tokens[...].astype(F32)
    back = back_own[...].astype(F32) + back_other[...].astype(F32)
    inverse = lax.rsqrt(jnp.mean(value * value, axis=1, keepdims=True) + EPS)
    scaled = gain[...] * back
    inner = jnp.mean(scaled * value, axis=1, keepdims=True)
    out[...] = (grad[...] + inverse * scaled - value * (inverse**3 * inner)).astype(BF)


def input_call(grad, back_own, back_other, tokens, gain):
    rows = tokens.shape[0]
    wide = pl.BlockSpec((TILE, D), lambda i: (i, 0))
    return pl.pallas_call(
        input_kernel,
        out_shape=jax.ShapeDtypeStruct((rows, D), BF),
        grid=(rows // TILE,),
        in_specs=[wide, wide, wide, wide, pl.BlockSpec((1, D), lambda i: (0, 0))],
        out_specs=wide,
        compiler_params=params(VMEM),
        cost_estimate=cost(12 * rows * D, 12 * MIB),
        name="input_grad",
    )(grad, back_own, back_other, tokens, gain)


def choose(line, options):
    value = options[0]
    for here in range(1, len(options)):
        if options[here] is not options[0]:
            value = jnp.where(line == here, options[here], value)
    return value


def pair_kernel(keep, core, mine, theirs):
    total = (keep[...].astype(F32) + core[...].astype(F32)).astype(BF)
    mine[...] = total[0]
    theirs[...] = total[1]


def pair_add(keep, core):
    shape = jax.ShapeDtypeStruct(keep.shape[1:], BF)
    return pl.pallas_call(
        pair_kernel,
        out_shape=(shape, shape),
        compiler_params=pltpu.CompilerParams(vmem_limit_bytes=VMEM * MIB),
        cost_estimate=cost(0, 0),
        name="pair_add",
    )(keep, core)


def low_kernel(left, right, out):
    out[...] = (left[...].astype(F32) + right[...].astype(F32)).astype(out.dtype)


def low_add(left, right):
    return pl.pallas_call(
        low_kernel,
        out_shape=jax.ShapeDtypeStruct(left.shape, BF),
        compiler_params=pltpu.CompilerParams(vmem_limit_bytes=VMEM * MIB),
        cost_estimate=cost(0, 0),
        name="low_add",
    )(left, right)


def chosen_kernel(flags, first, second, up_in, down_in, up, down):
    one, two = first[...].astype(F32), second[...].astype(F32)
    up[...] = (jnp.where(flags[0] > 0, one, two) + up_in[...].astype(F32)).astype(BF)
    down[...] = (jnp.where(flags[1] > 0, one, two) + down_in[...].astype(F32)).astype(BF)


def chosen_add(flags, first, second, up_in, down_in):
    shape = jax.ShapeDtypeStruct(first.shape, BF)
    vmem = pl.BlockSpec(memory_space=pltpu.VMEM)
    return pl.pallas_call(
        chosen_kernel,
        out_shape=(shape, shape),
        in_specs=[pl.BlockSpec(memory_space=pltpu.SMEM)] + [vmem] * 4,
        out_specs=(vmem, vmem),
        compiler_params=pltpu.CompilerParams(vmem_limit_bytes=VMEM * MIB),
        cost_estimate=cost(0, 0),
        name="chosen_add",
    )(flags, first, second, up_in, down_in)


def reduce_rows(keeps, sends, count):
    length = count // 4
    line = lax.axis_index("dp") // 4
    sums = []
    for keep, send in zip(keeps, sends):
        core = lax.ppermute(send, "dp", [(i, i ^ 1) for i in range(count)])
        mine, theirs = pair_add(keep, core)
        other = lax.ppermute(theirs, "dp", [(i, i ^ 2) for i in range(count)])
        sums.append(low_add(mine, other))
    above = below = None
    for step in range(1, length):
        gap = length - step
        slots = lambda towards: [
            length - 1 - (here ^ (here + towards)) if 0 <= here + towards < length else None
            for here in range(length)
        ]
        ups, downs = slots(gap), slots(-gap)
        used = sorted({slot for slot in ups + downs if slot is not None})
        if len(used) == 1 and step == 1:
            up = down = sums[used[0]]
        elif len(used) == 1:
            up, down = low_add(sums[used[0]], below), low_add(sums[used[0]], above)
        elif len(used) == 2:
            flags = jnp.stack(
                [
                    choose(line, [jnp.int32(slot == used[0]) for slot in side])
                    for side in (ups, downs)
                ]
            )
            up, down = chosen_add(flags, sums[used[0]], sums[used[1]], below, above)
        else:
            fill = lambda side: [sums[used[0] if slot is None else slot] for slot in side]
            up, down = choose(line, fill(ups)), choose(line, fill(downs))
            up, down = low_add(up, below), low_add(down, above)
        below = lax.ppermute(up, "dp", [(i, i + 4) for i in range(count - 4) if i // 4 + gap < length])
        above = lax.ppermute(down, "dp", [(i, i - 4) for i in range(4, count) if i // 4 >= gap])
    return sums[-1], below, above


def pin(values):
    return lax.optimization_barrier(values)


def body(
    tokens,
    cotangent,
    proj_qkv,
    proj_out,
    proj_gate_up,
    proj_down,
    norm_gains,
    first_qkv,
    first_out,
    first_gate_up,
    first_down,
    first_gains,
    second_qkv,
    second_out,
    second_gate_up,
    second_down,
    second_gains,
    cache,
    doc_segments,
    padding,
    retrieval,
):
    rows = tokens.shape[0]
    count = lax.axis_size("dp")
    device = lax.axis_index("dp")
    group = lax.axis_index("mp")
    rank = device % 2
    segment = device // 2
    shard = proj_qkv.shape[1]
    local = proj_qkv.shape[2]
    hidden_here = proj_gate_up.shape[2]
    core_pairs = [(i, i ^ 1) for i in range(count)]

    def across(value):
        return lax.ppermute(value, "mp", [(0, 1), (1, 0)])

    def beside(value):
        return lax.ppermute(value, "dp", core_pairs)

    gain_columns = jnp.pad(norm_gains.astype(BF).T, ((0, 0), (0, HEAD_DIM - 2)))
    shard_one = jnp.concatenate(
        [proj_qkv[part].astype(BF) for part in range(3)] + [gain_columns, proj_out.astype(BF).T],
        axis=1,
    )
    shard_two = jnp.concatenate(
        [proj_gate_up[0].astype(BF), proj_gate_up[1].astype(BF), proj_down.astype(BF).T], axis=1
    )
    length = count // 4
    weights_one = lax.all_gather(shard_one, "dp", axis=0, tiled=True)

    places = jnp.arange(SEG, dtype=jnp.int32)
    starts = jnp.cumsum(doc_segments) - doc_segments
    memory_on = jnp.logical_not(jnp.any(starts == segment))
    side = (device // 2) % 2
    info = jnp.stack([rank, group, memory_on.astype(jnp.int32), side, device // 4]).astype(jnp.int32)
    cosines, sines = rope_tables(places)
    valid = lax.dynamic_slice_in_dim(padding, segment * SEG, SEG)
    lane = jnp.arange(HEAD_DIM, dtype=jnp.int32)[None, :]
    bias = jnp.where((valid[:, None] == 0) & (lane == 0), NEGATIVE, 0.0).astype(BF)
    fetched = cache[retrieval[0]].reshape(RETR, 2, 2, 2, HEAD_DIM).transpose(2, 1, 3, 0, 4)
    mem_own = lax.dynamic_index_in_dim(fetched, rank, keepdims=False)
    mem_other = beside(lax.dynamic_index_in_dim(fetched, 1 - rank, keepdims=False))
    weights_one, shard_two, mem_own, mem_other, bias, cosines, sines = pin(
        (weights_one, shard_two, mem_own, mem_other, bias, cosines, sines)
    )
    weights_two = lax.all_gather(shard_two, "dp", axis=0, tiled=True)

    send, normed_one, gains = project_first(info, tokens, weights_one, cosines, sines)
    gain_one, gain_two = gains[0:1], gains[1:2]
    other = beside(send)
    own = project_second(info, normed_one, weights_one, cosines, sines)
    out_keep, out_send, turned, logs = attend_forward(info, own, other, mem_own, mem_other, bias)
    attend_part, attended = attend_out_call(info, out_keep, beside(out_send), weights_one)
    middle, normed_two = middle_call(tokens, attend_part, across(attend_part), gain_two)

    earlier, backs, backs_other = (), [], []
    for first in range(0, rows, TILE):
        *earlier, back = feed_call(normed_two, cotangent, weights_two, first, TILE, earlier)
        backs.append(back)
        backs_other.append(across(back))
    hidden, grad_gate, grad_up = earlier
    feed_grads = feed_weight_call(normed_two, cotangent, hidden, grad_gate, grad_up)
    hidden, _ = pin((hidden, feed_grads))
    feed_part = out_call(hidden, weights_two)
    middle, _ = pin((middle, feed_part))
    earlier, gain_two_grad = (), 0.0
    for index, first in enumerate(range(0, rows, TILE)):
        if first + TILE == rows:
            backs_other[index], feed_pinned = pin((backs_other[index], feed_part))
            feed_other = across(feed_pinned)
        *earlier, gain_part = residual_call(
            info, middle, backs[index], backs_other[index], cotangent, gain_two, weights_one, first, earlier
        )
        gain_two_grad = gain_two_grad + gain_part
    grad_middle, grad_low, grad_keep, grad_send = earlier
    grad_other = beside(grad_send)

    d_keeps, d_others = [], []
    for head in range(2):
        d_keep, d_send = attend_backward(
            info, own, other, mem_own, mem_other, bias, grad_keep, grad_other, turned, logs,
            cosines, sines, head,
        )
        d_keeps.append(d_keep)
        d_others.append(beside(d_send))
    back_one, joined, gain_one_grad = back_call(info, d_keeps + d_others, weights_one, tokens)
    back_one_other = across(back_one)
    attend_slots = attend_weight_call(
        info, normed_one, joined, grad_low, attended, gain_one_grad, gain_two_grad, shard
    )
    feed_other, attend_slots = pin((feed_other, attend_slots))
    total, below, above = reduce_rows(attend_slots[:length], attend_slots[length:], count)
    input_grad = input_call(grad_middle, back_one, back_one_other, tokens, gain_one)
    block_out = (middle + (feed_part.astype(F32) + feed_other.astype(F32))).astype(BF)
    input_grad, total, below, above = pin((input_grad, total, below, above))
    attend_sum = total.astype(F32) + (below.astype(F32) + above.astype(F32))
    feed_sum = lax.psum_scatter(feed_grads, "dp", scatter_dimension=0, tiled=True).astype(F32)
    gate_up_sum = jnp.stack([feed_sum[:, :hidden_here], feed_sum[:, hidden_here : 2 * hidden_here]])
    down_sum = feed_sum[:, 2 * hidden_here :].T
    qkv_sum = jnp.stack([attend_sum[:, part * local : (part + 1) * local] for part in range(3)])
    out_sum = attend_sum[:, 3 * local : 4 * local].T
    gains_sum = attend_sum[:, 4 * local : 4 * local + 2].T
    gains_sum = jnp.concatenate([gains_sum[0:1] + across(gains_sum[0:1]), gains_sum[1:2]], axis=0)

    qkv_first, qkv_second, qkv_new = adamw(
        proj_qkv, qkv_sum, first_qkv, second_qkv, 0.5 / math.sqrt(D)
    )
    out_first, out_second, out_new = adamw(
        proj_out, out_sum, first_out, second_out, 0.5 / math.sqrt(max(1, 4 * D // SEG))
    )
    gate_up_first, gate_up_second, gate_up_new = adamw(
        proj_gate_up, gate_up_sum, first_gate_up, second_gate_up, 0.5 / math.sqrt(D)
    )
    down_first, down_second, down_new = adamw(
        proj_down, down_sum, first_down, second_down, 0.5 / math.sqrt(FF)
    )
    gains_first, gains_second, gains_new = adamw(
        norm_gains, gains_sum, first_gains, second_gains, 0.6
    )
    return (
        block_out,
        input_grad,
        qkv_first,
        qkv_second,
        qkv_new,
        out_first,
        out_second,
        out_new,
        gate_up_first,
        gate_up_second,
        gate_up_new,
        down_first,
        down_second,
        down_new,
        gains_first,
        gains_second,
        gains_new,
    )


def solution(mesh):
    return jax.shard_map(
        body,
        mesh=mesh,
        in_specs=(
            P("dp", None),
            P("dp", None),
            P(None, "dp", "mp"),
            P("mp", "dp"),
            P(None, "dp", "mp"),
            P("mp", "dp"),
            P(None, "dp"),
            P(None, "dp", "mp"),
            P("mp", "dp"),
            P(None, "dp", "mp"),
            P("mp", "dp"),
            P(None, "dp"),
            P(None, "dp", "mp"),
            P("mp", "dp"),
            P(None, "dp", "mp"),
            P("mp", "dp"),
            P(None, "dp"),
            P("dp", None, "mp"),
            P(),
            P(),
            P("dp", None),
        ),
        out_specs=(
            P("dp", None),
            P("dp", None),
            P(None, "dp", "mp"),
            P(None, "dp", "mp"),
            P(None, "dp", "mp"),
            P("mp", "dp"),
            P("mp", "dp"),
            P("mp", "dp"),
            P(None, "dp", "mp"),
            P(None, "dp", "mp"),
            P(None, "dp", "mp"),
            P("mp", "dp"),
            P("mp", "dp"),
            P("mp", "dp"),
            P(None, "dp"),
            P(None, "dp"),
            P(None, "dp"),
        ),
        check_vma=False,
    )
```

```python
import functools
import math

import jax
import jax.numpy as jnp
from jax import lax
from jax.experimental import pallas as pl
from jax.experimental.pallas import tpu as pltpu
from jax.sharding import PartitionSpec as P

D = 1024
HEAD_DIM = 128
FF = 2816
SEG = 2048
RETR = 128
STEP = 10

EPS = 1e-05
BETA_ONE = 0.9
BETA_TWO = 0.95
ADAM_EPS = 1e-08
DECAY = 0.1
NEGATIVE = -1e30
SCALE = HEAD_DIM**-0.5
SCALE_TWO = SCALE * math.log2(math.e)

BF = jnp.bfloat16
F32 = jnp.float32
MIB = 1024 * 1024
TILE = 256
PART = 512
VMEM = 26
WEIGH = 1.0


def dot(left, right):
    return jnp.dot(left, right, preferred_element_type=F32)


def dot_nt(left, right):
    return lax.dot_general(left, right, (((1,), (1,)), ((), ())), preferred_element_type=F32)


def dot_tn(left, right):
    return lax.dot_general(left, right, (((0,), (0,)), ((), ())), preferred_element_type=F32)


def params(mib, axes=1):
    return pltpu.CompilerParams(
        dimension_semantics=("arbitrary",) * axes, vmem_limit_bytes=mib * MIB
    )


def cost(flops, moved, trans=0):
    return pl.CostEstimate(flops=int(flops * WEIGH), bytes_accessed=int(moved * WEIGH), transcendentals=int(trans))


def rope_tables(places):
    half_dim = HEAD_DIM // 2
    freqs = 10000.0 ** (-(jnp.arange(half_dim, dtype=F32) / half_dim))
    phase = places.astype(F32)[:, None] * freqs[None, :]
    cosines, sines = jnp.cos(phase), jnp.sin(phase)
    return jnp.concatenate([cosines, cosines], 1), jnp.concatenate([-sines, sines], 1)


def turn(value, cosines, sines):
    return value * cosines + pltpu.roll(value, HEAD_DIM // 2, 1) * sines


def adamw(weight, grad, first, second, rate):
    first_new = BETA_ONE * first + (1.0 - BETA_ONE) * grad
    second_new = BETA_TWO * second + (1.0 - BETA_TWO) * grad * grad
    first_hat = first_new / (1.0 - BETA_ONE**STEP)
    second_hat = second_new / (1.0 - BETA_TWO**STEP)
    updated = weight - rate * (first_hat / (jnp.sqrt(second_hat) + ADAM_EPS) + DECAY * weight)
    return (first_new, second_new, updated)


def rotate_out(result, part, cosines, sines, out):
    for head in range(2):
        value = result[:, head * HEAD_DIM : (head + 1) * HEAD_DIM]

        @pl.when(part < 2)
        def _():
            out[0, head] = turn(value, cosines[...], sines[...]).astype(BF)

        @pl.when(part == 2)
        def _():
            out[0, head] = value.astype(BF)


def first_kernel(info, tokens, gain_columns, weight, cosines, sines, out, normed, gains):
    part = pl.program_id(0)

    @pl.when(part == 0)
    def _():
        rows = gain_columns[...].astype(F32).T[:8, :]
        gains[...] = rows
        value = tokens[...].astype(F32)
        inverse = lax.rsqrt(jnp.mean(value * value, axis=1, keepdims=True) + EPS)
        normed[...] = (value * inverse * rows[0:1, :]).astype(BF)

    rotate_out(dot(normed[...], weight[...]), part, cosines, sines, out)


def second_kernel(info, normed, weight, cosines, sines, out):
    rotate_out(dot(normed[...], weight[...]), pl.program_id(0), cosines, sines, out)


def project_first(info, tokens, weights, cosines, sines):
    rows = tokens.shape[0]
    return pl.pallas_call(
        first_kernel,
        out_shape=(
            jax.ShapeDtypeStruct((3, 2, rows, HEAD_DIM), BF),
            jax.ShapeDtypeStruct((rows, D), BF),
            jax.ShapeDtypeStruct((8, D), F32),
        ),
        grid_spec=pltpu.PrefetchScalarGridSpec(
            num_scalar_prefetch=1,
            grid=(3,),
            in_specs=[
                pl.BlockSpec((rows, D), lambda j, info: (0, 0)),
                pl.BlockSpec((D, HEAD_DIM), lambda j, info: (0, 12)),
                pl.BlockSpec((D, 256), lambda j, info: (0, 2 * j + 1 - info[0])),
                pl.BlockSpec((rows, HEAD_DIM), lambda j, info: (info[0], 0)),
                pl.BlockSpec((rows, HEAD_DIM), lambda j, info: (info[0], 0)),
            ],
            out_specs=(
                pl.BlockSpec((1, 2, rows, HEAD_DIM), lambda j, info: (j, 0, 0, 0)),
                pl.BlockSpec((rows, D), lambda j, info: (0, 0)),
                pl.BlockSpec((8, D), lambda j, info: (0, 0)),
            ),
        ),
        compiler_params=params(VMEM),
        cost_estimate=cost(0, 0),
        name="project_first",
    )(info, in_hbm(tokens), weights, weights, in_hbm(cosines), in_hbm(sines))


def project_second(info, normed, weights, cosines, sines):
    rows = normed.shape[0]
    return pl.pallas_call(
        second_kernel,
        out_shape=jax.ShapeDtypeStruct((3, 2, rows, HEAD_DIM), BF),
        grid_spec=pltpu.PrefetchScalarGridSpec(
            num_scalar_prefetch=1,
            grid=(3,),
            in_specs=[
                pl.BlockSpec((rows, D), lambda j, info: (0, 0)),
                pl.BlockSpec((D, 256), lambda j, info: (0, 2 * j + info[0])),
                pl.BlockSpec((rows, HEAD_DIM), lambda j, info: (info[0], 0)),
                pl.BlockSpec((rows, HEAD_DIM), lambda j, info: (info[0], 0)),
            ],
            out_specs=pl.BlockSpec((1, 2, rows, HEAD_DIM), lambda j, info: (j, 0, 0, 0)),
        ),
        compiler_params=params(VMEM),
        cost_estimate=cost(0, 0),
        name="project_second",
    )(info, normed, weights, cosines, sines)


def place(scratch, own, other, rank, rows):
    scratch[pl.ds(pl.multiple_of(rank * rows, rows), rows), :] = own
    scratch[pl.ds(pl.multiple_of((1 - rank) * rows, rows), rows), :] = other


def chunks_of(tile, step):
    end = tile * TILE
    spans = [(start, min(step, end - start)) for start in range(0, end, step)]
    return spans + [(end, TILE)]


def causal(scores):
    rows = lax.broadcasted_iota(jnp.int32, scores.shape, 0)
    columns = lax.broadcasted_iota(jnp.int32, scores.shape, 1)
    return jnp.where(rows <= columns, scores, NEGATIVE)


def forward_kernel(
    info, own, other, mem_own, mem_other, bias, keep, send, turned, logs,
    q_s, k_s, v_s, vt_s, mem_s, s_s, out_s,
):
    rank = info[0]
    rows = own.shape[2]
    mem_bias = jnp.where(info[2] > 0, 0.0, NEGATIVE).astype(F32)
    place(q_s, own[0, 0], other[0, 0], rank, rows)
    place(k_s, own[1, 0], other[1, 0], rank, rows)
    place(v_s, own[2, 0], other[2, 0], rank, rows)
    mem_s[rank] = mem_own[:, 0]
    mem_s[1 - rank] = mem_other[:, 0]
    vt_s[...] = v_s[...].astype(F32).T.astype(BF)
    ones = (lax.broadcasted_iota(jnp.int32, (TILE, HEAD_DIM), 1) == 0).astype(BF)
    for tile in range(SEG // TILE):
        here = slice(tile * TILE, (tile + 1) * TILE)
        block = tile * TILE // rows
        query = q_s[here, :]
        wide = jnp.concatenate([query, ones], axis=1)
        spans = chunks_of(tile, 512)
        scores = dot_nt(mem_s[block, 0], query) + mem_bias
        s_s[SEG : SEG + RETR, :] = scores
        top = jnp.max(scores, axis=0, keepdims=True)
        for start, size in spans:
            span = slice(start, start + size)
            if start + size > SEG // 2:
                scores = dot_nt(jnp.concatenate([k_s[span, :], bias[span, :]], axis=1), wide)
            else:
                scores = dot_nt(k_s[span, :], query)
            if start == tile * TILE:
                scores = causal(scores)
            s_s[span, :] = scores
            top = jnp.maximum(top, jnp.max(scores, axis=0, keepdims=True))
        shift = top * SCALE_TWO
        exponent = jnp.exp2(s_s[SEG : SEG + RETR, :] * SCALE_TWO - shift)
        total = jnp.sum(exponent, axis=0, keepdims=True)
        result = dot(mem_s[block, 1].astype(F32).T.astype(BF), exponent.astype(BF))
        for start, size in spans:
            span = slice(start, start + size)
            exponent = jnp.exp2(s_s[span, :] * SCALE_TWO - shift)
            total = total + jnp.sum(exponent, axis=0, keepdims=True)
            result = result + dot(vt_s[:, span], exponent.astype(BF))
        result = result * (1.0 / total)
        turned[0, :, here] = result
        logs[0, :, here] = shift + jnp.log2(total)
        out_s[here, :] = result.T.astype(BF)
    keep[0] = out_s[pl.ds(pl.multiple_of(rank * rows, rows), rows), :]
    send[0] = out_s[pl.ds(pl.multiple_of((1 - rank) * rows, rows), rows), :]


def attend_forward(info, own, other, mem_own, mem_other, bias):
    rows = own.shape[2]
    part = pl.BlockSpec((3, 1, rows, HEAD_DIM), lambda h, info: (0, h, 0, 0))
    mem = pl.BlockSpec((2, 1, RETR, HEAD_DIM), lambda h, info: (0, h, 0, 0))
    half = pl.BlockSpec((1, rows, HEAD_DIM), lambda h, info: (h, 0, 0))
    return pl.pallas_call(
        forward_kernel,
        out_shape=(
            jax.ShapeDtypeStruct((2, rows, HEAD_DIM), BF),
            jax.ShapeDtypeStruct((2, rows, HEAD_DIM), BF),
            pltpu.HBM((2, HEAD_DIM, SEG), F32),
            jax.ShapeDtypeStruct((2, 1, SEG), F32),
        ),
        grid_spec=pltpu.PrefetchScalarGridSpec(
            num_scalar_prefetch=1,
            grid=(2,),
            in_specs=[
                part,
                part,
                mem,
                mem,
                pl.BlockSpec((SEG, HEAD_DIM), lambda h, info: (0, 0)),
            ],
            out_specs=(
                half,
                half,
                pl.BlockSpec((1, HEAD_DIM, SEG), lambda h, info: (h, 0, 0)),
                pl.BlockSpec((1, 1, SEG), lambda h, info: (h, 0, 0)),
            ),
            scratch_shapes=[
                pltpu.VMEM((SEG, HEAD_DIM), BF),
                pltpu.VMEM((SEG, HEAD_DIM), BF),
                pltpu.VMEM((SEG, HEAD_DIM), BF),
                pltpu.VMEM((HEAD_DIM, SEG), BF),
                pltpu.VMEM((2, 2, RETR, HEAD_DIM), BF),
                pltpu.VMEM((SEG + RETR, TILE), F32),
                pltpu.VMEM((SEG, HEAD_DIM), BF),
            ],
        ),
        compiler_params=params(VMEM),
        cost_estimate=cost(0, 0),
        name="attend_forward",
    )(info, own, other, mem_own, mem_other, bias)


def backward_kernel(
    info, own, other, mem_own, mem_other, bias, grad_own, grad_other, turned, logs, cosines, sines,
    keep, send, send_v,
    q_s, k_s, v_s, g_s, kt_s, mem_s, dots_s, dq_s, dk_s, dv_s,
):
    rank = info[0]
    rows = own.shape[2]
    mem_bias = jnp.where(info[2] > 0, 0.0, NEGATIVE).astype(F32)
    place(q_s, own[0, 0], other[0, 0], rank, rows)
    place(k_s, own[1, 0], other[1, 0], rank, rows)
    place(v_s, own[2, 0], other[2, 0], rank, rows)
    place(g_s, grad_own[0], grad_other[0], rank, rows)
    mem_s[rank] = mem_own[:, 0]
    mem_s[1 - rank] = mem_other[:, 0]
    kt_s[...] = k_s[...].astype(F32).T.astype(BF)
    dots_s[...] = jnp.sum(g_s[...].astype(F32).T * turned[0], axis=0, keepdims=True)
    dk_s[...] = jnp.zeros_like(dk_s)
    dv_s[...] = jnp.zeros_like(dv_s)
    ones = (lax.broadcasted_iota(jnp.int32, (TILE, HEAD_DIM), 1) == 0).astype(BF)
    for tile in range(SEG // TILE):
        here = slice(tile * TILE, (tile + 1) * TILE)
        block = tile * TILE // rows
        query = q_s[here, :]
        wide = jnp.concatenate([query, ones], axis=1)
        grad = g_s[here, :]
        log = logs[0, :, here]
        dots = dots_s[:, here]
        scores = dot_nt(mem_s[block, 0], query) + mem_bias
        probs = jnp.exp2(scores * SCALE_TWO - log)
        change = (probs * (dot_nt(mem_s[block, 1], grad) - dots)).astype(BF)
        result = dot(mem_s[block, 0].astype(F32).T.astype(BF), change)
        for start, size in chunks_of(tile, 512):
            span = slice(start, start + size)
            keys = k_s[span, :]
            if start + size > SEG // 2:
                scores = dot_nt(jnp.concatenate([keys, bias[span, :]], axis=1), wide)
            else:
                scores = dot_nt(keys, query)
            if start == tile * TILE:
                scores = causal(scores)
            probs = jnp.exp2(scores * SCALE_TWO - log)
            change = (probs * (dot_nt(v_s[span, :], grad) - dots)).astype(BF)
            dv_s[span, :] += dot(probs.astype(BF), grad)
            dk_s[span, :] += dot(change, query)
            result = result + dot(kt_s[:, span], change)
        dq_s[here, :] = turn(result.T * SCALE, cosines[here, :], -sines[here, :]).astype(BF)
    for outs, place_ in (((keep.at[0], keep.at[1], keep.at[2]), rank), ((send.at[0], send.at[1], send_v.at[0]), 1 - rank)):
        held = pl.ds(pl.multiple_of(place_ * rows, rows), rows)
        outs[0][0] = dq_s[held, :]
        outs[1][0] = turn(dk_s[held, :] * SCALE, cosines[held, :], -sines[held, :]).astype(BF)
        outs[2][0] = dv_s[held, :].astype(BF)


def attend_backward(
    info, own, other, mem_own, mem_other, bias, grad_own, grad_other, turned, logs, cosines, sines, head
):
    rows = own.shape[2]
    part = pl.BlockSpec((3, 1, rows, HEAD_DIM), lambda h, info: (0, head, 0, 0))
    mem = pl.BlockSpec((2, 1, RETR, HEAD_DIM), lambda h, info: (0, head, 0, 0))
    half = pl.BlockSpec((1, rows, HEAD_DIM), lambda h, info: (head, 0, 0))
    table = pl.BlockSpec((SEG, HEAD_DIM), lambda h, info: (0, 0))
    return pl.pallas_call(
        backward_kernel,
        out_shape=tuple(jax.ShapeDtypeStruct((parts, 1, rows, HEAD_DIM), BF) for parts in (3, 2, 1)),
        grid_spec=pltpu.PrefetchScalarGridSpec(
            num_scalar_prefetch=1,
            grid=(1,),
            in_specs=[
                part,
                part,
                mem,
                mem,
                table,
                half,
                pl.BlockSpec((1, rows, HEAD_DIM), lambda h, info: (0, 0, 0)),
                pl.BlockSpec((1, HEAD_DIM, SEG), lambda h, info: (head, 0, 0)),
                pl.BlockSpec((1, 1, SEG), lambda h, info: (head, 0, 0)),
                table,
                table,
            ],
            out_specs=tuple(
                pl.BlockSpec((parts, 1, rows, HEAD_DIM), lambda h, info: (0, 0, 0, 0)) for parts in (3, 2, 1)
            ),
            scratch_shapes=[pltpu.VMEM((SEG, HEAD_DIM), BF)] * 4
            + [
                pltpu.VMEM((HEAD_DIM, SEG), BF),
                pltpu.VMEM((2, 2, RETR, HEAD_DIM), BF),
                pltpu.VMEM((1, SEG), F32),
                pltpu.VMEM((SEG, HEAD_DIM), BF),
                pltpu.VMEM((SEG, HEAD_DIM), F32),
                pltpu.VMEM((SEG, HEAD_DIM), F32),
            ],
        ),
        compiler_params=params(VMEM),
        cost_estimate=cost(0, 0),
        name="attend_backward",
    )(
        info, own, other, mem_own, mem_other, bias, grad_own, grad_other, turned, logs, cosines, sines
    )


OUT_AT = 3 * FF // 2


def in_hbm(value):
    return pltpu.with_memory_space_constraint(value, pltpu.HBM)


def columns(width, start):
    return pl.BlockSpec(
        (pl.Element(D), pl.Element(width)), start, pipeline_mode=pl.Buffered(1)
    )


def middle_kernel(info, *refs):
    pieces, (tokens, weight, gain, middle, normed, attended, joined) = refs[:4], refs[4:]
    rank, group = info[0], info[1]
    for index, piece in enumerate(pieces):
        pair = (rank, 1 - rank)[index % 2]
        side = (group, 1 - group)[index // 2]
        for head in range(2):
            column = pl.multiple_of((side * 4 + pair * 2 + head) * HEAD_DIM, HEAD_DIM)
            joined[:, pl.ds(column, HEAD_DIM)] = piece[head]
    half = attended.shape[1]
    attended[...] = joined[:, pl.ds(pl.multiple_of(group * half, half), half)]
    value = tokens[...].astype(F32) + dot_nt(joined[...], weight[...])
    middle[...] = value
    inverse = lax.rsqrt(jnp.mean(value * value, axis=1, keepdims=True) + EPS)
    normed[...] = (value * inverse * gain[...]).astype(BF)


def middle_call(info, pieces, tokens, weights, gain, chunk):
    half = 4 * HEAD_DIM
    first = chunk * (PART // TILE)
    piece = pl.BlockSpec((2, TILE, HEAD_DIM), lambda i, info: (0, i + first, 0))
    one = pl.BlockSpec((TILE, D), lambda i, info: (i, 0))
    return pl.pallas_call(
        middle_kernel,
        out_shape=(
            pltpu.HBM((PART, D), F32),
            jax.ShapeDtypeStruct((PART, D), BF),
            jax.ShapeDtypeStruct((PART, half), BF),
        ),
        grid_spec=pltpu.PrefetchScalarGridSpec(
            num_scalar_prefetch=1,
            grid=(PART // TILE,),
            in_specs=[piece] * 4
            + [
                pl.BlockSpec((TILE, D), lambda i, info: (i + first, 0)),
                columns(D, lambda i, info: (0, OUT_AT)),
                pl.BlockSpec((1, D), lambda i, info: (0, 0)),
            ],
            out_specs=(one, one, pl.BlockSpec((TILE, half), lambda i, info: (i, 0))),
            scratch_shapes=[pltpu.VMEM((TILE, D), BF)],
        ),
        compiler_params=params(VMEM),
        cost_estimate=cost(0, 0),
        name="middle",
    )(info, *[in_hbm(piece) for piece in pieces], in_hbm(tokens), in_hbm(weights), gain)


def feed_kernel(normed, upstream, gate_w, up_w, down_w, *refs):
    hidden, gate_grad, up_grad, feed, back = refs[-5:]
    gate = dot(normed[...], gate_w[...])
    up_part = dot(normed[...], up_w[...])
    sigma = jax.nn.sigmoid(gate)
    silu = gate * sigma
    low = (silu * up_part).astype(BF)
    hidden[...] = low
    feed[...] = dot_nt(low, down_w[...]).astype(BF)
    grad = dot(upstream[...], down_w[...])
    grad_gate = (grad * up_part * sigma * (1.0 + gate * (1.0 - sigma))).astype(BF)
    grad_up = (grad * silu).astype(BF)
    gate_grad[...] = grad_gate
    up_grad[...] = grad_up
    back[...] = (dot_nt(grad_gate, gate_w[...]) + dot_nt(grad_up, up_w[...])).astype(BF)


def feed_call(normed, upstream, weights, first, count, earlier):
    rows = upstream.shape[0]
    width = FF // 2
    whole = lambda index: pl.BlockSpec((D, width), lambda i: (0, index), pipeline_mode=pl.Buffered(1))
    source = pl.BlockSpec((TILE, D), lambda i: (i + first // TILE, 0))
    narrow = pl.BlockSpec((TILE, width), lambda i: (i + first // TILE, 0))
    return pl.pallas_call(
        feed_kernel,
        out_shape=(pltpu.HBM((rows, width), BF),) * 3
        + (jax.ShapeDtypeStruct((rows, D), BF), jax.ShapeDtypeStruct((count, D), BF)),
        grid=(count // TILE,),
        in_specs=[pl.BlockSpec((TILE, D), lambda i: (first % PART // TILE, 0)), source, whole(0), whole(1), whole(2)]
        + [pl.BlockSpec(memory_space=pl.ANY)] * len(earlier),
        out_specs=(narrow, narrow, narrow, source, pl.BlockSpec((TILE, D), lambda i: (i, 0))),
        input_output_aliases={5 + index: index for index in range(len(earlier))},
        compiler_params=params(VMEM),
        cost_estimate=cost(5e7, 0),
        name="feed",
    )(normed, upstream, weights, weights, weights, *earlier)


def feed_weight_kernel(upstream, hidden, gate_grad, up_grad, *refs):
    normed, (out, held, left_s, sems, left_sem) = refs[:-5], refs[-5:]
    part, tile = pl.program_id(0), pl.program_id(1)
    copies = [
        pltpu.make_async_copy(source, held.at[index], sems.at[index])
        for index, source in enumerate((gate_grad, up_grad, hidden))
    ]
    chunks = [
        pltpu.make_async_copy(chunk, left_s.at[0, pl.ds(index * PART, PART), :], left_sem.at[index])
        for index, chunk in enumerate(normed)
    ]
    chunks.append(pltpu.make_async_copy(upstream, left_s.at[1], left_sem.at[len(normed)]))

    @pl.when((part == 0) & (tile == 0))
    def _():
        for copy in chunks[:-1]:
            copy.start()
        copies[0].start()
        copies[1].start()
        chunks[-1].start()
        copies[2].start()
        for copy in chunks[:-1]:
            copy.wait()
        copies[0].wait()

    @pl.when((part == 1) & (tile == 0))
    def _():
        copies[1].wait()

    @pl.when((part == 2) & (tile == 0))
    def _():
        chunks[-1].wait()
        copies[2].wait()

    column = pl.multiple_of(tile * TILE, TILE)
    left = left_s[part // 2, :, pl.ds(column, TILE)].astype(F32).T.astype(BF)
    out[...] = dot(left, held[part]).astype(BF)


def feed_weight_call(normed, upstream, hidden, gate_grad, up_grad):
    rows, width = hidden.shape
    anywhere = pl.BlockSpec(memory_space=pl.ANY)
    return pl.pallas_call(
        feed_weight_kernel,
        out_shape=pltpu.HBM((D, 3 * width), BF),
        grid=(3, D // TILE),
        in_specs=[anywhere] * (4 + len(normed)),
        out_specs=pl.BlockSpec((TILE, width), lambda part, tile: (tile, part)),
        scratch_shapes=[
            pltpu.VMEM((3, rows, width), BF),
            pltpu.VMEM((2, rows, D), BF),
            pltpu.SemaphoreType.DMA((3,)),
            pltpu.SemaphoreType.DMA((len(normed) + 1,)),
        ],
        compiler_params=params(VMEM, 2),
        cost_estimate=cost(5e7, 0),
        name="feed_weights",
    )(*[in_hbm(value) for value in (upstream, hidden, gate_grad, up_grad, *normed)])


def residual_kernel(info, middle, back_own, back_other, upstream, gain, weight, *refs):
    grad, low, keep, send_one, send_two = refs[-5:]
    rank = info[0]
    value = middle[...]
    back = back_own[...].astype(F32) + back_other[...].astype(F32)
    inverse = lax.rsqrt(jnp.mean(value * value, axis=1, keepdims=True) + EPS)
    scaled = gain[...] * back
    inner = jnp.mean(scaled * value, axis=1, keepdims=True)
    total = upstream[...].astype(F32) + inverse * scaled - value * (inverse**3 * inner)
    grad[...] = total
    branch = total.astype(BF)
    low[...] = branch

    for outs, pair in (((keep.at[0], keep.at[1]), rank), ((send_one.at[0], send_two.at[0]), 1 - rank)):
        column = pl.multiple_of(pair * 2 * HEAD_DIM, 2 * HEAD_DIM)
        result = dot(branch, weight[:, pl.ds(column, 2 * HEAD_DIM)]).astype(BF)
        for head in range(2):
            outs[head][...] = result[:, head * HEAD_DIM : (head + 1) * HEAD_DIM]


def residual_call(info, middle, back_own, back_other, upstream, gain, weights, first, earlier):
    rows, count = upstream.shape[0], back_own.shape[0]
    start, half = first // TILE, 4 * HEAD_DIM
    wide = pl.BlockSpec((TILE, D), lambda i, info: (i + start, 0))
    part = pl.BlockSpec((TILE, D), lambda i, info: (i, 0))
    row = pl.BlockSpec((1, D), lambda i, info: (0, 0))
    piece = pl.BlockSpec((2, TILE, HEAD_DIM), lambda i, info: (0, i + start, 0))
    single = pl.BlockSpec((1, TILE, HEAD_DIM), lambda i, info: (0, i + start, 0))
    return pl.pallas_call(
        residual_kernel,
        out_shape=(
            pltpu.HBM((rows, D), F32),
            jax.ShapeDtypeStruct((rows, D), BF),
            jax.ShapeDtypeStruct((2, rows, HEAD_DIM), BF),
            jax.ShapeDtypeStruct((1, rows, HEAD_DIM), BF),
            jax.ShapeDtypeStruct((1, rows, HEAD_DIM), BF),
        ),
        grid_spec=pltpu.PrefetchScalarGridSpec(
            num_scalar_prefetch=1,
            grid=(count // TILE,),
            in_specs=[
                pl.BlockSpec((TILE, D), lambda i, info: (i + first % PART // TILE, 0)),
                part,
                part,
                wide,
                row,
                columns(half, lambda i, info: (0, pl.multiple_of(OUT_AT + info[1] * half, HEAD_DIM))),
            ]
            + [pl.BlockSpec(memory_space=pl.ANY)] * len(earlier),
            out_specs=(wide, wide, piece, single, single),
        ),
        input_output_aliases={7 + index: index for index in range(len(earlier))},
        compiler_params=params(VMEM),
        cost_estimate=cost(3e11 if first + count == rows else 5e7, 0),
        name="residual",
    )(info, middle, back_own, back_other, in_hbm(upstream), gain, in_hbm(weights), *earlier)


def join(rank, pieces, joined):
    for head in range(2):
        own, other, other_v = pieces[head], pieces[2 + 2 * head], pieces[3 + 2 * head]
        for part in range(3):
            for value, pair in (
                (own[part, 0], rank),
                (other_v[0, 0] if part == 2 else other[part, 0], 1 - rank),
            ):
                column = pl.multiple_of((part * 4 + pair * 2 + head) * HEAD_DIM, HEAD_DIM)
                joined[:, pl.ds(column, HEAD_DIM)] = value


def back_kernel(info, *refs):
    pieces, (weight, out, joined) = refs[:6], refs[6:]
    join(info[0], pieces, joined)
    out[...] = dot_nt(joined[...], weight[...]).astype(BF)


def back_call(info, pieces, weights):
    rows = pieces[0].shape[2]
    width = 3 * 4 * HEAD_DIM
    piece = [
        pl.BlockSpec((parts, 1, TILE, HEAD_DIM), lambda i, info: (0, 0, i, 0))
        for parts in (3, 3, 2, 1, 2, 1)
    ]
    return pl.pallas_call(
        back_kernel,
        out_shape=jax.ShapeDtypeStruct((rows, D), BF),
        grid_spec=pltpu.PrefetchScalarGridSpec(
            num_scalar_prefetch=1,
            grid=(rows // TILE,),
            in_specs=piece + [pl.BlockSpec((D, width), lambda i, info: (0, 0))],
            out_specs=pl.BlockSpec((TILE, D), lambda i, info: (i, 0)),
            scratch_shapes=[pltpu.VMEM((TILE, width), BF)],
        ),
        compiler_params=params(VMEM),
        cost_estimate=cost(0, 0),
        name="back",
    )(info, *pieces, weights)


def attend_weight_kernel(info, normed, low, *refs):
    pieces, refs = refs[:6], refs[6:]
    attended, (keep, send, joined, out) = refs[:-4], refs[-4:]
    step = pl.program_id(0)

    @pl.when(step == 0)
    def _():
        join(info[0], pieces, joined)

    tile, width = normed.shape[1], joined.shape[1]
    left = normed[...].astype(F32).T.astype(BF)
    out[:, :width] = dot(left, joined[...]).astype(BF)
    left = low[...].astype(F32).T.astype(BF)
    out[:, width:] = dot(left, jnp.concatenate([part[...] for part in attended])).astype(BF)
    count, size = keep.shape[1], keep.shape[2]
    for line in range(tile // (4 * size)):
        slot = count - 1 - ((step * (tile // (4 * size)) + line) ^ info[4])
        for column in range(2):
            for target, core in ((keep, info[0]), (send, 1 - info[0])):
                side = info[3] if column == 0 else 1 - info[3]
                start = pl.multiple_of((line * 4 + side * 2 + core) * size, size)
                target[column, slot] = out[pl.ds(start, size), :]


def attend_weight_call(info, normed, low, attended, pieces, size):
    rows, half = normed.shape[0], attended[0].shape[1]
    width = 3 * half
    total = width + half
    left = pl.BlockSpec((rows, TILE), lambda i, info: (0, i))
    piece = [
        pl.BlockSpec((parts, 1, rows, HEAD_DIM), lambda i, info: (0, 0, 0, 0))
        for parts in (3, 3, 2, 1, 2, 1)
    ]
    count = D // (4 * size)
    return pl.pallas_call(
        attend_weight_kernel,
        out_shape=(jax.ShapeDtypeStruct((2, count, size, total), BF),) * 2,
        grid_spec=pltpu.PrefetchScalarGridSpec(
            num_scalar_prefetch=1,
            grid=(D // TILE,),
            in_specs=[left, left]
            + piece
            + [pl.BlockSpec((PART, half), lambda i, info: (0, 0))] * len(attended),
            out_specs=(pl.BlockSpec((2, count, size, total), lambda i, info: (0, 0, 0, 0)),) * 2,
            scratch_shapes=[pltpu.VMEM((rows, width), BF), pltpu.VMEM((TILE, total), BF)],
        ),
        compiler_params=params(VMEM),
        cost_estimate=cost(0, 0),
        name="attend_weights",
    )(info, normed, low, *pieces, *attended)


def input_kernel(grad, back_own, back_other, tokens, gain, out):
    value = tokens[...].astype(F32)
    back = back_own[...].astype(F32) + back_other[...].astype(F32)
    inverse = lax.rsqrt(jnp.mean(value * value, axis=1, keepdims=True) + EPS)
    scaled = gain[...] * back
    inner = jnp.mean(scaled * value, axis=1, keepdims=True)
    out[...] = (grad[...] + inverse * scaled - value * (inverse**3 * inner)).astype(BF)


def input_call(grad, back_own, back_other, tokens, gain):
    rows = tokens.shape[0]
    wide = pl.BlockSpec((TILE, D), lambda i: (i, 0))
    return pl.pallas_call(
        input_kernel,
        out_shape=jax.ShapeDtypeStruct((rows, D), BF),
        grid=(rows // TILE,),
        in_specs=[wide, wide, wide, wide, pl.BlockSpec((1, D), lambda i: (0, 0))],
        out_specs=wide,
        compiler_params=params(VMEM),
        cost_estimate=cost(12 * rows * D, 12 * MIB),
        name="input_grad",
    )(grad, back_own, back_other, tokens, gain)


def choose(line, options):
    value = options[0]
    for here in range(1, len(options)):
        if options[here] is not options[0]:
            value = jnp.where(line == here, options[here], value)
    return value


def pair_kernel(keep, core, *outs):
    half = keep.shape[1] // 2
    for part in range(2):
        slots = slice(part * half, (part + 1) * half)
        for column in range(2):
            outs[2 * part + column][...] = (
                keep[column, slots].astype(F32) + core[column, slots].astype(F32)
            ).astype(BF)


def pair_add(keep, core):
    count, size, width = keep.shape[1:]
    return pl.pallas_call(
        pair_kernel,
        out_shape=(jax.ShapeDtypeStruct((count // 2, size, width), BF),) * 4,
        compiler_params=pltpu.CompilerParams(vmem_limit_bytes=VMEM * MIB),
        cost_estimate=cost(0, 0),
        name="pair_add",
    )(keep, core)


def split_kernel(left, right, *outs):
    for index, out in enumerate(outs):
        out[...] = (left[index].astype(F32) + right[index].astype(F32)).astype(BF)


def split_add(left, right):
    count, size, width = left.shape
    return pl.pallas_call(
        split_kernel,
        out_shape=(jax.ShapeDtypeStruct((size, width), BF),) * count,
        compiler_params=pltpu.CompilerParams(vmem_limit_bytes=VMEM * MIB),
        cost_estimate=cost(0, 0),
        name="split_add",
    )(left, right)


def low_kernel(left, right, out):
    out[...] = (left[...].astype(F32) + right[...].astype(F32)).astype(out.dtype)


def low_add(left, right):
    return pl.pallas_call(
        low_kernel,
        out_shape=jax.ShapeDtypeStruct(left.shape, BF),
        compiler_params=pltpu.CompilerParams(vmem_limit_bytes=VMEM * MIB),
        cost_estimate=cost(0, 0),
        name="low_add",
    )(left, right)


def chosen_kernel(flags, first, second, up_in, down_in, up, down):
    one, two = first[...].astype(F32), second[...].astype(F32)
    up[...] = (jnp.where(flags[0] > 0, one, two) + up_in[...].astype(F32)).astype(BF)
    down[...] = (jnp.where(flags[1] > 0, one, two) + down_in[...].astype(F32)).astype(BF)


def chosen_add(flags, first, second, up_in, down_in):
    shape = jax.ShapeDtypeStruct(first.shape, BF)
    vmem = pl.BlockSpec(memory_space=pltpu.VMEM)
    return pl.pallas_call(
        chosen_kernel,
        out_shape=(shape, shape),
        in_specs=[pl.BlockSpec(memory_space=pltpu.SMEM)] + [vmem] * 4,
        out_specs=(vmem, vmem),
        compiler_params=pltpu.CompilerParams(vmem_limit_bytes=VMEM * MIB),
        cost_estimate=cost(0, 0),
        name="chosen_add",
    )(flags, first, second, up_in, down_in)


def reduce_rows(keep, send, count, first_wait, last_wait):
    length = count // 4
    line = lax.axis_index("dp") // 4
    core = lax.ppermute(send, "dp", [(i, i ^ 1) for i in range(count)])
    mine_one, theirs_one, mine_two, theirs_two = pair_add(keep, core)
    pairs = [(i, i ^ 2) for i in range(count)]
    other_one, first_wait = pin((lax.ppermute(theirs_one, "dp", pairs), first_wait))
    sums = list(split_add(mine_one, other_one))
    other = lax.ppermute(theirs_two, "dp", pairs)
    above = below = None
    for step in range(1, length):
        gap = length - step
        slots = lambda towards: [
            length - 1 - (here ^ (here + towards)) if 0 <= here + towards < length else None
            for here in range(length)
        ]
        ups, downs = slots(gap), slots(-gap)
        used = sorted({slot for slot in ups + downs if slot is not None})
        if len(used) == 1 and step == 1:
            up = down = sums[used[0]]
        elif len(used) == 1:
            up, down = low_add(sums[used[0]], below), low_add(sums[used[0]], above)
        elif len(used) == 2:
            flags = jnp.stack(
                [
                    choose(line, [jnp.int32(slot == used[0]) for slot in side])
                    for side in (ups, downs)
                ]
            )
            up, down = chosen_add(flags, sums[used[0]], sums[used[1]], below, above)
        else:
            fill = lambda side: [sums[used[0] if slot is None else slot] for slot in side]
            up, down = choose(line, fill(ups)), choose(line, fill(downs))
            up, down = low_add(up, below), low_add(down, above)
        if step == length - 1:
            up, down, last_wait = pin((up, down, last_wait))
        below = lax.ppermute(up, "dp", [(i, i + 4) for i in range(count - 4) if i // 4 + gap < length])
        above = lax.ppermute(down, "dp", [(i, i - 4) for i in range(4, count) if i // 4 >= gap])
        if step == length // 2 - 1:
            below, above, other = pin((below, above, other))
            sums += split_add(mine_two, other)
    return sums[-1], below, above, first_wait, last_wait


def interleave_kernel(info, *refs):
    pieces, out = refs[:4], refs[4]
    size = out.shape[0] // (4 * pieces[0].shape[0])
    length = pieces[0].shape[0]
    for index, piece in enumerate(pieces):
        side = info[3] if index % 2 == 0 else 1 - info[3]
        core = info[0] if index // 2 == 0 else 1 - info[0]
        for line in range(length):
            start = pl.multiple_of((line * 4 + side * 2 + core) * size, size)
            out[pl.ds(start, size), :] = piece[line]


def interleave(info, pieces, size):
    width = pieces[0].shape[1]
    pieces = [piece.reshape(-1, size, width) for piece in pieces]
    vmem = pl.BlockSpec(memory_space=pltpu.VMEM)
    return pl.pallas_call(
        interleave_kernel,
        out_shape=pltpu.VMEM((D, width), BF),
        in_specs=[pl.BlockSpec(memory_space=pltpu.SMEM)] + [vmem] * 4,
        out_specs=vmem,
        compiler_params=pltpu.CompilerParams(vmem_limit_bytes=VMEM * MIB),
        cost_estimate=cost(0, 0),
        name="interleave",
    )(info, *pieces)


def gain_kernel(own, other, gain, first, second, first_out, second_out, gain_out):
    low = gain[...].astype(BF).astype(F32)
    results = adamw(gain[...], (own[...] + other[...]) / low, first[...], second[...], 0.6)
    for out, result in zip((first_out, second_out, gain_out), results):
        out[...] = result


def gain_call(own, other, gain, first, second):
    shape = jax.ShapeDtypeStruct(gain.shape, F32)
    return pl.pallas_call(
        gain_kernel,
        out_shape=(shape, shape, shape),
        compiler_params=pltpu.CompilerParams(vmem_limit_bytes=VMEM * MIB),
        cost_estimate=cost(0, 0),
        name="gains",
    )(own, other, gain, first, second)


def shard_kernel(qkv, gains, out):
    width = qkv.shape[2]
    for part in range(3):
        out[:, part * width : (part + 1) * width] = qkv[part].astype(BF)
    rows = jnp.concatenate([gains[...], jnp.zeros((HEAD_DIM - 2, gains.shape[1]), F32)])
    out[:, 3 * width :] = rows.T.astype(BF)


def shard_call(qkv, gains):
    total = 3 * qkv.shape[2] + HEAD_DIM
    return pl.pallas_call(
        shard_kernel,
        out_shape=jax.ShapeDtypeStruct((qkv.shape[1], total), BF),
        compiler_params=pltpu.CompilerParams(vmem_limit_bytes=VMEM * MIB),
        cost_estimate=cost(0, 0),
        name="shard",
    )(qkv, gains)


def pin(values):
    return lax.optimization_barrier(values)


def body(
    tokens,
    cotangent,
    proj_qkv,
    proj_out,
    proj_gate_up,
    proj_down,
    norm_gains,
    first_qkv,
    first_out,
    first_gate_up,
    first_down,
    first_gains,
    second_qkv,
    second_out,
    second_gate_up,
    second_down,
    second_gains,
    cache,
    doc_segments,
    padding,
    retrieval,
):
    rows = tokens.shape[0]
    count = lax.axis_size("dp")
    device = lax.axis_index("dp")
    group = lax.axis_index("mp")
    rank = device % 2
    segment = device // 2
    shard = proj_qkv.shape[1]
    local = proj_qkv.shape[2]
    hidden_here = proj_gate_up.shape[2]
    core_pairs = [(i, i ^ 1) for i in range(count)]

    def across(value):
        return lax.ppermute(value, "mp", [(0, 1), (1, 0)])

    def beside(value):
        return lax.ppermute(value, "dp", core_pairs)

    shard_one = shard_call(proj_qkv, norm_gains)
    out_own = proj_out.astype(BF).T
    out_other = across(out_own)
    shard_two = jnp.concatenate(
        [
            proj_gate_up[0].astype(BF),
            proj_gate_up[1].astype(BF),
            proj_down.astype(BF).T,
            jnp.where(group == 0, out_own, out_other),
            jnp.where(group == 0, out_other, out_own),
        ],
        axis=1,
    )
    length = count // 4
    lines = [[i for i in range(count) if i % 4 == lane] for lane in range(4)]
    own_column = lax.all_gather(shard_one, "dp", axis=0, tiled=True, axis_index_groups=lines)
    next_column = lax.ppermute(own_column, "dp", [(i, i ^ 2) for i in range(count)])
    pieces = (own_column, next_column, beside(own_column), beside(next_column))
    weights_two = lax.all_gather(shard_two, "dp", axis=0, tiled=True)

    places = jnp.arange(SEG, dtype=jnp.int32)
    starts = jnp.cumsum(doc_segments) - doc_segments
    memory_on = jnp.logical_not(jnp.any(starts == segment))
    side = (device // 2) % 2
    info = jnp.stack([rank, group, memory_on.astype(jnp.int32), side, device // 4]).astype(jnp.int32)
    cosines, sines = rope_tables(places)
    valid = lax.dynamic_slice_in_dim(padding, segment * SEG, SEG)
    lane = jnp.arange(HEAD_DIM, dtype=jnp.int32)[None, :]
    bias = jnp.where((valid[:, None] == 0) & (lane == 0), NEGATIVE, 0.0).astype(BF)
    fetched = cache[retrieval[0]].reshape(RETR, 2, 2, 2, HEAD_DIM).transpose(2, 1, 3, 0, 4)
    mem_own = lax.dynamic_index_in_dim(fetched, rank, keepdims=False)
    mem_other = beside(lax.dynamic_index_in_dim(fetched, 1 - rank, keepdims=False))
    pieces, mem_own, mem_other, bias, cosines, sines, info = pin(
        (pieces, mem_own, mem_other, bias, cosines, sines, info)
    )
    weights_one = interleave(info, pieces, shard)

    send, normed_one, gains = project_first(info, tokens, weights_one, cosines, sines)
    gain_one, gain_two = gains[0:1], gains[1:2]
    other = beside(send)
    own = project_second(info, normed_one, weights_one, cosines, sines)
    out_keep, out_send, turned, logs = attend_forward(info, own, other, mem_own, mem_other, bias)
    out_recv = beside(out_send)
    pieces = (out_keep, out_recv, across(out_keep), across(out_recv))
    middles, normed_two, attended = [], [], []
    for chunk in range(rows // PART):
        middle, normed, own_out = middle_call(info, pieces, tokens, weights_two, gain_two, chunk)
        middles.append(middle)
        normed_two.append(normed)
        attended.append(own_out)

    earlier, backs, backs_other = (), [], []
    for chunk, first in enumerate(range(0, rows, TILE)):
        *earlier, back = feed_call(normed_two[first // PART], cotangent, weights_two, first, TILE, earlier)
        backs.append(back)
        backs_other.append(across(back))
    hidden, grad_gate, grad_up, feed_part = earlier
    hidden, backs_other[:2] = pin((hidden, backs_other[:2]))
    feed_grads = feed_weight_call(normed_two, cotangent, hidden, grad_gate, grad_up)
    feed_other = across(feed_part)
    backs[2], _ = pin((backs[2], feed_grads))
    earlier = ()
    for index in (2, 3, 0, 1):
        first = index * TILE
        earlier = residual_call(
            info, middles[first // PART], backs[index], backs_other[index], cotangent, gain_two, weights_two,
            first, earlier,
        )
    grad_middle, grad_low, grad_keep, *grad_sends = earlier
    grad_others = [beside(value) for value in grad_sends]

    d_keeps, d_others = [], []
    for head in range(2):
        d_keep, d_send, d_send_v = attend_backward(
            info, own, other, mem_own, mem_other, bias, grad_keep, grad_others[head], turned, logs,
            cosines, sines, head,
        )
        d_keeps.append(d_keep)
        d_others += [beside(d_send), beside(d_send_v)]
    moved = d_keeps + d_others
    back_one = back_call(info, moved, weights_one)
    moved[0], _ = pin((moved[0], back_one))
    attend_keep, attend_send = attend_weight_call(info, normed_one, grad_low, attended, moved, shard)
    back_one, feed_other = pin((back_one, feed_other))
    back_one_other = across(back_one)
    input_grad = input_call(grad_middle, back_one, back_one_other, tokens, gain_one)
    block_out = (
        jnp.concatenate(middles) + (feed_part.astype(F32) + feed_other.astype(F32))
    ).astype(BF)
    total, below, above, block_out, input_grad = reduce_rows(
        attend_keep, attend_send, count, block_out, input_grad
    )
    feed_sum = lax.psum_scatter(feed_grads, "dp", scatter_dimension=0, tiled=True).astype(F32)
    gate_up_sum = jnp.stack([feed_sum[:, :hidden_here], feed_sum[:, hidden_here : 2 * hidden_here]])
    down_sum = feed_sum[:, 2 * hidden_here :].T
    gate_up_first, gate_up_second, gate_up_new = adamw(
        proj_gate_up, gate_up_sum, first_gate_up, second_gate_up, 0.5 / math.sqrt(D)
    )
    down_first, down_second, down_new = adamw(
        proj_down, down_sum, first_down, second_down, 0.5 / math.sqrt(FF)
    )
    gate_up_new, down_new, total, below, above = pin((gate_up_new, down_new, total, below, above))
    attend_sum = total.astype(F32) + (below.astype(F32) + above.astype(F32))
    qkv_sum = jnp.stack([attend_sum[:, part * local : (part + 1) * local] for part in range(3)])
    out_sum = attend_sum[:, 3 * local : 4 * local].T
    low_qkv, low_gate_up = proj_qkv.astype(BF).astype(F32), proj_gate_up.astype(BF).astype(F32)
    gains_sum = jnp.stack(
        [jnp.sum(low_qkv * qkv_sum, axis=(0, 2)), jnp.sum(low_gate_up * gate_up_sum, axis=(0, 2))]
    )
    gains_first, gains_second, gains_new = gain_call(
        gains_sum, across(gains_sum), norm_gains, first_gains, second_gains
    )

    qkv_first, qkv_second, qkv_new = adamw(
        proj_qkv, qkv_sum, first_qkv, second_qkv, 0.5 / math.sqrt(D)
    )
    out_first, out_second, out_new = adamw(
        proj_out, out_sum, first_out, second_out, 0.5 / math.sqrt(max(1, 4 * D // SEG))
    )
    return (
        block_out,
        input_grad,
        qkv_first,
        qkv_second,
        qkv_new,
        out_first,
        out_second,
        out_new,
        gate_up_first,
        gate_up_second,
        gate_up_new,
        down_first,
        down_second,
        down_new,
        gains_first,
        gains_second,
        gains_new,
    )


def solution(mesh):
    return jax.shard_map(
        body,
        mesh=mesh,
        in_specs=(
            P("dp", None),
            P("dp", None),
            P(None, "dp", "mp"),
            P("mp", "dp"),
            P(None, "dp", "mp"),
            P("mp", "dp"),
            P(None, "dp"),
            P(None, "dp", "mp"),
            P("mp", "dp"),
            P(None, "dp", "mp"),
            P("mp", "dp"),
            P(None, "dp"),
            P(None, "dp", "mp"),
            P("mp", "dp"),
            P(None, "dp", "mp"),
            P("mp", "dp"),
            P(None, "dp"),
            P("dp", None, "mp"),
            P(),
            P(),
            P("dp", None),
        ),
        out_specs=(
            P("dp", None),
            P("dp", None),
            P(None, "dp", "mp"),
            P(None, "dp", "mp"),
            P(None, "dp", "mp"),
            P("mp", "dp"),
            P("mp", "dp"),
            P("mp", "dp"),
            P(None, "dp", "mp"),
            P(None, "dp", "mp"),
            P(None, "dp", "mp"),
            P("mp", "dp"),
            P("mp", "dp"),
            P("mp", "dp"),
            P(None, "dp"),
            P(None, "dp"),
            P(None, "dp"),
        ),
        check_vma=False,
    )
```

```python
import functools
import math

import jax
import jax.numpy as jnp
from jax import lax
from jax.experimental import pallas as pl
from jax.experimental.pallas import tpu as pltpu
from jax.sharding import PartitionSpec as P

D = 1024
HEAD_DIM = 128
FF = 2816
SEG = 2048
RETR = 128
STEP = 10

EPS = 1e-05
BETA_ONE = 0.9
BETA_TWO = 0.95
ADAM_EPS = 1e-08
DECAY = 0.1
NEGATIVE = -1e30
SCALE = HEAD_DIM**-0.5
SCALE_TWO = SCALE * math.log2(math.e)

BF = jnp.bfloat16
F32 = jnp.float32
MIB = 1024 * 1024
TILE = 256
VMEM = 26
WEIGH = 1.0


def dot(left, right):
    return jnp.dot(left, right, preferred_element_type=F32)


def dot_nt(left, right):
    return lax.dot_general(left, right, (((1,), (1,)), ((), ())), preferred_element_type=F32)


def dot_tn(left, right):
    return lax.dot_general(left, right, (((0,), (0,)), ((), ())), preferred_element_type=F32)


def params(mib, axes=1):
    return pltpu.CompilerParams(
        dimension_semantics=("arbitrary",) * axes, vmem_limit_bytes=mib * MIB
    )


def cost(flops, moved, trans=0):
    return pl.CostEstimate(flops=int(flops * WEIGH), bytes_accessed=int(moved * WEIGH), transcendentals=int(trans))


def rope_tables(places):
    half_dim = HEAD_DIM // 2
    freqs = 10000.0 ** (-(jnp.arange(half_dim, dtype=F32) / half_dim))
    phase = places.astype(F32)[:, None] * freqs[None, :]
    cosines, sines = jnp.cos(phase), jnp.sin(phase)
    return jnp.concatenate([cosines, cosines], 1), jnp.concatenate([-sines, sines], 1)


def turn(value, cosines, sines):
    return value * cosines + pltpu.roll(value, HEAD_DIM // 2, 1) * sines


def adamw(weight, grad, first, second, rate):
    first_new = BETA_ONE * first + (1.0 - BETA_ONE) * grad
    second_new = BETA_TWO * second + (1.0 - BETA_TWO) * grad * grad
    first_hat = first_new / (1.0 - BETA_ONE**STEP)
    second_hat = second_new / (1.0 - BETA_TWO**STEP)
    updated = weight - rate * (first_hat / (jnp.sqrt(second_hat) + ADAM_EPS) + DECAY * weight)
    return (first_new, second_new, updated)


def rotate_out(result, part, cosines, sines, out):
    for head in range(2):
        value = result[:, head * HEAD_DIM : (head + 1) * HEAD_DIM]

        @pl.when(part < 2)
        def _():
            out[0, head] = turn(value, cosines[...], sines[...]).astype(BF)

        @pl.when(part == 2)
        def _():
            out[0, head] = value.astype(BF)


def first_kernel(info, tokens, gain_columns, weight, cosines, sines, out, normed, gains):
    part = pl.program_id(0)

    @pl.when(part == 0)
    def _():
        rows = gain_columns[...].astype(F32).T[:8, :]
        gains[...] = rows
        value = tokens[...].astype(F32)
        inverse = lax.rsqrt(jnp.mean(value * value, axis=1, keepdims=True) + EPS)
        normed[...] = (value * inverse * rows[0:1, :]).astype(BF)

    rotate_out(dot(normed[...], weight[...]), part, cosines, sines, out)


def second_kernel(info, normed, weight, cosines, sines, out):
    rotate_out(dot(normed[...], weight[...]), pl.program_id(0), cosines, sines, out)


def project_first(info, tokens, weights, cosines, sines):
    rows = tokens.shape[0]
    return pl.pallas_call(
        first_kernel,
        out_shape=(
            jax.ShapeDtypeStruct((3, 2, rows, HEAD_DIM), BF),
            jax.ShapeDtypeStruct((rows, D), BF),
            jax.ShapeDtypeStruct((8, D), F32),
        ),
        grid_spec=pltpu.PrefetchScalarGridSpec(
            num_scalar_prefetch=1,
            grid=(3,),
            in_specs=[
                pl.BlockSpec((rows, D), lambda j, info: (0, 0)),
                pl.BlockSpec((D, HEAD_DIM), lambda j, info: (0, 12)),
                pl.BlockSpec((D, 256), lambda j, info: (0, 2 * j + 1 - info[0])),
                pl.BlockSpec((rows, HEAD_DIM), lambda j, info: (info[0], 0)),
                pl.BlockSpec((rows, HEAD_DIM), lambda j, info: (info[0], 0)),
            ],
            out_specs=(
                pl.BlockSpec((1, 2, rows, HEAD_DIM), lambda j, info: (j, 0, 0, 0)),
                pl.BlockSpec((rows, D), lambda j, info: (0, 0)),
                pl.BlockSpec((8, D), lambda j, info: (0, 0)),
            ),
        ),
        compiler_params=params(VMEM),
        cost_estimate=cost(0, 0),
        name="project_first",
    )(info, in_hbm(tokens), weights, weights, in_hbm(cosines), in_hbm(sines))


def project_second(info, normed, weights, cosines, sines):
    rows = normed.shape[0]
    return pl.pallas_call(
        second_kernel,
        out_shape=jax.ShapeDtypeStruct((3, 2, rows, HEAD_DIM), BF),
        grid_spec=pltpu.PrefetchScalarGridSpec(
            num_scalar_prefetch=1,
            grid=(3,),
            in_specs=[
                pl.BlockSpec((rows, D), lambda j, info: (0, 0)),
                pl.BlockSpec((D, 256), lambda j, info: (0, 2 * j + info[0])),
                pl.BlockSpec((rows, HEAD_DIM), lambda j, info: (info[0], 0)),
                pl.BlockSpec((rows, HEAD_DIM), lambda j, info: (info[0], 0)),
            ],
            out_specs=pl.BlockSpec((1, 2, rows, HEAD_DIM), lambda j, info: (j, 0, 0, 0)),
        ),
        compiler_params=params(VMEM),
        cost_estimate=cost(0, 0),
        name="project_second",
    )(info, normed, weights, cosines, sines)


def place(scratch, own, other, rank, rows):
    scratch[pl.ds(pl.multiple_of(rank * rows, rows), rows), :] = own
    scratch[pl.ds(pl.multiple_of((1 - rank) * rows, rows), rows), :] = other


def chunks_of(tile, step):
    end = tile * TILE
    spans = [(start, min(step, end - start)) for start in range(0, end, step)]
    return spans + [(end, TILE)]


def causal(scores):
    rows = lax.broadcasted_iota(jnp.int32, scores.shape, 0)
    columns = lax.broadcasted_iota(jnp.int32, scores.shape, 1)
    return jnp.where(rows <= columns, scores, NEGATIVE)


def forward_kernel(
    info, own, other, mem_own, mem_other, bias, keep, send, turned, logs,
    q_s, k_s, v_s, vt_s, mem_s, s_s, out_s,
):
    rank = info[0]
    rows = own.shape[2]
    mem_bias = jnp.where(info[2] > 0, 0.0, NEGATIVE).astype(F32)
    place(q_s, own[0, 0], other[0, 0], rank, rows)
    place(k_s, own[1, 0], other[1, 0], rank, rows)
    place(v_s, own[2, 0], other[2, 0], rank, rows)
    mem_s[rank] = mem_own[:, 0]
    mem_s[1 - rank] = mem_other[:, 0]
    vt_s[...] = v_s[...].astype(F32).T.astype(BF)
    ones = (lax.broadcasted_iota(jnp.int32, (TILE, HEAD_DIM), 1) == 0).astype(BF)
    for tile in range(SEG // TILE):
        here = slice(tile * TILE, (tile + 1) * TILE)
        block = tile * TILE // rows
        query = q_s[here, :]
        wide = jnp.concatenate([query, ones], axis=1)
        spans = chunks_of(tile, 512)
        scores = dot_nt(mem_s[block, 0], query) + mem_bias
        s_s[SEG : SEG + RETR, :] = scores
        top = jnp.max(scores, axis=0, keepdims=True)
        for start, size in spans:
            span = slice(start, start + size)
            if start + size > SEG // 2:
                scores = dot_nt(jnp.concatenate([k_s[span, :], bias[span, :]], axis=1), wide)
            else:
                scores = dot_nt(k_s[span, :], query)
            if start == tile * TILE:
                scores = causal(scores)
            s_s[span, :] = scores
            top = jnp.maximum(top, jnp.max(scores, axis=0, keepdims=True))
        shift = top * SCALE_TWO
        exponent = jnp.exp2(s_s[SEG : SEG + RETR, :] * SCALE_TWO - shift)
        total = jnp.sum(exponent, axis=0, keepdims=True)
        result = dot(mem_s[block, 1].astype(F32).T.astype(BF), exponent.astype(BF))
        for start, size in spans:
            span = slice(start, start + size)
            exponent = jnp.exp2(s_s[span, :] * SCALE_TWO - shift)
            total = total + jnp.sum(exponent, axis=0, keepdims=True)
            result = result + dot(vt_s[:, span], exponent.astype(BF))
        result = result * (1.0 / total)
        turned[0, :, here] = result
        logs[0, :, here] = shift + jnp.log2(total)
        out_s[here, :] = result.T.astype(BF)
    keep[0] = out_s[pl.ds(pl.multiple_of(rank * rows, rows), rows), :]
    send[0] = out_s[pl.ds(pl.multiple_of((1 - rank) * rows, rows), rows), :]


def attend_forward(info, own, other, mem_own, mem_other, bias):
    rows = own.shape[2]
    part = pl.BlockSpec((3, 1, rows, HEAD_DIM), lambda h, info: (0, h, 0, 0))
    mem = pl.BlockSpec((2, 1, RETR, HEAD_DIM), lambda h, info: (0, h, 0, 0))
    half = pl.BlockSpec((1, rows, HEAD_DIM), lambda h, info: (h, 0, 0))
    return pl.pallas_call(
        forward_kernel,
        out_shape=(
            jax.ShapeDtypeStruct((2, rows, HEAD_DIM), BF),
            jax.ShapeDtypeStruct((2, rows, HEAD_DIM), BF),
            pltpu.HBM((2, HEAD_DIM, SEG), F32),
            jax.ShapeDtypeStruct((2, 1, SEG), F32),
        ),
        grid_spec=pltpu.PrefetchScalarGridSpec(
            num_scalar_prefetch=1,
            grid=(2,),
            in_specs=[
                part,
                part,
                mem,
                mem,
                pl.BlockSpec((SEG, HEAD_DIM), lambda h, info: (0, 0)),
            ],
            out_specs=(
                half,
                half,
                pl.BlockSpec((1, HEAD_DIM, SEG), lambda h, info: (h, 0, 0)),
                pl.BlockSpec((1, 1, SEG), lambda h, info: (h, 0, 0)),
            ),
            scratch_shapes=[
                pltpu.VMEM((SEG, HEAD_DIM), BF),
                pltpu.VMEM((SEG, HEAD_DIM), BF),
                pltpu.VMEM((SEG, HEAD_DIM), BF),
                pltpu.VMEM((HEAD_DIM, SEG), BF),
                pltpu.VMEM((2, 2, RETR, HEAD_DIM), BF),
                pltpu.VMEM((SEG + RETR, TILE), F32),
                pltpu.VMEM((SEG, HEAD_DIM), BF),
            ],
        ),
        compiler_params=params(VMEM),
        cost_estimate=cost(0, 0),
        name="attend_forward",
    )(info, own, other, mem_own, mem_other, bias)


def backward_kernel(
    info, own, other, mem_own, mem_other, bias, grad_own, grad_other, turned, logs, cosines, sines,
    keep, send, send_v,
    q_s, k_s, v_s, g_s, kt_s, mem_s, dots_s, dq_s, dk_s, dv_s,
):
    rank = info[0]
    rows = own.shape[2]
    mem_bias = jnp.where(info[2] > 0, 0.0, NEGATIVE).astype(F32)
    place(q_s, own[0, 0], other[0, 0], rank, rows)
    place(k_s, own[1, 0], other[1, 0], rank, rows)
    place(v_s, own[2, 0], other[2, 0], rank, rows)
    place(g_s, grad_own[0], grad_other[0], rank, rows)
    mem_s[rank] = mem_own[:, 0]
    mem_s[1 - rank] = mem_other[:, 0]
    kt_s[...] = k_s[...].astype(F32).T.astype(BF)
    dots_s[...] = jnp.sum(g_s[...].astype(F32).T * turned[0], axis=0, keepdims=True)
    dk_s[...] = jnp.zeros_like(dk_s)
    dv_s[...] = jnp.zeros_like(dv_s)
    ones = (lax.broadcasted_iota(jnp.int32, (TILE, HEAD_DIM), 1) == 0).astype(BF)
    for tile in range(SEG // TILE):
        here = slice(tile * TILE, (tile + 1) * TILE)
        block = tile * TILE // rows
        query = q_s[here, :]
        wide = jnp.concatenate([query, ones], axis=1)
        grad = g_s[here, :]
        log = logs[0, :, here]
        dots = dots_s[:, here]
        scores = dot_nt(mem_s[block, 0], query) + mem_bias
        probs = jnp.exp2(scores * SCALE_TWO - log)
        change = (probs * (dot_nt(mem_s[block, 1], grad) - dots)).astype(BF)
        result = dot(mem_s[block, 0].astype(F32).T.astype(BF), change)
        for start, size in chunks_of(tile, 512):
            span = slice(start, start + size)
            keys = k_s[span, :]
            if start + size > SEG // 2:
                scores = dot_nt(jnp.concatenate([keys, bias[span, :]], axis=1), wide)
            else:
                scores = dot_nt(keys, query)
            if start == tile * TILE:
                scores = causal(scores)
            probs = jnp.exp2(scores * SCALE_TWO - log)
            change = (probs * (dot_nt(v_s[span, :], grad) - dots)).astype(BF)
            dv_s[span, :] += dot(probs.astype(BF), grad)
            dk_s[span, :] += dot(change, query)
            result = result + dot(kt_s[:, span], change)
        dq_s[here, :] = turn(result.T * SCALE, cosines[here, :], -sines[here, :]).astype(BF)
    for outs, place_ in (((keep.at[0], keep.at[1], keep.at[2]), rank), ((send.at[0], send.at[1], send_v.at[0]), 1 - rank)):
        held = pl.ds(pl.multiple_of(place_ * rows, rows), rows)
        outs[0][0] = dq_s[held, :]
        outs[1][0] = turn(dk_s[held, :] * SCALE, cosines[held, :], -sines[held, :]).astype(BF)
        outs[2][0] = dv_s[held, :].astype(BF)


def attend_backward(
    info, own, other, mem_own, mem_other, bias, grad_own, grad_other, turned, logs, cosines, sines, head
):
    rows = own.shape[2]
    part = pl.BlockSpec((3, 1, rows, HEAD_DIM), lambda h, info: (0, head, 0, 0))
    mem = pl.BlockSpec((2, 1, RETR, HEAD_DIM), lambda h, info: (0, head, 0, 0))
    half = pl.BlockSpec((1, rows, HEAD_DIM), lambda h, info: (head, 0, 0))
    table = pl.BlockSpec((SEG, HEAD_DIM), lambda h, info: (0, 0))
    return pl.pallas_call(
        backward_kernel,
        out_shape=tuple(jax.ShapeDtypeStruct((parts, 1, rows, HEAD_DIM), BF) for parts in (3, 2, 1)),
        grid_spec=pltpu.PrefetchScalarGridSpec(
            num_scalar_prefetch=1,
            grid=(1,),
            in_specs=[
                part,
                part,
                mem,
                mem,
                table,
                half,
                pl.BlockSpec((1, rows, HEAD_DIM), lambda h, info: (0, 0, 0)),
                pl.BlockSpec((1, HEAD_DIM, SEG), lambda h, info: (head, 0, 0)),
                pl.BlockSpec((1, 1, SEG), lambda h, info: (head, 0, 0)),
                table,
                table,
            ],
            out_specs=tuple(
                pl.BlockSpec((parts, 1, rows, HEAD_DIM), lambda h, info: (0, 0, 0, 0)) for parts in (3, 2, 1)
            ),
            scratch_shapes=[pltpu.VMEM((SEG, HEAD_DIM), BF)] * 4
            + [
                pltpu.VMEM((HEAD_DIM, SEG), BF),
                pltpu.VMEM((2, 2, RETR, HEAD_DIM), BF),
                pltpu.VMEM((1, SEG), F32),
                pltpu.VMEM((SEG, HEAD_DIM), BF),
                pltpu.VMEM((SEG, HEAD_DIM), F32),
                pltpu.VMEM((SEG, HEAD_DIM), F32),
            ],
        ),
        compiler_params=params(VMEM),
        cost_estimate=cost(0, 0),
        name="attend_backward",
    )(
        info, own, other, mem_own, mem_other, bias, grad_own, grad_other, turned, logs, cosines, sines
    )


OUT_AT = 3 * FF // 2


def in_hbm(value):
    return pltpu.with_memory_space_constraint(value, pltpu.HBM)


def columns(width, start):
    return pl.BlockSpec(
        (pl.Element(D), pl.Element(width)), start, pipeline_mode=pl.Buffered(1)
    )


def middle_kernel(info, *refs):
    pieces, (tokens, weight, gain, middle, normed, attended, joined) = refs[:4], refs[4:]
    rank, group = info[0], info[1]
    for index, piece in enumerate(pieces):
        side = (group, 1 - group)[index // 2]
        pair = (rank, 1 - rank)[index % 2]
        for head in range(2):
            column = pl.multiple_of((side * 4 + pair * 2 + head) * HEAD_DIM, HEAD_DIM)
            joined[:, pl.ds(column, HEAD_DIM)] = piece[head]
    half = attended.shape[1]
    attended[...] = joined[:, pl.ds(pl.multiple_of(group * half, half), half)]
    value = tokens[...].astype(F32) + dot_nt(joined[...], weight[...])
    middle[...] = value
    inverse = lax.rsqrt(jnp.mean(value * value, axis=1, keepdims=True) + EPS)
    normed[...] = (value * inverse * gain[...]).astype(BF)


def middle_call(info, pieces, tokens, weights, gain):
    rows, half = tokens.shape[0], 4 * HEAD_DIM
    piece = pl.BlockSpec((2, TILE, HEAD_DIM), lambda i, info: (0, i, 0))
    wide = pl.BlockSpec((TILE, D), lambda i, info: (i, 0))
    return pl.pallas_call(
        middle_kernel,
        out_shape=(
            pltpu.HBM((rows, D), F32),
            jax.ShapeDtypeStruct((rows, D), BF),
            jax.ShapeDtypeStruct((rows, half), BF),
        ),
        grid_spec=pltpu.PrefetchScalarGridSpec(
            num_scalar_prefetch=1,
            grid=(rows // TILE,),
            in_specs=[piece] * 4
            + [
                wide,
                columns(D, lambda i, info: (0, OUT_AT)),
                pl.BlockSpec((1, D), lambda i, info: (0, 0)),
            ],
            out_specs=(wide, wide, pl.BlockSpec((TILE, half), lambda i, info: (i, 0))),
            scratch_shapes=[pltpu.VMEM((TILE, D), BF)],
        ),
        compiler_params=params(VMEM),
        cost_estimate=cost(0, 0),
        name="middle",
    )(info, *[in_hbm(piece) for piece in pieces], in_hbm(tokens), in_hbm(weights), gain)


def feed_kernel(normed, upstream, gate_w, up_w, down_w, *refs):
    hidden, gate_grad, up_grad, feed, back = refs[-5:]
    gate = dot(normed[...], gate_w[...])
    up_part = dot(normed[...], up_w[...])
    sigma = jax.nn.sigmoid(gate)
    silu = gate * sigma
    low = (silu * up_part).astype(BF)
    hidden[...] = low
    feed[...] = dot_nt(low, down_w[...]).astype(BF)
    grad = dot(upstream[...], down_w[...])
    grad_gate = (grad * up_part * sigma * (1.0 + gate * (1.0 - sigma))).astype(BF)
    grad_up = (grad * silu).astype(BF)
    gate_grad[...] = grad_gate
    up_grad[...] = grad_up
    back[...] = (dot_nt(grad_gate, gate_w[...]) + dot_nt(grad_up, up_w[...])).astype(BF)


def feed_call(normed, upstream, weights, first, count, earlier):
    rows = upstream.shape[0]
    width = FF // 2
    whole = lambda index: pl.BlockSpec((D, width), lambda i: (0, index), pipeline_mode=pl.Buffered(1))
    source = pl.BlockSpec((TILE, D), lambda i: (i + first // TILE, 0))
    narrow = pl.BlockSpec((TILE, width), lambda i: (i + first // TILE, 0))
    return pl.pallas_call(
        feed_kernel,
        out_shape=(pltpu.VMEM((rows, width), BF),) * 3
        + (jax.ShapeDtypeStruct((rows, D), BF), jax.ShapeDtypeStruct((count, D), BF)),
        grid=(count // TILE,),
        in_specs=[source, source, whole(0), whole(1), whole(2)]
        + [pl.BlockSpec(memory_space=pl.ANY)] * len(earlier),
        out_specs=(narrow, narrow, narrow, source, pl.BlockSpec((TILE, D), lambda i: (i, 0))),
        input_output_aliases={5 + index: index for index in range(len(earlier))},
        compiler_params=params(VMEM),
        cost_estimate=cost(5e7, 0),
        name="feed",
    )(normed, upstream, weights, weights, weights, *earlier)


def feed_weight_kernel(normed, upstream, hidden, gate_grad, up_grad, out):
    width = hidden.shape[1]
    left = normed[...].astype(F32).T.astype(BF)
    out[:, :width] = dot(left, gate_grad[...]).astype(BF)
    out[:, width : 2 * width] = dot(left, up_grad[...]).astype(BF)
    left = upstream[...].astype(F32).T.astype(BF)
    out[:, 2 * width :] = dot(left, hidden[...]).astype(BF)


def feed_weight_call(normed, upstream, hidden, gate_grad, up_grad):
    rows, width = hidden.shape
    left = pl.BlockSpec((rows, TILE), lambda i: (0, i))
    whole = pl.BlockSpec((rows, width), lambda i: (0, 0), pipeline_mode=pl.Buffered(1))
    return pl.pallas_call(
        feed_weight_kernel,
        out_shape=pltpu.HBM((D, 3 * width), BF),
        grid=(D // TILE,),
        in_specs=[left, left, whole, whole, whole],
        out_specs=pl.BlockSpec((TILE, 3 * width), lambda i: (i, 0)),
        compiler_params=params(VMEM),
        cost_estimate=cost(5e7, 0),
        name="feed_weights",
    )(normed, in_hbm(upstream), hidden, gate_grad, up_grad)


def residual_kernel(info, middle, back_own, back_other, upstream, gain, weight, *refs):
    grad, low, keep, send_one, send_two = refs[-5:]
    rank = info[0]
    value = middle[...]
    back = back_own[...].astype(F32) + back_other[...].astype(F32)
    inverse = lax.rsqrt(jnp.mean(value * value, axis=1, keepdims=True) + EPS)
    scaled = gain[...] * back
    inner = jnp.mean(scaled * value, axis=1, keepdims=True)
    total = upstream[...].astype(F32) + inverse * scaled - value * (inverse**3 * inner)
    grad[...] = total
    branch = total.astype(BF)
    low[...] = branch

    for outs, pair in (((keep.at[0], keep.at[1]), rank), ((send_one.at[0], send_two.at[0]), 1 - rank)):
        column = pl.multiple_of(pair * 2 * HEAD_DIM, 2 * HEAD_DIM)
        result = dot(branch, weight[:, pl.ds(column, 2 * HEAD_DIM)]).astype(BF)
        for head in range(2):
            outs[head][...] = result[:, head * HEAD_DIM : (head + 1) * HEAD_DIM]


def residual_call(info, middle, back_own, back_other, upstream, gain, weights, first, earlier):
    rows, count = upstream.shape[0], back_own.shape[0]
    start, half = first // TILE, 4 * HEAD_DIM
    wide = pl.BlockSpec((TILE, D), lambda i, info: (i + start, 0))
    part = pl.BlockSpec((TILE, D), lambda i, info: (i, 0))
    row = pl.BlockSpec((1, D), lambda i, info: (0, 0))
    piece = pl.BlockSpec((2, TILE, HEAD_DIM), lambda i, info: (0, i + start, 0))
    single = pl.BlockSpec((1, TILE, HEAD_DIM), lambda i, info: (0, i + start, 0))
    return pl.pallas_call(
        residual_kernel,
        out_shape=(
            pltpu.HBM((rows, D), F32),
            jax.ShapeDtypeStruct((rows, D), BF),
            jax.ShapeDtypeStruct((2, rows, HEAD_DIM), BF),
            jax.ShapeDtypeStruct((1, rows, HEAD_DIM), BF),
            jax.ShapeDtypeStruct((1, rows, HEAD_DIM), BF),
        ),
        grid_spec=pltpu.PrefetchScalarGridSpec(
            num_scalar_prefetch=1,
            grid=(count // TILE,),
            in_specs=[
                wide,
                part,
                part,
                wide,
                row,
                columns(half, lambda i, info: (0, pl.multiple_of(OUT_AT + info[1] * half, HEAD_DIM))),
            ]
            + [pl.BlockSpec(memory_space=pl.ANY)] * len(earlier),
            out_specs=(wide, wide, piece, single, single),
        ),
        input_output_aliases={7 + index: index for index in range(len(earlier))},
        compiler_params=params(VMEM),
        cost_estimate=cost(3e11 if first + count == rows else 5e7, 0),
        name="residual",
    )(info, middle, back_own, back_other, in_hbm(upstream), gain, in_hbm(weights), *earlier)


def join(rank, pieces, joined):
    for head in range(2):
        own, other, other_v = pieces[head], pieces[2 + 2 * head], pieces[3 + 2 * head]
        for part in range(3):
            for value, pair in (
                (own[part, 0], rank),
                (other_v[0, 0] if part == 2 else other[part, 0], 1 - rank),
            ):
                column = pl.multiple_of((part * 4 + pair * 2 + head) * HEAD_DIM, HEAD_DIM)
                joined[:, pl.ds(column, HEAD_DIM)] = value


def back_kernel(info, *refs):
    pieces, (weight, out, joined) = refs[:6], refs[6:]
    join(info[0], pieces, joined)
    out[...] = dot_nt(joined[...], weight[...]).astype(BF)


def back_call(info, pieces, weights):
    rows = pieces[0].shape[2]
    width = 3 * 4 * HEAD_DIM
    piece = [
        pl.BlockSpec((parts, 1, TILE, HEAD_DIM), lambda i, info: (0, 0, i, 0))
        for parts in (3, 3, 2, 1, 2, 1)
    ]
    return pl.pallas_call(
        back_kernel,
        out_shape=jax.ShapeDtypeStruct((rows, D), BF),
        grid_spec=pltpu.PrefetchScalarGridSpec(
            num_scalar_prefetch=1,
            grid=(rows // TILE,),
            in_specs=piece + [pl.BlockSpec((D, width), lambda i, info: (0, 0))],
            out_specs=pl.BlockSpec((TILE, D), lambda i, info: (i, 0)),
            scratch_shapes=[pltpu.VMEM((TILE, width), BF)],
        ),
        compiler_params=params(VMEM),
        cost_estimate=cost(0, 0),
        name="back",
    )(info, *pieces, weights)


def attend_weight_kernel(info, normed, low, *refs):
    pieces, refs = refs[:6], refs[6:]
    attended, (keep, send, joined, out) = refs[:-4], refs[-4:]
    step = pl.program_id(0)

    @pl.when(step == 0)
    def _():
        join(info[0], pieces, joined)

    tile, width = normed.shape[1], joined.shape[1]
    left = normed[...].astype(F32).T.astype(BF)
    out[:, :width] = dot(left, joined[...]).astype(BF)
    left = low[...].astype(F32).T.astype(BF)
    out[:, width:] = dot(left, attended[0][...]).astype(BF)
    count, size = keep.shape[1], keep.shape[2]
    for line in range(tile // (4 * size)):
        slot = count - 1 - ((step * (tile // (4 * size)) + line) ^ info[4])
        for column in range(2):
            for target, core in ((keep, info[0]), (send, 1 - info[0])):
                side = info[3] if column == 0 else 1 - info[3]
                start = pl.multiple_of((line * 4 + side * 2 + core) * size, size)
                target[column, slot] = out[pl.ds(start, size), :]


def attend_weight_call(info, normed, low, attended, pieces, size):
    rows, half = normed.shape[0], attended.shape[1]
    width = 3 * half
    total = width + half
    left = pl.BlockSpec((rows, TILE), lambda i, info: (0, i))
    piece = [
        pl.BlockSpec((parts, 1, rows, HEAD_DIM), lambda i, info: (0, 0, 0, 0))
        for parts in (3, 3, 2, 1, 2, 1)
    ]
    count = D // (4 * size)
    return pl.pallas_call(
        attend_weight_kernel,
        out_shape=(jax.ShapeDtypeStruct((2, count, size, total), BF),) * 2,
        grid_spec=pltpu.PrefetchScalarGridSpec(
            num_scalar_prefetch=1,
            grid=(D // TILE,),
            in_specs=[left, left]
            + piece
            + [pl.BlockSpec((rows, half), lambda i, info: (0, 0))],
            out_specs=(pl.BlockSpec((2, count, size, total), lambda i, info: (0, 0, 0, 0)),) * 2,
            scratch_shapes=[pltpu.VMEM((rows, width), BF), pltpu.VMEM((TILE, total), BF)],
        ),
        compiler_params=params(VMEM),
        cost_estimate=cost(0, 0),
        name="attend_weights",
    )(info, normed, low, *pieces, attended)


def input_kernel(grad, back_own, back_other, tokens, gain, out):
    value = tokens[...].astype(F32)
    back = back_own[...].astype(F32) + back_other[...].astype(F32)
    inverse = lax.rsqrt(jnp.mean(value * value, axis=1, keepdims=True) + EPS)
    scaled = gain[...] * back
    inner = jnp.mean(scaled * value, axis=1, keepdims=True)
    out[...] = (grad[...] + inverse * scaled - value * (inverse**3 * inner)).astype(BF)


def input_call(grad, back_own, back_other, tokens, gain):
    rows = tokens.shape[0]
    wide = pl.BlockSpec((TILE, D), lambda i: (i, 0))
    return pl.pallas_call(
        input_kernel,
        out_shape=jax.ShapeDtypeStruct((rows, D), BF),
        grid=(rows // TILE,),
        in_specs=[wide, wide, wide, wide, pl.BlockSpec((1, D), lambda i: (0, 0))],
        out_specs=wide,
        compiler_params=params(VMEM),
        cost_estimate=cost(12 * rows * D, 12 * MIB),
        name="input_grad",
    )(grad, back_own, back_other, tokens, gain)


def choose(line, options):
    value = options[0]
    for here in range(1, len(options)):
        if options[here] is not options[0]:
            value = jnp.where(line == here, options[here], value)
    return value


def pair_kernel(keep, core, *outs):
    half = keep.shape[1] // 2
    for part in range(2):
        slots = slice(part * half, (part + 1) * half)
        for column in range(2):
            outs[2 * part + column][...] = (
                keep[column, slots].astype(F32) + core[column, slots].astype(F32)
            ).astype(BF)


def pair_add(keep, core):
    count, size, width = keep.shape[1:]
    return pl.pallas_call(
        pair_kernel,
        out_shape=(jax.ShapeDtypeStruct((count // 2, size, width), BF),) * 4,
        compiler_params=pltpu.CompilerParams(vmem_limit_bytes=VMEM * MIB),
        cost_estimate=cost(0, 0),
        name="pair_add",
    )(keep, core)


def split_kernel(left, right, *outs):
    for index, out in enumerate(outs):
        out[...] = (left[index].astype(F32) + right[index].astype(F32)).astype(BF)


def split_add(left, right):
    count, size, width = left.shape
    return pl.pallas_call(
        split_kernel,
        out_shape=(jax.ShapeDtypeStruct((size, width), BF),) * count,
        compiler_params=pltpu.CompilerParams(vmem_limit_bytes=VMEM * MIB),
        cost_estimate=cost(0, 0),
        name="split_add",
    )(left, right)


def low_kernel(left, right, out):
    out[...] = (left[...].astype(F32) + right[...].astype(F32)).astype(out.dtype)


def low_add(left, right):
    return pl.pallas_call(
        low_kernel,
        out_shape=jax.ShapeDtypeStruct(left.shape, BF),
        compiler_params=pltpu.CompilerParams(vmem_limit_bytes=VMEM * MIB),
        cost_estimate=cost(0, 0),
        name="low_add",
    )(left, right)


def chosen_kernel(flags, first, second, up_in, down_in, up, down):
    one, two = first[...].astype(F32), second[...].astype(F32)
    up[...] = (jnp.where(flags[0] > 0, one, two) + up_in[...].astype(F32)).astype(BF)
    down[...] = (jnp.where(flags[1] > 0, one, two) + down_in[...].astype(F32)).astype(BF)


def chosen_add(flags, first, second, up_in, down_in):
    shape = jax.ShapeDtypeStruct(first.shape, BF)
    vmem = pl.BlockSpec(memory_space=pltpu.VMEM)
    return pl.pallas_call(
        chosen_kernel,
        out_shape=(shape, shape),
        in_specs=[pl.BlockSpec(memory_space=pltpu.SMEM)] + [vmem] * 4,
        out_specs=(vmem, vmem),
        compiler_params=pltpu.CompilerParams(vmem_limit_bytes=VMEM * MIB),
        cost_estimate=cost(0, 0),
        name="chosen_add",
    )(flags, first, second, up_in, down_in)


def reduce_rows(keep, send, count, first_wait, last_wait):
    length = count // 4
    line = lax.axis_index("dp") // 4
    core = lax.ppermute(send, "dp", [(i, i ^ 1) for i in range(count)])
    mine_one, theirs_one, mine_two, theirs_two = pair_add(keep, core)
    pairs = [(i, i ^ 2) for i in range(count)]
    other_one, first_wait = pin((lax.ppermute(theirs_one, "dp", pairs), first_wait))
    sums = list(split_add(mine_one, other_one))
    other = lax.ppermute(theirs_two, "dp", pairs)
    above = below = None
    for step in range(1, length):
        gap = length - step
        slots = lambda towards: [
            length - 1 - (here ^ (here + towards)) if 0 <= here + towards < length else None
            for here in range(length)
        ]
        ups, downs = slots(gap), slots(-gap)
        used = sorted({slot for slot in ups + downs if slot is not None})
        if len(used) == 1 and step == 1:
            up = down = sums[used[0]]
        elif len(used) == 1:
            up, down = low_add(sums[used[0]], below), low_add(sums[used[0]], above)
        elif len(used) == 2:
            flags = jnp.stack(
                [
                    choose(line, [jnp.int32(slot == used[0]) for slot in side])
                    for side in (ups, downs)
                ]
            )
            up, down = chosen_add(flags, sums[used[0]], sums[used[1]], below, above)
        else:
            fill = lambda side: [sums[used[0] if slot is None else slot] for slot in side]
            up, down = choose(line, fill(ups)), choose(line, fill(downs))
            up, down = low_add(up, below), low_add(down, above)
        if step == length - 1:
            up, down, last_wait = pin((up, down, last_wait))
        below = lax.ppermute(up, "dp", [(i, i + 4) for i in range(count - 4) if i // 4 + gap < length])
        above = lax.ppermute(down, "dp", [(i, i - 4) for i in range(4, count) if i // 4 >= gap])
        if step == length // 2 - 1:
            below, above, other = pin((below, above, other))
            sums += split_add(mine_two, other)
    return sums[-1], below, above, first_wait, last_wait


def interleave_kernel(info, *refs):
    pieces, out = refs[:4], refs[4]
    size = out.shape[0] // (4 * pieces[0].shape[0])
    length = pieces[0].shape[0]
    for index, piece in enumerate(pieces):
        side = info[3] if index % 2 == 0 else 1 - info[3]
        core = info[0] if index // 2 == 0 else 1 - info[0]
        for line in range(length):
            start = pl.multiple_of((line * 4 + side * 2 + core) * size, size)
            out[pl.ds(start, size), :] = piece[line]


def interleave(info, pieces, size):
    width = pieces[0].shape[1]
    pieces = [piece.reshape(-1, size, width) for piece in pieces]
    vmem = pl.BlockSpec(memory_space=pltpu.VMEM)
    return pl.pallas_call(
        interleave_kernel,
        out_shape=pltpu.VMEM((D, width), BF),
        in_specs=[pl.BlockSpec(memory_space=pltpu.SMEM)] + [vmem] * 4,
        out_specs=vmem,
        compiler_params=pltpu.CompilerParams(vmem_limit_bytes=VMEM * MIB),
        cost_estimate=cost(0, 0),
        name="interleave",
    )(info, *pieces)


def gain_kernel(own, other, gain, first, second, first_out, second_out, gain_out):
    low = gain[...].astype(BF).astype(F32)
    results = adamw(gain[...], (own[...] + other[...]) / low, first[...], second[...], 0.6)
    for out, result in zip((first_out, second_out, gain_out), results):
        out[...] = result


def gain_call(own, other, gain, first, second):
    shape = jax.ShapeDtypeStruct(gain.shape, F32)
    return pl.pallas_call(
        gain_kernel,
        out_shape=(shape, shape, shape),
        compiler_params=pltpu.CompilerParams(vmem_limit_bytes=VMEM * MIB),
        cost_estimate=cost(0, 0),
        name="gains",
    )(own, other, gain, first, second)


def shard_kernel(qkv, gains, out):
    width = qkv.shape[2]
    for part in range(3):
        out[:, part * width : (part + 1) * width] = qkv[part].astype(BF)
    rows = jnp.concatenate([gains[...], jnp.zeros((HEAD_DIM - 2, gains.shape[1]), F32)])
    out[:, 3 * width :] = rows.T.astype(BF)


def shard_call(qkv, gains):
    total = 3 * qkv.shape[2] + HEAD_DIM
    return pl.pallas_call(
        shard_kernel,
        out_shape=jax.ShapeDtypeStruct((qkv.shape[1], total), BF),
        compiler_params=pltpu.CompilerParams(vmem_limit_bytes=VMEM * MIB),
        cost_estimate=cost(0, 0),
        name="shard",
    )(qkv, gains)


def pin(values):
    return lax.optimization_barrier(values)


def body(
    tokens,
    cotangent,
    proj_qkv,
    proj_out,
    proj_gate_up,
    proj_down,
    norm_gains,
    first_qkv,
    first_out,
    first_gate_up,
    first_down,
    first_gains,
    second_qkv,
    second_out,
    second_gate_up,
    second_down,
    second_gains,
    cache,
    doc_segments,
    padding,
    retrieval,
):
    rows = tokens.shape[0]
    count = lax.axis_size("dp")
    device = lax.axis_index("dp")
    group = lax.axis_index("mp")
    rank = device % 2
    segment = device // 2
    shard = proj_qkv.shape[1]
    local = proj_qkv.shape[2]
    hidden_here = proj_gate_up.shape[2]
    core_pairs = [(i, i ^ 1) for i in range(count)]

    def across(value):
        return lax.ppermute(value, "mp", [(0, 1), (1, 0)])

    def beside(value):
        return lax.ppermute(value, "dp", core_pairs)

    shard_one = shard_call(proj_qkv, norm_gains)
    out_own = proj_out.astype(BF).T
    out_other = across(out_own)
    shard_two = jnp.concatenate(
        [
            proj_gate_up[0].astype(BF),
            proj_gate_up[1].astype(BF),
            proj_down.astype(BF).T,
            jnp.where(group == 0, out_own, out_other),
            jnp.where(group == 0, out_other, out_own),
        ],
        axis=1,
    )
    length = count // 4
    lines = [[i for i in range(count) if i % 4 == lane] for lane in range(4)]
    own_column = lax.all_gather(shard_one, "dp", axis=0, tiled=True, axis_index_groups=lines)
    next_column = lax.ppermute(own_column, "dp", [(i, i ^ 2) for i in range(count)])
    pieces = (own_column, next_column, beside(own_column), beside(next_column))
    weights_two = lax.all_gather(shard_two, "dp", axis=0, tiled=True)

    places = jnp.arange(SEG, dtype=jnp.int32)
    starts = jnp.cumsum(doc_segments) - doc_segments
    memory_on = jnp.logical_not(jnp.any(starts == segment))
    side = (device // 2) % 2
    info = jnp.stack([rank, group, memory_on.astype(jnp.int32), side, device // 4]).astype(jnp.int32)
    cosines, sines = rope_tables(places)
    valid = lax.dynamic_slice_in_dim(padding, segment * SEG, SEG)
    lane = jnp.arange(HEAD_DIM, dtype=jnp.int32)[None, :]
    bias = jnp.where((valid[:, None] == 0) & (lane == 0), NEGATIVE, 0.0).astype(BF)
    fetched = cache[retrieval[0]].reshape(RETR, 2, 2, 2, HEAD_DIM).transpose(2, 1, 3, 0, 4)
    mem_own = lax.dynamic_index_in_dim(fetched, rank, keepdims=False)
    mem_other = beside(lax.dynamic_index_in_dim(fetched, 1 - rank, keepdims=False))
    pieces, mem_own, mem_other, bias, cosines, sines, info = pin(
        (pieces, mem_own, mem_other, bias, cosines, sines, info)
    )
    weights_one = interleave(info, pieces, shard)

    send, normed_one, gains = project_first(info, tokens, weights_one, cosines, sines)
    gain_one, gain_two = gains[0:1], gains[1:2]
    other = beside(send)
    own = project_second(info, normed_one, weights_one, cosines, sines)
    out_keep, out_send, turned, logs = attend_forward(info, own, other, mem_own, mem_other, bias)
    out_recv = beside(out_send)
    pieces = (out_keep, out_recv, across(out_keep), across(out_recv))
    middle, normed_two, attended = middle_call(info, pieces, tokens, weights_two, gain_two)

    earlier, backs, backs_other = (), [], []
    for chunk, first in enumerate(range(0, rows, TILE)):
        if first + TILE == rows:
            earlier, backs_other[0] = pin((earlier, backs_other[0]))
        *earlier, back = feed_call(normed_two, cotangent, weights_two, first, TILE, earlier)
        backs.append(back)
        backs_other.append(across(back))
    hidden, grad_gate, grad_up, feed_part = earlier
    hidden, backs_other[1] = pin((hidden, backs_other[1]))
    feed_grads = feed_weight_call(normed_two, cotangent, hidden, grad_gate, grad_up)
    feed_other = across(feed_part)
    backs[2], _ = pin((backs[2], feed_grads))
    earlier = ()
    for index in (2, 3, 0, 1):
        first = index * TILE
        earlier = residual_call(
            info, middle, backs[index], backs_other[index], cotangent, gain_two, weights_two,
            first, earlier,
        )
    grad_middle, grad_low, grad_keep, *grad_sends = earlier
    grad_others = [beside(value) for value in grad_sends]

    d_keeps, d_others = [], []
    for head in range(2):
        d_keep, d_send, d_send_v = attend_backward(
            info, own, other, mem_own, mem_other, bias, grad_keep, grad_others[head], turned, logs,
            cosines, sines, head,
        )
        d_keeps.append(d_keep)
        d_others += [beside(d_send), beside(d_send_v)]
    moved = d_keeps + d_others
    back_one = back_call(info, moved, weights_one)
    moved[0], _ = pin((moved[0], back_one))
    attend_keep, attend_send = attend_weight_call(info, normed_one, grad_low, attended, moved, shard)
    back_one, feed_other = pin((back_one, feed_other))
    back_one_other = across(back_one)
    input_grad = input_call(grad_middle, back_one, back_one_other, tokens, gain_one)
    block_out = (
        middle + (feed_part.astype(F32) + feed_other.astype(F32))
    ).astype(BF)
    total, below, above, block_out, input_grad = reduce_rows(
        attend_keep, attend_send, count, block_out, input_grad
    )
    feed_sum = lax.psum_scatter(feed_grads, "dp", scatter_dimension=0, tiled=True).astype(F32)
    gate_up_sum = jnp.stack([feed_sum[:, :hidden_here], feed_sum[:, hidden_here : 2 * hidden_here]])
    down_sum = feed_sum[:, 2 * hidden_here :].T
    gate_up_first, gate_up_second, gate_up_new = adamw(
        proj_gate_up, gate_up_sum, first_gate_up, second_gate_up, 0.5 / math.sqrt(D)
    )
    down_first, down_second, down_new = adamw(
        proj_down, down_sum, first_down, second_down, 0.5 / math.sqrt(FF)
    )
    gate_up_new, down_new, total, below, above = pin((gate_up_new, down_new, total, below, above))
    attend_sum = total.astype(F32) + (below.astype(F32) + above.astype(F32))
    qkv_sum = jnp.stack([attend_sum[:, part * local : (part + 1) * local] for part in range(3)])
    out_sum = attend_sum[:, 3 * local : 4 * local].T
    low_qkv, low_gate_up = proj_qkv.astype(BF).astype(F32), proj_gate_up.astype(BF).astype(F32)
    gains_sum = jnp.stack(
        [jnp.sum(low_qkv * qkv_sum, axis=(0, 2)), jnp.sum(low_gate_up * gate_up_sum, axis=(0, 2))]
    )
    gains_first, gains_second, gains_new = gain_call(
        gains_sum, across(gains_sum), norm_gains, first_gains, second_gains
    )

    qkv_first, qkv_second, qkv_new = adamw(
        proj_qkv, qkv_sum, first_qkv, second_qkv, 0.5 / math.sqrt(D)
    )
    out_first, out_second, out_new = adamw(
        proj_out, out_sum, first_out, second_out, 0.5 / math.sqrt(max(1, 4 * D // SEG))
    )
    return (
        block_out,
        input_grad,
        qkv_first,
        qkv_second,
        qkv_new,
        out_first,
        out_second,
        out_new,
        gate_up_first,
        gate_up_second,
        gate_up_new,
        down_first,
        down_second,
        down_new,
        gains_first,
        gains_second,
        gains_new,
    )


def solution(mesh):
    return jax.shard_map(
        body,
        mesh=mesh,
        in_specs=(
            P("dp", None),
            P("dp", None),
            P(None, "dp", "mp"),
            P("mp", "dp"),
            P(None, "dp", "mp"),
            P("mp", "dp"),
            P(None, "dp"),
            P(None, "dp", "mp"),
            P("mp", "dp"),
            P(None, "dp", "mp"),
            P("mp", "dp"),
            P(None, "dp"),
            P(None, "dp", "mp"),
            P("mp", "dp"),
            P(None, "dp", "mp"),
            P("mp", "dp"),
            P(None, "dp"),
            P("dp", None, "mp"),
            P(),
            P(),
            P("dp", None),
        ),
        out_specs=(
            P("dp", None),
            P("dp", None),
            P(None, "dp", "mp"),
            P(None, "dp", "mp"),
            P(None, "dp", "mp"),
            P("mp", "dp"),
            P("mp", "dp"),
            P("mp", "dp"),
            P(None, "dp", "mp"),
            P(None, "dp", "mp"),
            P(None, "dp", "mp"),
            P("mp", "dp"),
            P("mp", "dp"),
            P("mp", "dp"),
            P(None, "dp"),
            P(None, "dp"),
            P(None, "dp"),
        ),
        check_vma=False,
    )
```

```python
import functools
import math

import jax
import jax.numpy as jnp
from jax import lax
from jax.experimental import pallas as pl
from jax.experimental.pallas import tpu as pltpu
from jax.sharding import PartitionSpec as P

D = 1024
HEAD_DIM = 128
FF = 2816
SEG = 2048
RETR = 128
STEP = 10

EPS = 1e-05
BETA_ONE = 0.9
BETA_TWO = 0.95
ADAM_EPS = 1e-08
DECAY = 0.1
NEGATIVE = -1e30
SCALE = HEAD_DIM**-0.5
SCALE_TWO = SCALE * math.log2(math.e)

BF = jnp.bfloat16
F32 = jnp.float32
MIB = 1024 * 1024
TILE = 256
VMEM = 26
WEIGH = 1.0


def dot(left, right):
    return jnp.dot(left, right, preferred_element_type=F32)


def dot_nt(left, right):
    return lax.dot_general(left, right, (((1,), (1,)), ((), ())), preferred_element_type=F32)


def dot_tn(left, right):
    return lax.dot_general(left, right, (((0,), (0,)), ((), ())), preferred_element_type=F32)


def params(mib, axes=1):
    return pltpu.CompilerParams(
        dimension_semantics=("arbitrary",) * axes, vmem_limit_bytes=mib * MIB
    )


def cost(flops, moved, trans=0):
    return pl.CostEstimate(flops=int(flops * WEIGH), bytes_accessed=int(moved * WEIGH), transcendentals=int(trans))


def rope_tables(places):
    half_dim = HEAD_DIM // 2
    freqs = 10000.0 ** (-(jnp.arange(half_dim, dtype=F32) / half_dim))
    phase = places.astype(F32)[:, None] * freqs[None, :]
    cosines, sines = jnp.cos(phase), jnp.sin(phase)
    return jnp.concatenate([cosines, cosines], 1), jnp.concatenate([-sines, sines], 1)


def turn(value, cosines, sines):
    return value * cosines + pltpu.roll(value, HEAD_DIM // 2, 1) * sines


def adamw(weight, grad, first, second, rate):
    first_new = BETA_ONE * first + (1.0 - BETA_ONE) * grad
    second_new = BETA_TWO * second + (1.0 - BETA_TWO) * grad * grad
    first_hat = first_new / (1.0 - BETA_ONE**STEP)
    second_hat = second_new / (1.0 - BETA_TWO**STEP)
    updated = weight - rate * (first_hat / (jnp.sqrt(second_hat) + ADAM_EPS) + DECAY * weight)
    return (first_new, second_new, updated)


def rotate_out(result, part, cosines, sines, out):
    for head in range(2):
        value = result[:, head * HEAD_DIM : (head + 1) * HEAD_DIM]

        @pl.when(part < 2)
        def _():
            out[0, head] = turn(value, cosines[...], sines[...]).astype(BF)

        @pl.when(part == 2)
        def _():
            out[0, head] = value.astype(BF)


def first_kernel(info, tokens, gain_columns, weight, cosines, sines, out, normed, gains):
    part = pl.program_id(0)

    @pl.when(part == 0)
    def _():
        rows = gain_columns[...].astype(F32).T[:8, :]
        gains[...] = rows
        value = tokens[...].astype(F32)
        inverse = lax.rsqrt(jnp.mean(value * value, axis=1, keepdims=True) + EPS)
        normed[...] = (value * inverse * rows[0:1, :]).astype(BF)

    rotate_out(dot(normed[...], weight[...]), part, cosines, sines, out)


def second_kernel(info, normed, weight, cosines, sines, out):
    rotate_out(dot(normed[...], weight[...]), pl.program_id(0), cosines, sines, out)


def project_first(info, tokens, weights, cosines, sines):
    rows = tokens.shape[0]
    return pl.pallas_call(
        first_kernel,
        out_shape=(
            jax.ShapeDtypeStruct((3, 2, rows, HEAD_DIM), BF),
            jax.ShapeDtypeStruct((rows, D), BF),
            jax.ShapeDtypeStruct((8, D), F32),
        ),
        grid_spec=pltpu.PrefetchScalarGridSpec(
            num_scalar_prefetch=1,
            grid=(3,),
            in_specs=[
                pl.BlockSpec((rows, D), lambda j, info: (0, 0)),
                pl.BlockSpec((D, HEAD_DIM), lambda j, info: (0, 12)),
                pl.BlockSpec((D, 256), lambda j, info: (0, 2 * j + 1 - info[0])),
                pl.BlockSpec((rows, HEAD_DIM), lambda j, info: (info[0], 0)),
                pl.BlockSpec((rows, HEAD_DIM), lambda j, info: (info[0], 0)),
            ],
            out_specs=(
                pl.BlockSpec((1, 2, rows, HEAD_DIM), lambda j, info: (j, 0, 0, 0)),
                pl.BlockSpec((rows, D), lambda j, info: (0, 0)),
                pl.BlockSpec((8, D), lambda j, info: (0, 0)),
            ),
        ),
        compiler_params=params(VMEM),
        cost_estimate=cost(0, 0),
        name="project_first",
    )(info, tokens, weights, weights, cosines, sines)


def project_second(info, normed, weights, cosines, sines):
    rows = normed.shape[0]
    return pl.pallas_call(
        second_kernel,
        out_shape=jax.ShapeDtypeStruct((3, 2, rows, HEAD_DIM), BF),
        grid_spec=pltpu.PrefetchScalarGridSpec(
            num_scalar_prefetch=1,
            grid=(3,),
            in_specs=[
                pl.BlockSpec((rows, D), lambda j, info: (0, 0)),
                pl.BlockSpec((D, 256), lambda j, info: (0, 2 * j + info[0])),
                pl.BlockSpec((rows, HEAD_DIM), lambda j, info: (info[0], 0)),
                pl.BlockSpec((rows, HEAD_DIM), lambda j, info: (info[0], 0)),
            ],
            out_specs=pl.BlockSpec((1, 2, rows, HEAD_DIM), lambda j, info: (j, 0, 0, 0)),
        ),
        compiler_params=params(VMEM),
        cost_estimate=cost(0, 0),
        name="project_second",
    )(info, normed, weights, cosines, sines)


def place(scratch, own, other, rank, rows):
    scratch[pl.ds(pl.multiple_of(rank * rows, rows), rows), :] = own
    scratch[pl.ds(pl.multiple_of((1 - rank) * rows, rows), rows), :] = other


def chunks_of(tile, step):
    end = tile * TILE
    spans = [(start, min(step, end - start)) for start in range(0, end, step)]
    return spans + [(end, TILE)]


def causal(scores):
    rows = lax.broadcasted_iota(jnp.int32, scores.shape, 0)
    columns = lax.broadcasted_iota(jnp.int32, scores.shape, 1)
    return jnp.where(rows <= columns, scores, NEGATIVE)


def forward_kernel(
    info, own, other, mem_own, mem_other, bias, keep, send, turned, logs,
    q_s, k_s, v_s, vt_s, mem_s, s_s, out_s,
):
    rank = info[0]
    rows = own.shape[2]
    mem_bias = jnp.where(info[2] > 0, 0.0, NEGATIVE).astype(F32)
    place(q_s, own[0, 0], other[0, 0], rank, rows)
    place(k_s, own[1, 0], other[1, 0], rank, rows)
    place(v_s, own[2, 0], other[2, 0], rank, rows)
    mem_s[rank] = mem_own[:, 0]
    mem_s[1 - rank] = mem_other[:, 0]
    vt_s[...] = v_s[...].astype(F32).T.astype(BF)
    ones = (lax.broadcasted_iota(jnp.int32, (TILE, HEAD_DIM), 1) == 0).astype(BF)
    for tile in range(SEG // TILE):
        here = slice(tile * TILE, (tile + 1) * TILE)
        block = tile * TILE // rows
        query = q_s[here, :]
        wide = jnp.concatenate([query, ones], axis=1)
        spans = chunks_of(tile, 512)
        scores = dot_nt(mem_s[block, 0], query) + mem_bias
        s_s[SEG : SEG + RETR, :] = scores
        top = jnp.max(scores, axis=0, keepdims=True)
        for start, size in spans:
            span = slice(start, start + size)
            if start + size > SEG // 2:
                scores = dot_nt(jnp.concatenate([k_s[span, :], bias[span, :]], axis=1), wide)
            else:
                scores = dot_nt(k_s[span, :], query)
            if start == tile * TILE:
                scores = causal(scores)
            s_s[span, :] = scores
            top = jnp.maximum(top, jnp.max(scores, axis=0, keepdims=True))
        shift = top * SCALE_TWO
        exponent = jnp.exp2(s_s[SEG : SEG + RETR, :] * SCALE_TWO - shift)
        total = jnp.sum(exponent, axis=0, keepdims=True)
        result = dot(mem_s[block, 1].astype(F32).T.astype(BF), exponent.astype(BF))
        for start, size in spans:
            span = slice(start, start + size)
            exponent = jnp.exp2(s_s[span, :] * SCALE_TWO - shift)
            total = total + jnp.sum(exponent, axis=0, keepdims=True)
            result = result + dot(vt_s[:, span], exponent.astype(BF))
        result = result * (1.0 / total)
        turned[0, :, here] = result
        logs[0, :, here] = shift + jnp.log2(total)
        out_s[here, :] = result.T.astype(BF)
    keep[0] = out_s[pl.ds(pl.multiple_of(rank * rows, rows), rows), :]
    send[0] = out_s[pl.ds(pl.multiple_of((1 - rank) * rows, rows), rows), :]


def attend_forward(info, own, other, mem_own, mem_other, bias):
    rows = own.shape[2]
    part = pl.BlockSpec((3, 1, rows, HEAD_DIM), lambda h, info: (0, h, 0, 0))
    mem = pl.BlockSpec((2, 1, RETR, HEAD_DIM), lambda h, info: (0, h, 0, 0))
    half = pl.BlockSpec((1, rows, HEAD_DIM), lambda h, info: (h, 0, 0))
    return pl.pallas_call(
        forward_kernel,
        out_shape=(
            jax.ShapeDtypeStruct((2, rows, HEAD_DIM), BF),
            jax.ShapeDtypeStruct((2, rows, HEAD_DIM), BF),
            pltpu.HBM((2, HEAD_DIM, SEG), F32),
            jax.ShapeDtypeStruct((2, 1, SEG), F32),
        ),
        grid_spec=pltpu.PrefetchScalarGridSpec(
            num_scalar_prefetch=1,
            grid=(2,),
            in_specs=[
                part,
                part,
                mem,
                mem,
                pl.BlockSpec((SEG, HEAD_DIM), lambda h, info: (0, 0)),
            ],
            out_specs=(
                half,
                half,
                pl.BlockSpec((1, HEAD_DIM, SEG), lambda h, info: (h, 0, 0)),
                pl.BlockSpec((1, 1, SEG), lambda h, info: (h, 0, 0)),
            ),
            scratch_shapes=[
                pltpu.VMEM((SEG, HEAD_DIM), BF),
                pltpu.VMEM((SEG, HEAD_DIM), BF),
                pltpu.VMEM((SEG, HEAD_DIM), BF),
                pltpu.VMEM((HEAD_DIM, SEG), BF),
                pltpu.VMEM((2, 2, RETR, HEAD_DIM), BF),
                pltpu.VMEM((SEG + RETR, TILE), F32),
                pltpu.VMEM((SEG, HEAD_DIM), BF),
            ],
        ),
        compiler_params=params(VMEM),
        cost_estimate=cost(0, 0),
        name="attend_forward",
    )(info, own, other, mem_own, mem_other, bias)


def backward_kernel(
    info, own, other, mem_own, mem_other, bias, grad_own, grad_other, turned, logs, cosines, sines,
    keep, send, send_v,
    q_s, k_s, v_s, g_s, kt_s, mem_s, dots_s, dq_s, dk_s, dv_s,
):
    rank = info[0]
    rows = own.shape[2]
    mem_bias = jnp.where(info[2] > 0, 0.0, NEGATIVE).astype(F32)
    place(q_s, own[0, 0], other[0, 0], rank, rows)
    place(k_s, own[1, 0], other[1, 0], rank, rows)
    place(v_s, own[2, 0], other[2, 0], rank, rows)
    place(g_s, grad_own[0], grad_other[0], rank, rows)
    mem_s[rank] = mem_own[:, 0]
    mem_s[1 - rank] = mem_other[:, 0]
    kt_s[...] = k_s[...].astype(F32).T.astype(BF)
    dots_s[...] = jnp.sum(g_s[...].astype(F32).T * turned[0], axis=0, keepdims=True)
    dk_s[...] = jnp.zeros_like(dk_s)
    dv_s[...] = jnp.zeros_like(dv_s)
    ones = (lax.broadcasted_iota(jnp.int32, (TILE, HEAD_DIM), 1) == 0).astype(BF)
    for tile in range(SEG // TILE):
        here = slice(tile * TILE, (tile + 1) * TILE)
        block = tile * TILE // rows
        query = q_s[here, :]
        wide = jnp.concatenate([query, ones], axis=1)
        grad = g_s[here, :]
        log = logs[0, :, here]
        dots = dots_s[:, here]
        scores = dot_nt(mem_s[block, 0], query) + mem_bias
        probs = jnp.exp2(scores * SCALE_TWO - log)
        change = (probs * (dot_nt(mem_s[block, 1], grad) - dots)).astype(BF)
        result = dot(mem_s[block, 0].astype(F32).T.astype(BF), change)
        for start, size in chunks_of(tile, 512):
            span = slice(start, start + size)
            keys = k_s[span, :]
            if start + size > SEG // 2:
                scores = dot_nt(jnp.concatenate([keys, bias[span, :]], axis=1), wide)
            else:
                scores = dot_nt(keys, query)
            if start == tile * TILE:
                scores = causal(scores)
            probs = jnp.exp2(scores * SCALE_TWO - log)
            change = (probs * (dot_nt(v_s[span, :], grad) - dots)).astype(BF)
            dv_s[span, :] += dot(probs.astype(BF), grad)
            dk_s[span, :] += dot(change, query)
            result = result + dot(kt_s[:, span], change)
        dq_s[here, :] = turn(result.T * SCALE, cosines[here, :], -sines[here, :]).astype(BF)
    for outs, place_ in (((keep.at[0], keep.at[1], keep.at[2]), rank), ((send.at[0], send.at[1], send_v.at[0]), 1 - rank)):
        held = pl.ds(pl.multiple_of(place_ * rows, rows), rows)
        outs[0][0] = dq_s[held, :]
        outs[1][0] = turn(dk_s[held, :] * SCALE, cosines[held, :], -sines[held, :]).astype(BF)
        outs[2][0] = dv_s[held, :].astype(BF)


def attend_backward(
    info, own, other, mem_own, mem_other, bias, grad_own, grad_other, turned, logs, cosines, sines, head
):
    rows = own.shape[2]
    part = pl.BlockSpec((3, 1, rows, HEAD_DIM), lambda h, info: (0, head, 0, 0))
    mem = pl.BlockSpec((2, 1, RETR, HEAD_DIM), lambda h, info: (0, head, 0, 0))
    half = pl.BlockSpec((1, rows, HEAD_DIM), lambda h, info: (head, 0, 0))
    table = pl.BlockSpec((SEG, HEAD_DIM), lambda h, info: (0, 0))
    return pl.pallas_call(
        backward_kernel,
        out_shape=tuple(jax.ShapeDtypeStruct((parts, 1, rows, HEAD_DIM), BF) for parts in (3, 2, 1)),
        grid_spec=pltpu.PrefetchScalarGridSpec(
            num_scalar_prefetch=1,
            grid=(1,),
            in_specs=[
                part,
                part,
                mem,
                mem,
                table,
                half,
                pl.BlockSpec((1, rows, HEAD_DIM), lambda h, info: (0, 0, 0)),
                pl.BlockSpec((1, HEAD_DIM, SEG), lambda h, info: (head, 0, 0)),
                pl.BlockSpec((1, 1, SEG), lambda h, info: (head, 0, 0)),
                table,
                table,
            ],
            out_specs=tuple(
                pl.BlockSpec((parts, 1, rows, HEAD_DIM), lambda h, info: (0, 0, 0, 0)) for parts in (3, 2, 1)
            ),
            scratch_shapes=[pltpu.VMEM((SEG, HEAD_DIM), BF)] * 4
            + [
                pltpu.VMEM((HEAD_DIM, SEG), BF),
                pltpu.VMEM((2, 2, RETR, HEAD_DIM), BF),
                pltpu.VMEM((1, SEG), F32),
                pltpu.VMEM((SEG, HEAD_DIM), BF),
                pltpu.VMEM((SEG, HEAD_DIM), F32),
                pltpu.VMEM((SEG, HEAD_DIM), F32),
            ],
        ),
        compiler_params=params(VMEM),
        cost_estimate=cost(0, 0),
        name="attend_backward",
    )(
        info, own, other, mem_own, mem_other, bias, grad_own, grad_other, turned, logs, cosines, sines
    )


OUT_AT = 3 * FF // 2


def in_hbm(value):
    return pltpu.with_memory_space_constraint(value, pltpu.HBM)


def columns(width, start):
    return pl.BlockSpec(
        (pl.Element(D), pl.Element(width)), start, pipeline_mode=pl.Buffered(1)
    )


def middle_kernel(info, *refs):
    pieces, (tokens, weight, gain, middle, normed, attended, joined) = refs[:4], refs[4:]
    rank, group = info[0], info[1]
    for index, piece in enumerate(pieces):
        side = (group, 1 - group)[index // 2]
        pair = (rank, 1 - rank)[index % 2]
        for head in range(2):
            column = pl.multiple_of((side * 4 + pair * 2 + head) * HEAD_DIM, HEAD_DIM)
            joined[:, pl.ds(column, HEAD_DIM)] = piece[head]
    half = attended.shape[1]
    attended[...] = joined[:, pl.ds(pl.multiple_of(group * half, half), half)]
    value = tokens[...].astype(F32) + dot_nt(joined[...], weight[...])
    middle[...] = value
    inverse = lax.rsqrt(jnp.mean(value * value, axis=1, keepdims=True) + EPS)
    normed[...] = (value * inverse * gain[...]).astype(BF)


def middle_call(info, pieces, tokens, weights, gain):
    rows, half = tokens.shape[0], 4 * HEAD_DIM
    piece = pl.BlockSpec((2, TILE, HEAD_DIM), lambda i, info: (0, i, 0))
    wide = pl.BlockSpec((TILE, D), lambda i, info: (i, 0))
    return pl.pallas_call(
        middle_kernel,
        out_shape=(
            pltpu.HBM((rows, D), F32),
            jax.ShapeDtypeStruct((rows, D), BF),
            pltpu.HBM((rows, half), BF),
        ),
        grid_spec=pltpu.PrefetchScalarGridSpec(
            num_scalar_prefetch=1,
            grid=(rows // TILE,),
            in_specs=[piece] * 4
            + [
                wide,
                columns(D, lambda i, info: (0, OUT_AT)),
                pl.BlockSpec((1, D), lambda i, info: (0, 0)),
            ],
            out_specs=(wide, wide, pl.BlockSpec((TILE, half), lambda i, info: (i, 0))),
            scratch_shapes=[pltpu.VMEM((TILE, D), BF)],
        ),
        compiler_params=params(VMEM),
        cost_estimate=cost(0, 0),
        name="middle",
    )(info, *[in_hbm(piece) for piece in pieces], in_hbm(tokens), in_hbm(weights), gain)


def feed_kernel(normed, upstream, gate_w, up_w, down_w, *refs):
    hidden, gate_grad, up_grad, feed, back = refs[-5:]
    gate = dot(normed[...], gate_w[...])
    up_part = dot(normed[...], up_w[...])
    sigma = jax.nn.sigmoid(gate)
    silu = gate * sigma
    low = (silu * up_part).astype(BF)
    hidden[...] = low
    feed[...] = dot_nt(low, down_w[...]).astype(BF)
    grad = dot(upstream[...], down_w[...])
    grad_gate = (grad * up_part * sigma * (1.0 + gate * (1.0 - sigma))).astype(BF)
    grad_up = (grad * silu).astype(BF)
    gate_grad[...] = grad_gate
    up_grad[...] = grad_up
    back[...] = (dot_nt(grad_gate, gate_w[...]) + dot_nt(grad_up, up_w[...])).astype(BF)


def feed_call(normed, upstream, weights, first, count, earlier):
    rows = upstream.shape[0]
    width = FF // 2
    whole = lambda index: pl.BlockSpec((D, width), lambda i: (0, index), pipeline_mode=pl.Buffered(1))
    source = pl.BlockSpec((TILE, D), lambda i: (i + first // TILE, 0))
    narrow = pl.BlockSpec((TILE, width), lambda i: (i + first // TILE, 0))
    return pl.pallas_call(
        feed_kernel,
        out_shape=(pltpu.VMEM((rows, width), BF),) * 3
        + (jax.ShapeDtypeStruct((rows, D), BF), jax.ShapeDtypeStruct((count, D), BF)),
        grid=(count // TILE,),
        in_specs=[source, source, whole(0), whole(1), whole(2)]
        + [pl.BlockSpec(memory_space=pl.ANY)] * len(earlier),
        out_specs=(narrow, narrow, narrow, source, pl.BlockSpec((TILE, D), lambda i: (i, 0))),
        input_output_aliases={5 + index: index for index in range(len(earlier))},
        compiler_params=params(VMEM),
        cost_estimate=cost(5e7, 0),
        name="feed",
    )(normed, upstream, weights, weights, weights, *earlier)


DOWN_SPLIT = 768


DOWN_SPLIT = 768


def scatter(info, out, keep, send):
    step, tile = pl.program_id(0), out.shape[0]
    count, size = keep.shape[1], keep.shape[2]
    for line in range(tile // (4 * size)):
        slot = count - 1 - ((step * (tile // (4 * size)) + line) ^ info[4])
        for column in range(2):
            for target, core in ((keep, info[0]), (send, 1 - info[0])):
                side = info[3] if column == 0 else 1 - info[3]
                start = pl.multiple_of((line * 4 + side * 2 + core) * size, size)
                target[column, slot] = out[pl.ds(start, size), :]


def feed_weight_kernel(info, normed, upstream, hidden, gate_grad, up_grad, out, keep, send, last):
    width = gate_grad.shape[1]
    left = normed[...].astype(F32).T.astype(BF)
    out[:, :width] = dot(left, gate_grad[...]).astype(BF)
    out[:, width : 2 * width] = dot(left, up_grad[...]).astype(BF)
    left = upstream[...].astype(F32).T.astype(BF)
    result = dot(left, hidden[...]).astype(BF)
    out[:, 2 * width :] = result[:, :DOWN_SPLIT]
    last[...] = result[:, DOWN_SPLIT:]
    scatter(info, last, keep, send)


def feed_weight_call(info, normed, upstream, hidden, gate_grad, up_grad, size):
    rows, width = gate_grad.shape
    total, rest, count = 2 * width + DOWN_SPLIT, width - DOWN_SPLIT, D // (4 * size)
    left = pl.BlockSpec((rows, TILE), lambda i, info: (0, i))
    whole = pl.BlockSpec((rows, width), lambda i, info: (0, 0), pipeline_mode=pl.Buffered(1))
    return pl.pallas_call(
        feed_weight_kernel,
        out_shape=(pltpu.HBM((D, total), BF),)
        + (jax.ShapeDtypeStruct((2, count, size, rest), BF),) * 2,
        grid_spec=pltpu.PrefetchScalarGridSpec(
            num_scalar_prefetch=1,
            grid=(D // TILE,),
            in_specs=[left, left, whole, whole, whole],
            out_specs=(pl.BlockSpec((TILE, total), lambda i, info: (i, 0)),)
            + (pl.BlockSpec((2, count, size, rest), lambda i, info: (0, 0, 0, 0)),) * 2,
            scratch_shapes=[pltpu.VMEM((TILE, rest), BF)],
        ),
        compiler_params=params(24),
        cost_estimate=cost(5e7, 0),
        name="feed_weights",
    )(info, normed, in_hbm(upstream), hidden, gate_grad, up_grad)


def residual_kernel(count, info, middle, upstream, gain, weight, *refs):
    grad, low, keep, send_one, send_two, back_s = refs[-6:]
    rank = info[0]
    for index in range(count):

        @pl.when(pl.program_id(0) == index)
        def _():
            back_s[...] = refs[index][...].astype(F32) + refs[count + index][...].astype(F32)

    value = middle[...]
    inverse = lax.rsqrt(jnp.mean(value * value, axis=1, keepdims=True) + EPS)
    scaled = gain[...] * back_s[...]
    inner = jnp.mean(scaled * value, axis=1, keepdims=True)
    total = upstream[...].astype(F32) + inverse * scaled - value * (inverse**3 * inner)
    grad[...] = total
    branch = total.astype(BF)
    low[...] = branch
    for outs, pair in (((keep.at[0], keep.at[1]), rank), ((send_one.at[0], send_two.at[0]), 1 - rank)):
        column = pl.multiple_of(pair * 2 * HEAD_DIM, 2 * HEAD_DIM)
        result = dot(branch, weight[:, pl.ds(column, 2 * HEAD_DIM)]).astype(BF)
        for head in range(2):
            outs[head][...] = result[:, head * HEAD_DIM : (head + 1) * HEAD_DIM]


def residual_call(info, middle, owns, others, upstream, gain, weights, first, earlier):
    rows, half, count = upstream.shape[0], 4 * HEAD_DIM, len(owns)
    wide = pl.BlockSpec((TILE, D), lambda i, info: (i + first, 0))
    part = pl.BlockSpec((TILE, D), lambda i, info: (0, 0), pipeline_mode=pl.Buffered(1))
    piece = pl.BlockSpec((2, TILE, HEAD_DIM), lambda i, info: (0, i + first, 0))
    single = pl.BlockSpec((1, TILE, HEAD_DIM), lambda i, info: (0, i + first, 0))
    return pl.pallas_call(
        functools.partial(residual_kernel, count),
        out_shape=(
            pltpu.HBM((rows, D), F32),
            jax.ShapeDtypeStruct((rows, D), BF),
            jax.ShapeDtypeStruct((2, rows, HEAD_DIM), BF),
            jax.ShapeDtypeStruct((1, rows, HEAD_DIM), BF),
            jax.ShapeDtypeStruct((1, rows, HEAD_DIM), BF),
        ),
        grid_spec=pltpu.PrefetchScalarGridSpec(
            num_scalar_prefetch=1,
            grid=(count,),
            in_specs=[
                wide,
                wide,
                pl.BlockSpec((1, D), lambda i, info: (0, 0)),
                columns(half, lambda i, info: (0, pl.multiple_of(OUT_AT + info[1] * half, HEAD_DIM))),
            ]
            + [part] * (2 * count)
            + [pl.BlockSpec(memory_space=pl.ANY)] * len(earlier),
            out_specs=(wide, wide, piece, single, single),
            scratch_shapes=[pltpu.VMEM((TILE, D), F32)],
        ),
        input_output_aliases={5 + 2 * count + index: index for index in range(len(earlier))},
        compiler_params=params(18),
        cost_estimate=cost(3e11 if first + count == rows // TILE else 5e7, 0),
        name="residual",
    )(info, in_hbm(middle), in_hbm(upstream), gain, in_hbm(weights), *owns, *others, *earlier)


def join(rank, pieces, joined):
    for head in range(2):
        own, other, other_v = pieces[head], pieces[2 + 2 * head], pieces[3 + 2 * head]
        for part in range(3):
            for value, pair in (
                (own[part, 0], rank),
                (other_v[0, 0] if part == 2 else other[part, 0], 1 - rank),
            ):
                column = pl.multiple_of((part * 4 + pair * 2 + head) * HEAD_DIM, HEAD_DIM)
                joined[:, pl.ds(column, HEAD_DIM)] = value


def back_kernel(info, *refs):
    pieces, (weight, out, joined) = refs[:6], refs[6:]
    join(info[0], pieces, joined)
    out[...] = dot_nt(joined[...], weight[...]).astype(BF)


def back_call(info, pieces, weights):
    rows = pieces[0].shape[2]
    width = 3 * 4 * HEAD_DIM
    piece = [
        pl.BlockSpec((parts, 1, TILE, HEAD_DIM), lambda i, info: (0, 0, i, 0))
        for parts in (3, 3, 2, 1, 2, 1)
    ]
    return pl.pallas_call(
        back_kernel,
        out_shape=jax.ShapeDtypeStruct((rows, D), BF),
        grid_spec=pltpu.PrefetchScalarGridSpec(
            num_scalar_prefetch=1,
            grid=(rows // TILE,),
            in_specs=piece + [pl.BlockSpec((D, width), lambda i, info: (0, 0))],
            out_specs=pl.BlockSpec((TILE, D), lambda i, info: (i, 0)),
            scratch_shapes=[pltpu.VMEM((TILE, width), BF)],
        ),
        compiler_params=params(VMEM),
        cost_estimate=cost(0, 0),
        name="back",
    )(info, *pieces, weights)


def attend_weight_kernel(info, normed, low, *refs):
    pieces, refs = refs[:6], refs[6:]
    attended, (keep, send, joined, out) = refs[:-4], refs[-4:]
    step = pl.program_id(0)

    @pl.when(step == 0)
    def _():
        join(info[0], pieces, joined)

    tile, width = normed.shape[1], joined.shape[1]
    left = normed[...].astype(F32).T.astype(BF)
    out[:, :width] = dot(left, joined[...]).astype(BF)
    left = low[...].astype(F32).T.astype(BF)
    out[:, width:] = dot(left, attended[0][...]).astype(BF)
    scatter(info, out, keep, send)


def attend_weight_call(info, normed, low, attended, pieces, size):
    rows, half = normed.shape[0], attended.shape[1]
    width = 3 * half
    total = width + half
    left = pl.BlockSpec((rows, TILE), lambda i, info: (0, i))
    piece = [
        pl.BlockSpec((parts, 1, rows, HEAD_DIM), lambda i, info: (0, 0, 0, 0))
        for parts in (3, 3, 2, 1, 2, 1)
    ]
    count = D // (4 * size)
    return pl.pallas_call(
        attend_weight_kernel,
        out_shape=(jax.ShapeDtypeStruct((2, count, size, total), BF),) * 2,
        grid_spec=pltpu.PrefetchScalarGridSpec(
            num_scalar_prefetch=1,
            grid=(D // TILE,),
            in_specs=[left, left]
            + piece
            + [pl.BlockSpec((rows, half), lambda i, info: (0, 0))],
            out_specs=(pl.BlockSpec((2, count, size, total), lambda i, info: (0, 0, 0, 0)),) * 2,
            scratch_shapes=[pltpu.VMEM((rows, width), BF), pltpu.VMEM((TILE, total), BF)],
        ),
        compiler_params=params(VMEM),
        cost_estimate=cost(0, 0),
        name="attend_weights",
    )(info, normed, low, *pieces, attended)


def input_kernel(grad, back_own, back_other, tokens, gain, out):
    value = tokens[...].astype(F32)
    back = back_own[...].astype(F32) + back_other[...].astype(F32)
    inverse = lax.rsqrt(jnp.mean(value * value, axis=1, keepdims=True) + EPS)
    scaled = gain[...] * back
    inner = jnp.mean(scaled * value, axis=1, keepdims=True)
    out[...] = (grad[...] + inverse * scaled - value * (inverse**3 * inner)).astype(BF)


def input_call(grad, back_own, back_other, tokens, gain):
    rows = tokens.shape[0]
    wide = pl.BlockSpec((TILE, D), lambda i: (i, 0))
    return pl.pallas_call(
        input_kernel,
        out_shape=jax.ShapeDtypeStruct((rows, D), BF),
        grid=(rows // TILE,),
        in_specs=[wide, wide, wide, wide, pl.BlockSpec((1, D), lambda i: (0, 0))],
        out_specs=wide,
        compiler_params=params(VMEM),
        cost_estimate=cost(12 * rows * D, 12 * MIB),
        name="input_grad",
    )(grad, back_own, back_other, tokens, gain)


def choose(line, options):
    value = options[0]
    for here in range(1, len(options)):
        if options[here] is not options[0]:
            value = jnp.where(line == here, options[here], value)
    return value


def pair_kernel(keep, core, *outs):
    half = keep.shape[1] // 2
    for part in range(2):
        slots = slice(part * half, (part + 1) * half)
        for column in range(2):
            outs[2 * part + column][...] = (
                keep[column, slots].astype(F32) + core[column, slots].astype(F32)
            ).astype(BF)


def pair_add(keep, core):
    count, size, width = keep.shape[1:]
    return pl.pallas_call(
        pair_kernel,
        out_shape=(jax.ShapeDtypeStruct((count // 2, size, width), BF),) * 4,
        compiler_params=pltpu.CompilerParams(vmem_limit_bytes=VMEM * MIB),
        cost_estimate=cost(0, 0),
        name="pair_add",
    )(keep, core)


def split_kernel(left_one, right_one, left_two, right_two, *outs):
    width = left_one.shape[2]
    for index, out in enumerate(outs):
        out[:, :width] = (left_one[index].astype(F32) + right_one[index].astype(F32)).astype(BF)
        out[:, width:] = (left_two[index].astype(F32) + right_two[index].astype(F32)).astype(BF)


def split_add(one, two):
    count, size, width = one[0].shape
    total = width + two[0].shape[2]
    return pl.pallas_call(
        split_kernel,
        out_shape=(jax.ShapeDtypeStruct((size, total), BF),) * count,
        compiler_params=pltpu.CompilerParams(vmem_limit_bytes=VMEM * MIB),
        cost_estimate=cost(0, 0),
        name="split_add",
    )(*one, *two)


def low_kernel(left, right, out):
    out[...] = (left[...].astype(F32) + right[...].astype(F32)).astype(out.dtype)


def low_add(left, right):
    return pl.pallas_call(
        low_kernel,
        out_shape=jax.ShapeDtypeStruct(left.shape, BF),
        compiler_params=pltpu.CompilerParams(vmem_limit_bytes=VMEM * MIB),
        cost_estimate=cost(0, 0),
        name="low_add",
    )(left, right)


def chosen_kernel(flags, first, second, up_in, down_in, up, down):
    one, two = first[...].astype(F32), second[...].astype(F32)
    up[...] = (jnp.where(flags[0] > 0, one, two) + up_in[...].astype(F32)).astype(BF)
    down[...] = (jnp.where(flags[1] > 0, one, two) + down_in[...].astype(F32)).astype(BF)


def chosen_add(flags, first, second, up_in, down_in):
    shape = jax.ShapeDtypeStruct(first.shape, BF)
    vmem = pl.BlockSpec(memory_space=pltpu.VMEM)
    return pl.pallas_call(
        chosen_kernel,
        out_shape=(shape, shape),
        in_specs=[pl.BlockSpec(memory_space=pltpu.SMEM)] + [vmem] * 4,
        out_specs=(vmem, vmem),
        compiler_params=pltpu.CompilerParams(vmem_limit_bytes=VMEM * MIB),
        cost_estimate=cost(0, 0),
        name="chosen_add",
    )(flags, first, second, up_in, down_in)


def reduce_rows(paired, count, first_wait, last_wait):
    length = count // 4
    line = lax.axis_index("dp") // 4
    pairs = [(i, i ^ 2) for i in range(count)]
    over = lambda value: lax.ppermute(value, "dp", pairs)
    (mine_one, theirs_one, mine_two, theirs_two), (down_one, far_one, down_two, far_two) = paired
    others, first_wait = pin(((over(theirs_one), over(far_one)), first_wait))
    sums = list(split_add((mine_one, others[0]), (down_one, others[1])))
    others = (over(theirs_two), over(far_two))
    above = below = None
    for step in range(1, length):
        gap = length - step
        slots = lambda towards: [
            length - 1 - (here ^ (here + towards)) if 0 <= here + towards < length else None
            for here in range(length)
        ]
        ups, downs = slots(gap), slots(-gap)
        used = sorted({slot for slot in ups + downs if slot is not None})
        if len(used) == 1 and step == 1:
            up = down = sums[used[0]]
        elif len(used) == 1:
            up, down = low_add(sums[used[0]], below), low_add(sums[used[0]], above)
        elif len(used) == 2:
            flags = jnp.stack(
                [
                    choose(line, [jnp.int32(slot == used[0]) for slot in side])
                    for side in (ups, downs)
                ]
            )
            up, down = chosen_add(flags, sums[used[0]], sums[used[1]], below, above)
        else:
            fill = lambda side: [sums[used[0] if slot is None else slot] for slot in side]
            up, down = choose(line, fill(ups)), choose(line, fill(downs))
            up, down = low_add(up, below), low_add(down, above)
        if step == length - 1:
            up, down, last_wait = pin((up, down, last_wait))
        below = lax.ppermute(up, "dp", [(i, i + 4) for i in range(count - 4) if i // 4 + gap < length])
        above = lax.ppermute(down, "dp", [(i, i - 4) for i in range(4, count) if i // 4 >= gap])
        if step == length // 2 - 1:
            below, above, others = pin((below, above, others))
            sums += split_add((mine_two, others[0]), (down_two, others[1]))
    return sums[-1], below, above, first_wait, last_wait


def interleave_kernel(info, *refs):
    pieces, out = refs[:4], refs[4]
    size = out.shape[0] // (4 * pieces[0].shape[0])
    length = pieces[0].shape[0]
    for index, piece in enumerate(pieces):
        side = info[3] if index % 2 == 0 else 1 - info[3]
        core = info[0] if index // 2 == 0 else 1 - info[0]
        for line in range(length):
            start = pl.multiple_of((line * 4 + side * 2 + core) * size, size)
            out[pl.ds(start, size), :] = piece[line]


def interleave(info, pieces, size):
    width = pieces[0].shape[1]
    pieces = [piece.reshape(-1, size, width) for piece in pieces]
    vmem = pl.BlockSpec(memory_space=pltpu.VMEM)
    return pl.pallas_call(
        interleave_kernel,
        out_shape=pltpu.VMEM((D, width), BF),
        in_specs=[pl.BlockSpec(memory_space=pltpu.SMEM)] + [vmem] * 4,
        out_specs=vmem,
        compiler_params=pltpu.CompilerParams(vmem_limit_bytes=VMEM * MIB),
        cost_estimate=cost(0, 0),
        name="interleave",
    )(info, *pieces)


def gain_kernel(own, other, gain, first, second, first_out, second_out, gain_out):
    low = gain[...].astype(BF).astype(F32)
    results = adamw(gain[...], (own[...] + other[...]) / low, first[...], second[...], 0.6)
    for out, result in zip((first_out, second_out, gain_out), results):
        out[...] = result


def gain_call(own, other, gain, first, second):
    shape = jax.ShapeDtypeStruct(gain.shape, F32)
    return pl.pallas_call(
        gain_kernel,
        out_shape=(shape, shape, shape),
        compiler_params=pltpu.CompilerParams(vmem_limit_bytes=VMEM * MIB),
        cost_estimate=cost(0, 0),
        name="gains",
    )(own, other, gain, first, second)


def shard_kernel(qkv, gains, out):
    width = qkv.shape[2]
    for part in range(3):
        out[:, part * width : (part + 1) * width] = qkv[part].astype(BF)
    rows = jnp.concatenate([gains[...], jnp.zeros((HEAD_DIM - 2, gains.shape[1]), F32)])
    out[:, 3 * width :] = rows.T.astype(BF)


def shard_call(qkv, gains):
    total = 3 * qkv.shape[2] + HEAD_DIM
    return pl.pallas_call(
        shard_kernel,
        out_shape=jax.ShapeDtypeStruct((qkv.shape[1], total), BF),
        compiler_params=pltpu.CompilerParams(vmem_limit_bytes=VMEM * MIB),
        cost_estimate=cost(0, 0),
        name="shard",
    )(qkv, gains)


def pin(values):
    return lax.optimization_barrier(values)


def body(
    tokens,
    cotangent,
    proj_qkv,
    proj_out,
    proj_gate_up,
    proj_down,
    norm_gains,
    first_qkv,
    first_out,
    first_gate_up,
    first_down,
    first_gains,
    second_qkv,
    second_out,
    second_gate_up,
    second_down,
    second_gains,
    cache,
    doc_segments,
    padding,
    retrieval,
):
    rows = tokens.shape[0]
    count = lax.axis_size("dp")
    device = lax.axis_index("dp")
    group = lax.axis_index("mp")
    rank = device % 2
    segment = device // 2
    shard = proj_qkv.shape[1]
    local = proj_qkv.shape[2]
    hidden_here = proj_gate_up.shape[2]
    core_pairs = [(i, i ^ 1) for i in range(count)]

    def across(value):
        return lax.ppermute(value, "mp", [(0, 1), (1, 0)])

    def beside(value):
        return lax.ppermute(value, "dp", core_pairs)

    shard_one = shard_call(proj_qkv, norm_gains)
    out_own = proj_out.astype(BF).T
    out_other = across(out_own)
    shard_two = jnp.concatenate(
        [
            proj_gate_up[0].astype(BF),
            proj_gate_up[1].astype(BF),
            proj_down.astype(BF).T,
            jnp.where(group == 0, out_own, out_other),
            jnp.where(group == 0, out_other, out_own),
        ],
        axis=1,
    )
    length = count // 4
    lines = [[i for i in range(count) if i % 4 == lane] for lane in range(4)]
    own_column = lax.all_gather(shard_one, "dp", axis=0, tiled=True, axis_index_groups=lines)
    next_column = lax.ppermute(own_column, "dp", [(i, i ^ 2) for i in range(count)])
    pieces = (own_column, next_column, beside(own_column), beside(next_column))
    weights_two = lax.all_gather(shard_two, "dp", axis=0, tiled=True)

    places = jnp.arange(SEG, dtype=jnp.int32)
    starts = jnp.cumsum(doc_segments) - doc_segments
    memory_on = jnp.logical_not(jnp.any(starts == segment))
    side = (device // 2) % 2
    info = jnp.stack([rank, group, memory_on.astype(jnp.int32), side, device // 4]).astype(jnp.int32)
    cosines, sines = rope_tables(places)
    valid = lax.dynamic_slice_in_dim(padding, segment * SEG, SEG)
    lane = jnp.arange(HEAD_DIM, dtype=jnp.int32)[None, :]
    bias = jnp.where((valid[:, None] == 0) & (lane == 0), NEGATIVE, 0.0).astype(BF)
    fetched = cache[retrieval[0]].reshape(RETR, 2, 2, 2, HEAD_DIM).transpose(2, 1, 3, 0, 4)
    mem_own = lax.dynamic_index_in_dim(fetched, rank, keepdims=False)
    mem_other = beside(lax.dynamic_index_in_dim(fetched, 1 - rank, keepdims=False))
    pieces, mem_own, mem_other, bias, cosines, sines, info = pin(
        (pieces, mem_own, mem_other, bias, cosines, sines, info)
    )
    weights_one = interleave(info, pieces, shard)

    send, normed_one, gains = project_first(info, tokens, weights_one, cosines, sines)
    gain_one, gain_two = gains[0:1], gains[1:2]
    other = beside(send)
    own = project_second(info, normed_one, weights_one, cosines, sines)
    out_keep, out_send, turned, logs = attend_forward(info, own, other, mem_own, mem_other, bias)
    out_recv = beside(out_send)
    pieces = (out_keep, out_recv, across(out_keep), across(out_recv))
    middle, normed_two, attended = middle_call(info, pieces, tokens, weights_two, gain_two)

    earlier, backs, backs_other = (), [], []
    for chunk, first in enumerate(range(0, rows, TILE)):
        if first + TILE == rows:
            earlier, backs_other[0] = pin((earlier, backs_other[0]))
        *earlier, back = feed_call(normed_two, cotangent, weights_two, first, TILE, earlier)
        backs.append(back)
        backs_other.append(across(back))
    hidden, grad_gate, grad_up, feed_part = earlier
    feed_grads, down_keep, down_send = feed_weight_call(
        info, normed_two, cotangent, hidden, grad_gate, grad_up, shard
    )
    feed_other = across(feed_part)
    backs[0], _ = pin((backs[0], feed_grads))
    earlier = ()
    for chunks in ((0, 1), (2,), (3,)):
        earlier = residual_call(
            info, middle, [backs[index] for index in chunks], [backs_other[index] for index in chunks],
            cotangent, gain_two, weights_two, chunks[0], earlier,
        )
    grad_middle, grad_low, grad_keep, *grad_sends = earlier
    grad_others = [beside(value) for value in grad_sends]

    d_keeps, d_others = [], []
    for head in range(2):
        d_keep, d_send, d_send_v = attend_backward(
            info, own, other, mem_own, mem_other, bias, grad_keep, grad_others[head], turned, logs,
            cosines, sines, head,
        )
        d_keeps.append(d_keep)
        d_others += [beside(d_send), beside(d_send_v)]
    moved = d_keeps + d_others
    back_one = back_call(info, moved, weights_one)
    moved[0], _ = pin((moved[0], back_one))
    attend_keep, attend_send = attend_weight_call(info, normed_one, grad_low, attended, moved, shard)
    back_one, feed_other = pin((back_one, feed_other))
    back_one_other = across(back_one)
    input_grad = input_call(grad_middle, back_one, back_one_other, tokens, gain_one)
    block_out = (
        middle + (feed_part.astype(F32) + feed_other.astype(F32))
    ).astype(BF)
    paired = [
        pair_add(keep, beside(send))
        for keep, send in ((attend_keep, attend_send), (down_keep, down_send))
    ]
    total, below, above, block_out, input_grad = reduce_rows(paired, count, block_out, input_grad)
    feed_sum = lax.psum_scatter(feed_grads, "dp", scatter_dimension=0, tiled=True).astype(F32)
    gate_up_sum = jnp.stack([feed_sum[:, :hidden_here], feed_sum[:, hidden_here : 2 * hidden_here]])
    gate_up_first, gate_up_second, gate_up_new = adamw(
        proj_gate_up, gate_up_sum, first_gate_up, second_gate_up, 0.5 / math.sqrt(D)
    )
    gate_up_new, total, below, above = pin((gate_up_new, total, below, above))
    attend_sum = total.astype(F32) + (below.astype(F32) + above.astype(F32))
    down_sum = jnp.concatenate([feed_sum[:, 2 * hidden_here :].T, attend_sum[:, 4 * local :].T])
    down_first, down_second, down_new = adamw(
        proj_down, down_sum, first_down, second_down, 0.5 / math.sqrt(FF)
    )
    qkv_sum = jnp.stack([attend_sum[:, part * local : (part + 1) * local] for part in range(3)])
    out_sum = attend_sum[:, 3 * local : 4 * local].T
    low_qkv, low_gate_up = proj_qkv.astype(BF).astype(F32), proj_gate_up.astype(BF).astype(F32)
    gains_sum = jnp.stack(
        [jnp.sum(low_qkv * qkv_sum, axis=(0, 2)), jnp.sum(low_gate_up * gate_up_sum, axis=(0, 2))]
    )
    gains_first, gains_second, gains_new = gain_call(
        gains_sum, across(gains_sum), norm_gains, first_gains, second_gains
    )

    qkv_first, qkv_second, qkv_new = adamw(
        proj_qkv, qkv_sum, first_qkv, second_qkv, 0.5 / math.sqrt(D)
    )
    out_first, out_second, out_new = adamw(
        proj_out, out_sum, first_out, second_out, 0.5 / math.sqrt(max(1, 4 * D // SEG))
    )
    return (
        block_out,
        input_grad,
        qkv_first,
        qkv_second,
        qkv_new,
        out_first,
        out_second,
        out_new,
        gate_up_first,
        gate_up_second,
        gate_up_new,
        down_first,
        down_second,
        down_new,
        gains_first,
        gains_second,
        gains_new,
    )


def solution(mesh):
    return jax.shard_map(
        body,
        mesh=mesh,
        in_specs=(
            P("dp", None),
            P("dp", None),
            P(None, "dp", "mp"),
            P("mp", "dp"),
            P(None, "dp", "mp"),
            P("mp", "dp"),
            P(None, "dp"),
            P(None, "dp", "mp"),
            P("mp", "dp"),
            P(None, "dp", "mp"),
            P("mp", "dp"),
            P(None, "dp"),
            P(None, "dp", "mp"),
            P("mp", "dp"),
            P(None, "dp", "mp"),
            P("mp", "dp"),
            P(None, "dp"),
            P("dp", None, "mp"),
            P(),
            P(),
            P("dp", None),
        ),
        out_specs=(
            P("dp", None),
            P("dp", None),
            P(None, "dp", "mp"),
            P(None, "dp", "mp"),
            P(None, "dp", "mp"),
            P("mp", "dp"),
            P("mp", "dp"),
            P("mp", "dp"),
            P(None, "dp", "mp"),
            P(None, "dp", "mp"),
            P(None, "dp", "mp"),
            P("mp", "dp"),
            P("mp", "dp"),
            P("mp", "dp"),
            P(None, "dp"),
            P(None, "dp"),
            P(None, "dp"),
        ),
        check_vma=False,
    )
```

```python
import functools
import math

import jax
import jax.numpy as jnp
from jax import lax
from jax.experimental import pallas as pl
from jax.experimental.pallas import tpu as pltpu
from jax.sharding import PartitionSpec as P

D = 1024
HEAD_DIM = 128
FF = 2816
SEG = 2048
RETR = 128
STEP = 10

EPS = 1e-05
BETA_ONE = 0.9
BETA_TWO = 0.95
ADAM_EPS = 1e-08
DECAY = 0.1
NEGATIVE = -1e30
SCALE = HEAD_DIM**-0.5
SCALE_TWO = SCALE * math.log2(math.e)

BF = jnp.bfloat16
F32 = jnp.float32
MIB = 1024 * 1024
TILE = 256
VMEM = 26
WEIGH = 1.0


def dot(left, right):
    return jnp.dot(left, right, preferred_element_type=F32)


def dot_nt(left, right):
    return lax.dot_general(left, right, (((1,), (1,)), ((), ())), preferred_element_type=F32)


def dot_tn(left, right):
    return lax.dot_general(left, right, (((0,), (0,)), ((), ())), preferred_element_type=F32)


def params(mib, axes=1):
    return pltpu.CompilerParams(
        dimension_semantics=("arbitrary",) * axes, vmem_limit_bytes=mib * MIB
    )


def cost(flops, moved, trans=0):
    return pl.CostEstimate(flops=int(flops * WEIGH), bytes_accessed=int(moved * WEIGH), transcendentals=int(trans))


def rope_tables(places):
    half_dim = HEAD_DIM // 2
    freqs = 10000.0 ** (-(jnp.arange(half_dim, dtype=F32) / half_dim))
    phase = places.astype(F32)[:, None] * freqs[None, :]
    cosines, sines = jnp.cos(phase), jnp.sin(phase)
    return jnp.concatenate([cosines, cosines], 1), jnp.concatenate([-sines, sines], 1)


def turn(value, cosines, sines):
    return value * cosines + pltpu.roll(value, HEAD_DIM // 2, 1) * sines


def adamw(weight, grad, first, second, rate):
    first_new = BETA_ONE * first + (1.0 - BETA_ONE) * grad
    second_new = BETA_TWO * second + (1.0 - BETA_TWO) * grad * grad
    first_hat = first_new / (1.0 - BETA_ONE**STEP)
    second_hat = second_new / (1.0 - BETA_TWO**STEP)
    updated = weight - rate * (first_hat / (jnp.sqrt(second_hat) + ADAM_EPS) + DECAY * weight)
    return (first_new, second_new, updated)


def rotate_out(result, part, cosines, sines, out):
    for head in range(2):
        value = result[:, head * HEAD_DIM : (head + 1) * HEAD_DIM]

        @pl.when(part < 2)
        def _():
            out[0, head] = turn(value, cosines[...], sines[...]).astype(BF)

        @pl.when(part == 2)
        def _():
            out[0, head] = value.astype(BF)


def first_kernel(info, tokens, gain_columns, weight, cosines, sines, out, normed, gains):
    part = pl.program_id(0)

    @pl.when(part == 0)
    def _():
        rows = gain_columns[...].astype(F32).T[:8, :]
        gains[...] = rows
        value = tokens[...].astype(F32)
        inverse = lax.rsqrt(jnp.mean(value * value, axis=1, keepdims=True) + EPS)
        normed[...] = (value * inverse * rows[0:1, :]).astype(BF)

    rotate_out(dot(normed[...], weight[...]), part, cosines, sines, out)


def second_kernel(info, normed, weight, cosines, sines, out):
    rotate_out(dot(normed[...], weight[...]), pl.program_id(0), cosines, sines, out)


def project_first(info, tokens, weights, cosines, sines):
    rows = tokens.shape[0]
    return pl.pallas_call(
        first_kernel,
        out_shape=(
            jax.ShapeDtypeStruct((3, 2, rows, HEAD_DIM), BF),
            jax.ShapeDtypeStruct((rows, D), BF),
            jax.ShapeDtypeStruct((8, D), F32),
        ),
        grid_spec=pltpu.PrefetchScalarGridSpec(
            num_scalar_prefetch=1,
            grid=(3,),
            in_specs=[
                pl.BlockSpec((rows, D), lambda j, info: (0, 0)),
                pl.BlockSpec((D, HEAD_DIM), lambda j, info: (0, 12)),
                pl.BlockSpec((D, 256), lambda j, info: (0, 2 * j + 1 - info[0])),
                pl.BlockSpec((rows, HEAD_DIM), lambda j, info: (info[0], 0)),
                pl.BlockSpec((rows, HEAD_DIM), lambda j, info: (info[0], 0)),
            ],
            out_specs=(
                pl.BlockSpec((1, 2, rows, HEAD_DIM), lambda j, info: (j, 0, 0, 0)),
                pl.BlockSpec((rows, D), lambda j, info: (0, 0)),
                pl.BlockSpec((8, D), lambda j, info: (0, 0)),
            ),
        ),
        compiler_params=params(VMEM),
        cost_estimate=cost(0, 0),
        name="project_first",
    )(info, tokens, weights, weights, cosines, sines)


def project_second(info, normed, weights, cosines, sines):
    rows = normed.shape[0]
    return pl.pallas_call(
        second_kernel,
        out_shape=pltpu.HBM((3, 2, rows, HEAD_DIM), BF),
        grid_spec=pltpu.PrefetchScalarGridSpec(
            num_scalar_prefetch=1,
            grid=(3,),
            in_specs=[
                pl.BlockSpec((rows, D), lambda j, info: (0, 0)),
                pl.BlockSpec((D, 256), lambda j, info: (0, 2 * j + info[0])),
                pl.BlockSpec((rows, HEAD_DIM), lambda j, info: (info[0], 0)),
                pl.BlockSpec((rows, HEAD_DIM), lambda j, info: (info[0], 0)),
            ],
            out_specs=pl.BlockSpec((1, 2, rows, HEAD_DIM), lambda j, info: (j, 0, 0, 0)),
        ),
        compiler_params=params(VMEM),
        cost_estimate=cost(0, 0),
        name="project_second",
    )(info, normed, weights, cosines, sines)


def place(scratch, own, other, rank, rows):
    scratch[pl.ds(pl.multiple_of(rank * rows, rows), rows), :] = own
    scratch[pl.ds(pl.multiple_of((1 - rank) * rows, rows), rows), :] = other


def chunks_of(tile, step):
    end = tile * TILE
    spans = [(start, min(step, end - start)) for start in range(0, end, step)]
    return spans + [(end, TILE)]


def causal(scores):
    rows = lax.broadcasted_iota(jnp.int32, scores.shape, 0)
    columns = lax.broadcasted_iota(jnp.int32, scores.shape, 1)
    return jnp.where(rows <= columns, scores, NEGATIVE)


def forward_kernel(
    info, own, other, mem_own, mem_other, bias, keep, send, turned, logs,
    q_s, k_s, v_s, vt_s, mem_s, s_s, out_s,
):
    rank = info[0]
    rows = own.shape[2]
    mem_bias = jnp.where(info[2] > 0, 0.0, NEGATIVE).astype(F32)
    place(q_s, own[0, 0], other[0, 0], rank, rows)
    place(k_s, own[1, 0], other[1, 0], rank, rows)
    place(v_s, own[2, 0], other[2, 0], rank, rows)
    mem_s[rank] = mem_own[:, 0]
    mem_s[1 - rank] = mem_other[:, 0]
    vt_s[...] = v_s[...].astype(F32).T.astype(BF)
    ones = (lax.broadcasted_iota(jnp.int32, (TILE, HEAD_DIM), 1) == 0).astype(BF)
    for tile in range(SEG // TILE):
        here = slice(tile * TILE, (tile + 1) * TILE)
        block = tile * TILE // rows
        query = q_s[here, :]
        wide = jnp.concatenate([query, ones], axis=1)
        spans = chunks_of(tile, 512)
        scores = dot_nt(mem_s[block, 0], query) + mem_bias
        s_s[SEG : SEG + RETR, :] = scores
        top = jnp.max(scores, axis=0, keepdims=True)
        for start, size in spans:
            span = slice(start, start + size)
            if start + size > SEG // 2:
                scores = dot_nt(jnp.concatenate([k_s[span, :], bias[span, :]], axis=1), wide)
            else:
                scores = dot_nt(k_s[span, :], query)
            if start == tile * TILE:
                scores = causal(scores)
            s_s[span, :] = scores
            top = jnp.maximum(top, jnp.max(scores, axis=0, keepdims=True))
        shift = top * SCALE_TWO
        exponent = jnp.exp2(s_s[SEG : SEG + RETR, :] * SCALE_TWO - shift)
        total = jnp.sum(exponent, axis=0, keepdims=True)
        result = dot(mem_s[block, 1].astype(F32).T.astype(BF), exponent.astype(BF))
        for start, size in spans:
            span = slice(start, start + size)
            exponent = jnp.exp2(s_s[span, :] * SCALE_TWO - shift)
            total = total + jnp.sum(exponent, axis=0, keepdims=True)
            result = result + dot(vt_s[:, span], exponent.astype(BF))
        result = result * (1.0 / total)
        turned[0, :, here] = result
        logs[0, :, here] = shift + jnp.log2(total)
        out_s[here, :] = result.T.astype(BF)
    keep[0] = out_s[pl.ds(pl.multiple_of(rank * rows, rows), rows), :]
    send[0] = out_s[pl.ds(pl.multiple_of((1 - rank) * rows, rows), rows), :]


def attend_forward(info, own, other, mem_own, mem_other, bias):
    rows = own.shape[2]
    part = pl.BlockSpec((3, 1, rows, HEAD_DIM), lambda h, info: (0, h, 0, 0))
    mem = pl.BlockSpec((2, 1, RETR, HEAD_DIM), lambda h, info: (0, h, 0, 0))
    half = pl.BlockSpec((1, rows, HEAD_DIM), lambda h, info: (h, 0, 0))
    return pl.pallas_call(
        forward_kernel,
        out_shape=(
            jax.ShapeDtypeStruct((2, rows, HEAD_DIM), BF),
            jax.ShapeDtypeStruct((2, rows, HEAD_DIM), BF),
            pltpu.HBM((2, HEAD_DIM, SEG), F32),
            jax.ShapeDtypeStruct((2, 1, SEG), F32),
        ),
        grid_spec=pltpu.PrefetchScalarGridSpec(
            num_scalar_prefetch=1,
            grid=(2,),
            in_specs=[
                part,
                part,
                mem,
                mem,
                pl.BlockSpec((SEG, HEAD_DIM), lambda h, info: (0, 0)),
            ],
            out_specs=(
                half,
                half,
                pl.BlockSpec((1, HEAD_DIM, SEG), lambda h, info: (h, 0, 0)),
                pl.BlockSpec((1, 1, SEG), lambda h, info: (h, 0, 0)),
            ),
            scratch_shapes=[
                pltpu.VMEM((SEG, HEAD_DIM), BF),
                pltpu.VMEM((SEG, HEAD_DIM), BF),
                pltpu.VMEM((SEG, HEAD_DIM), BF),
                pltpu.VMEM((HEAD_DIM, SEG), BF),
                pltpu.VMEM((2, 2, RETR, HEAD_DIM), BF),
                pltpu.VMEM((SEG + RETR, TILE), F32),
                pltpu.VMEM((SEG, HEAD_DIM), BF),
            ],
        ),
        compiler_params=params(VMEM),
        cost_estimate=cost(0, 0),
        name="attend_forward",
    )(info, own, other, mem_own, mem_other, bias)


def backward_kernel(
    info, own, other, mem_own, mem_other, bias, grad_own, grad_other, turned, logs, cosines, sines,
    keep, send, send_v,
    q_s, k_s, v_s, g_s, kt_s, mem_s, dots_s, dq_s, dk_s, dv_s,
):
    rank = info[0]
    rows = own.shape[2]
    mem_bias = jnp.where(info[2] > 0, 0.0, NEGATIVE).astype(F32)
    place(q_s, own[0, 0], other[0, 0], rank, rows)
    place(k_s, own[1, 0], other[1, 0], rank, rows)
    place(v_s, own[2, 0], other[2, 0], rank, rows)
    place(g_s, grad_own[0], grad_other[0], rank, rows)
    mem_s[rank] = mem_own[:, 0]
    mem_s[1 - rank] = mem_other[:, 0]
    kt_s[...] = k_s[...].astype(F32).T.astype(BF)
    dots_s[...] = jnp.sum(g_s[...].astype(F32).T * turned[0], axis=0, keepdims=True)
    dk_s[...] = jnp.zeros_like(dk_s)
    dv_s[...] = jnp.zeros_like(dv_s)
    ones = (lax.broadcasted_iota(jnp.int32, (TILE, HEAD_DIM), 1) == 0).astype(BF)
    for tile in range(SEG // TILE):
        here = slice(tile * TILE, (tile + 1) * TILE)
        block = tile * TILE // rows
        query = q_s[here, :]
        wide = jnp.concatenate([query, ones], axis=1)
        grad = g_s[here, :]
        log = logs[0, :, here]
        dots = dots_s[:, here]
        scores = dot_nt(mem_s[block, 0], query) + mem_bias
        probs = jnp.exp2(scores * SCALE_TWO - log)
        change = (probs * (dot_nt(mem_s[block, 1], grad) - dots)).astype(BF)
        result = dot(mem_s[block, 0].astype(F32).T.astype(BF), change)
        for start, size in chunks_of(tile, 512):
            span = slice(start, start + size)
            keys = k_s[span, :]
            if start + size > SEG // 2:
                scores = dot_nt(jnp.concatenate([keys, bias[span, :]], axis=1), wide)
            else:
                scores = dot_nt(keys, query)
            if start == tile * TILE:
                scores = causal(scores)
            probs = jnp.exp2(scores * SCALE_TWO - log)
            change = (probs * (dot_nt(v_s[span, :], grad) - dots)).astype(BF)
            dv_s[span, :] += dot(probs.astype(BF), grad)
            dk_s[span, :] += dot(change, query)
            result = result + dot(kt_s[:, span], change)
        dq_s[here, :] = turn(result.T * SCALE, cosines[here, :], -sines[here, :]).astype(BF)
    for outs, place_ in (((keep.at[0], keep.at[1], keep.at[2]), rank), ((send.at[0], send.at[1], send_v.at[0]), 1 - rank)):
        held = pl.ds(pl.multiple_of(place_ * rows, rows), rows)
        outs[0][0] = dq_s[held, :]
        outs[1][0] = turn(dk_s[held, :] * SCALE, cosines[held, :], -sines[held, :]).astype(BF)
        outs[2][0] = dv_s[held, :].astype(BF)


def attend_backward(
    info, own, other, mem_own, mem_other, bias, grad_own, grad_other, turned, logs, cosines, sines, head
):
    rows = own.shape[2]
    part = pl.BlockSpec((3, 1, rows, HEAD_DIM), lambda h, info: (0, head, 0, 0))
    mem = pl.BlockSpec((2, 1, RETR, HEAD_DIM), lambda h, info: (0, head, 0, 0))
    half = pl.BlockSpec((1, rows, HEAD_DIM), lambda h, info: (head, 0, 0))
    table = pl.BlockSpec((SEG, HEAD_DIM), lambda h, info: (0, 0))
    return pl.pallas_call(
        backward_kernel,
        out_shape=tuple(jax.ShapeDtypeStruct((parts, 1, rows, HEAD_DIM), BF) for parts in (3, 2, 1)),
        grid_spec=pltpu.PrefetchScalarGridSpec(
            num_scalar_prefetch=1,
            grid=(1,),
            in_specs=[
                part,
                part,
                mem,
                mem,
                table,
                half,
                pl.BlockSpec((1, rows, HEAD_DIM), lambda h, info: (0, 0, 0)),
                pl.BlockSpec((1, HEAD_DIM, SEG), lambda h, info: (head, 0, 0)),
                pl.BlockSpec((1, 1, SEG), lambda h, info: (head, 0, 0)),
                table,
                table,
            ],
            out_specs=tuple(
                pl.BlockSpec((parts, 1, rows, HEAD_DIM), lambda h, info: (0, 0, 0, 0)) for parts in (3, 2, 1)
            ),
            scratch_shapes=[pltpu.VMEM((SEG, HEAD_DIM), BF)] * 4
            + [
                pltpu.VMEM((HEAD_DIM, SEG), BF),
                pltpu.VMEM((2, 2, RETR, HEAD_DIM), BF),
                pltpu.VMEM((1, SEG), F32),
                pltpu.VMEM((SEG, HEAD_DIM), BF),
                pltpu.VMEM((SEG, HEAD_DIM), F32),
                pltpu.VMEM((SEG, HEAD_DIM), F32),
            ],
        ),
        compiler_params=params(VMEM),
        cost_estimate=cost(0, 0),
        name="attend_backward",
    )(
        info, own, other, mem_own, mem_other, bias, grad_own, grad_other, turned, logs, cosines, sines
    )


OUT_AT = 3 * FF // 2


def in_hbm(value):
    return pltpu.with_memory_space_constraint(value, pltpu.HBM)


def columns(width, start):
    return pl.BlockSpec(
        (pl.Element(D), pl.Element(width)), start, pipeline_mode=pl.Buffered(1)
    )


def middle_kernel(info, *refs):
    pieces, (tokens, weight, gain, middle, normed, attended, joined) = refs[:4], refs[4:]
    rank, group = info[0], info[1]
    for index, piece in enumerate(pieces):
        side = (group, 1 - group)[index // 2]
        pair = (rank, 1 - rank)[index % 2]
        for head in range(2):
            column = pl.multiple_of((side * 4 + pair * 2 + head) * HEAD_DIM, HEAD_DIM)
            joined[:, pl.ds(column, HEAD_DIM)] = piece[head]
    half = attended.shape[1]
    attended[...] = joined[:, pl.ds(pl.multiple_of(group * half, half), half)]
    value = tokens[...].astype(F32) + dot_nt(joined[...], weight[...])
    middle[...] = value
    inverse = lax.rsqrt(jnp.mean(value * value, axis=1, keepdims=True) + EPS)
    normed[...] = (value * inverse * gain[...]).astype(BF)


def middle_call(info, pieces, tokens, weights, gain):
    rows, half = tokens.shape[0], 4 * HEAD_DIM
    piece = pl.BlockSpec((2, TILE, HEAD_DIM), lambda i, info: (0, i, 0))
    wide = pl.BlockSpec((TILE, D), lambda i, info: (i, 0))
    return pl.pallas_call(
        middle_kernel,
        out_shape=(
            pltpu.HBM((rows, D), F32),
            jax.ShapeDtypeStruct((rows, D), BF),
            pltpu.HBM((rows, half), BF),
        ),
        grid_spec=pltpu.PrefetchScalarGridSpec(
            num_scalar_prefetch=1,
            grid=(rows // TILE,),
            in_specs=[piece] * 4
            + [
                wide,
                columns(D, lambda i, info: (0, OUT_AT)),
                pl.BlockSpec((1, D), lambda i, info: (0, 0)),
            ],
            out_specs=(wide, wide, pl.BlockSpec((TILE, half), lambda i, info: (i, 0))),
            scratch_shapes=[pltpu.VMEM((TILE, D), BF)],
        ),
        compiler_params=params(VMEM),
        cost_estimate=cost(0, 0),
        name="middle",
    )(info, *[in_hbm(piece) for piece in pieces], in_hbm(tokens), in_hbm(weights), gain)


def feed_kernel(normed, upstream, gate_w, up_w, down_w, *refs):
    hidden, gate_grad, up_grad, feed, back = refs[-5:]
    gate = dot(normed[...], gate_w[...])
    up_part = dot(normed[...], up_w[...])
    sigma = jax.nn.sigmoid(gate)
    silu = gate * sigma
    low = (silu * up_part).astype(BF)
    hidden[...] = low
    feed[...] = dot_nt(low, down_w[...]).astype(BF)
    grad = dot(upstream[...], down_w[...])
    grad_gate = (grad * up_part * sigma * (1.0 + gate * (1.0 - sigma))).astype(BF)
    grad_up = (grad * silu).astype(BF)
    gate_grad[...] = grad_gate
    up_grad[...] = grad_up
    back[...] = (dot_nt(grad_gate, gate_w[...]) + dot_nt(grad_up, up_w[...])).astype(BF)


def feed_call(normed, upstream, weights, first, count, earlier):
    rows = upstream.shape[0]
    width = FF // 2
    whole = lambda index: pl.BlockSpec((D, width), lambda i: (0, index), pipeline_mode=pl.Buffered(1))
    source = pl.BlockSpec((TILE, D), lambda i: (i + first // TILE, 0))
    narrow = pl.BlockSpec((TILE, width), lambda i: (i + first // TILE, 0))
    return pl.pallas_call(
        feed_kernel,
        out_shape=(pltpu.VMEM((rows, width), BF),) * 3
        + (jax.ShapeDtypeStruct((rows, D), BF), jax.ShapeDtypeStruct((count, D), BF)),
        grid=(count // TILE,),
        in_specs=[source, source, whole(0), whole(1), whole(2)]
        + [pl.BlockSpec(memory_space=pl.ANY)] * len(earlier),
        out_specs=(narrow, narrow, narrow, source, pl.BlockSpec((TILE, D), lambda i: (i, 0))),
        input_output_aliases={5 + index: index for index in range(len(earlier))},
        compiler_params=params(VMEM),
        cost_estimate=cost(5e7, 0),
        name="feed",
    )(normed, upstream, weights, weights, weights, *earlier)


DOWN_SPLIT = 1024


def scatter(info, out, keep, send):
    step, tile = pl.program_id(0), out.shape[0]
    count, size = keep.shape[1], keep.shape[2]
    for line in range(tile // (4 * size)):
        slot = count - 1 - ((step * (tile // (4 * size)) + line) ^ info[4])
        for column in range(2):
            for target, core in ((keep, info[0]), (send, 1 - info[0])):
                side = info[3] if column == 0 else 1 - info[3]
                start = pl.multiple_of((line * 4 + side * 2 + core) * size, size)
                target[column, slot] = out[pl.ds(start, size), :]


def feed_weight_kernel(info, normed, upstream, hidden, gate_grad, up_grad, out, keep, send, last):
    width = gate_grad.shape[1]
    left = normed[...].astype(F32).T.astype(BF)
    out[:, :width] = dot(left, gate_grad[...]).astype(BF)
    out[:, width : 2 * width] = dot(left, up_grad[...]).astype(BF)
    left = upstream[...].astype(F32).T.astype(BF)
    result = dot(left, hidden[...]).astype(BF)
    out[:, 2 * width :] = result[:, :DOWN_SPLIT]
    last[...] = result[:, DOWN_SPLIT:]
    scatter(info, last, keep, send)


def feed_weight_call(info, normed, upstream, hidden, gate_grad, up_grad, size):
    rows, width = gate_grad.shape
    total, rest, count = 2 * width + DOWN_SPLIT, width - DOWN_SPLIT, D // (4 * size)
    left = pl.BlockSpec((rows, TILE), lambda i, info: (0, i))
    whole = pl.BlockSpec((rows, width), lambda i, info: (0, 0), pipeline_mode=pl.Buffered(1))
    return pl.pallas_call(
        feed_weight_kernel,
        out_shape=(pltpu.HBM((D, total), BF),)
        + (jax.ShapeDtypeStruct((2, count, size, rest), BF),) * 2,
        grid_spec=pltpu.PrefetchScalarGridSpec(
            num_scalar_prefetch=1,
            grid=(D // TILE,),
            in_specs=[left, left, whole, whole, whole],
            out_specs=(pl.BlockSpec((TILE, total), lambda i, info: (i, 0)),)
            + (pl.BlockSpec((2, count, size, rest), lambda i, info: (0, 0, 0, 0)),) * 2,
            scratch_shapes=[pltpu.VMEM((TILE, rest), BF)],
        ),
        compiler_params=params(24),
        cost_estimate=cost(5e7, 0),
        name="feed_weights",
    )(info, normed, in_hbm(upstream), hidden, gate_grad, up_grad)


def residual_kernel(count, info, middle, upstream, gain, weight, *refs):
    grad, low, keep, send_one, send_two, back_s = refs[-6:]
    rank = info[0]
    for index in range(count):

        @pl.when(pl.program_id(0) == index)
        def _():
            back_s[...] = refs[index][...].astype(F32) + refs[count + index][...].astype(F32)

    value = middle[...]
    inverse = lax.rsqrt(jnp.mean(value * value, axis=1, keepdims=True) + EPS)
    scaled = gain[...] * back_s[...]
    inner = jnp.mean(scaled * value, axis=1, keepdims=True)
    total = upstream[...].astype(F32) + inverse * scaled - value * (inverse**3 * inner)
    grad[...] = total
    branch = total.astype(BF)
    low[...] = branch
    for outs, pair in (((keep.at[0], keep.at[1]), rank), ((send_one.at[0], send_two.at[0]), 1 - rank)):
        column = pl.multiple_of(pair * 2 * HEAD_DIM, 2 * HEAD_DIM)
        result = dot(branch, weight[:, pl.ds(column, 2 * HEAD_DIM)]).astype(BF)
        for head in range(2):
            outs[head][...] = result[:, head * HEAD_DIM : (head + 1) * HEAD_DIM]


def residual_call(info, middle, owns, others, upstream, gain, weights, first, earlier):
    rows, half, count = upstream.shape[0], 4 * HEAD_DIM, len(owns)
    wide = pl.BlockSpec((TILE, D), lambda i, info: (i + first, 0))
    part = pl.BlockSpec((TILE, D), lambda i, info: (0, 0), pipeline_mode=pl.Buffered(1))
    piece = pl.BlockSpec((2, TILE, HEAD_DIM), lambda i, info: (0, i + first, 0))
    single = pl.BlockSpec((1, TILE, HEAD_DIM), lambda i, info: (0, i + first, 0))
    return pl.pallas_call(
        functools.partial(residual_kernel, count),
        out_shape=(
            pltpu.HBM((rows, D), F32),
            jax.ShapeDtypeStruct((rows, D), BF),
            jax.ShapeDtypeStruct((2, rows, HEAD_DIM), BF),
            jax.ShapeDtypeStruct((1, rows, HEAD_DIM), BF),
            jax.ShapeDtypeStruct((1, rows, HEAD_DIM), BF),
        ),
        grid_spec=pltpu.PrefetchScalarGridSpec(
            num_scalar_prefetch=1,
            grid=(count,),
            in_specs=[
                wide,
                wide,
                pl.BlockSpec((1, D), lambda i, info: (0, 0)),
                columns(half, lambda i, info: (0, pl.multiple_of(OUT_AT + info[1] * half, HEAD_DIM))),
            ]
            + [part] * (2 * count)
            + [pl.BlockSpec(memory_space=pl.ANY)] * len(earlier),
            out_specs=(wide, wide, piece, single, single),
            scratch_shapes=[pltpu.VMEM((TILE, D), F32)],
        ),
        input_output_aliases={5 + 2 * count + index: index for index in range(len(earlier))},
        compiler_params=params(18),
        cost_estimate=cost(3e11 if first + count == rows // TILE else 5e7, 0),
        name="residual",
    )(info, in_hbm(middle), in_hbm(upstream), gain, in_hbm(weights), *owns, *others, *earlier)


def join(rank, pieces, joined):
    for head in range(2):
        own, other, other_v = pieces[head], pieces[2 + 2 * head], pieces[3 + 2 * head]
        for part in range(3):
            for value, pair in (
                (own[part, 0], rank),
                (other_v[0, 0] if part == 2 else other[part, 0], 1 - rank),
            ):
                column = pl.multiple_of((part * 4 + pair * 2 + head) * HEAD_DIM, HEAD_DIM)
                joined[:, pl.ds(column, HEAD_DIM)] = value


def back_kernel(info, *refs):
    pieces, (weight, out, joined) = refs[:6], refs[6:]
    join(info[0], pieces, joined)
    out[...] = dot_nt(joined[...], weight[...]).astype(BF)


def back_call(info, pieces, weights):
    rows = pieces[0].shape[2]
    width = 3 * 4 * HEAD_DIM
    piece = [
        pl.BlockSpec((parts, 1, TILE, HEAD_DIM), lambda i, info: (0, 0, i, 0))
        for parts in (3, 3, 2, 1, 2, 1)
    ]
    return pl.pallas_call(
        back_kernel,
        out_shape=jax.ShapeDtypeStruct((rows, D), BF),
        grid_spec=pltpu.PrefetchScalarGridSpec(
            num_scalar_prefetch=1,
            grid=(rows // TILE,),
            in_specs=piece + [pl.BlockSpec((D, width), lambda i, info: (0, 0))],
            out_specs=pl.BlockSpec((TILE, D), lambda i, info: (i, 0)),
            scratch_shapes=[pltpu.VMEM((TILE, width), BF)],
        ),
        compiler_params=params(VMEM),
        cost_estimate=cost(0, 0),
        name="back",
    )(info, *pieces, weights)


def attend_weight_kernel(info, normed, low, *refs):
    pieces, refs = refs[:6], refs[6:]
    attended, (keep, send, joined, out) = refs[:-4], refs[-4:]
    step = pl.program_id(0)

    @pl.when(step == 0)
    def _():
        join(info[0], pieces, joined)

    tile, width = normed.shape[1], joined.shape[1]
    left = normed[...].astype(F32).T.astype(BF)
    out[:, :width] = dot(left, joined[...]).astype(BF)
    left = low[...].astype(F32).T.astype(BF)
    out[:, width:] = dot(left, attended[0][...]).astype(BF)
    scatter(info, out, keep, send)


def attend_weight_call(info, normed, low, attended, pieces, size):
    rows, half = normed.shape[0], attended.shape[1]
    width = 3 * half
    total = width + half
    left = pl.BlockSpec((rows, TILE), lambda i, info: (0, i))
    piece = [
        pl.BlockSpec((parts, 1, rows, HEAD_DIM), lambda i, info: (0, 0, 0, 0))
        for parts in (3, 3, 2, 1, 2, 1)
    ]
    count = D // (4 * size)
    return pl.pallas_call(
        attend_weight_kernel,
        out_shape=(jax.ShapeDtypeStruct((2, count, size, total), BF),) * 2,
        grid_spec=pltpu.PrefetchScalarGridSpec(
            num_scalar_prefetch=1,
            grid=(D // TILE,),
            in_specs=[left, left]
            + piece
            + [pl.BlockSpec((rows, half), lambda i, info: (0, 0))],
            out_specs=(pl.BlockSpec((2, count, size, total), lambda i, info: (0, 0, 0, 0)),) * 2,
            scratch_shapes=[pltpu.VMEM((rows, width), BF), pltpu.VMEM((TILE, total), BF)],
        ),
        compiler_params=params(VMEM),
        cost_estimate=cost(0, 0),
        name="attend_weights",
    )(info, normed, low, *pieces, attended)


def input_kernel(grad, back_own, back_other, tokens, gain, out):
    value = tokens[...].astype(F32)
    back = back_own[...].astype(F32) + back_other[...].astype(F32)
    inverse = lax.rsqrt(jnp.mean(value * value, axis=1, keepdims=True) + EPS)
    scaled = gain[...] * back
    inner = jnp.mean(scaled * value, axis=1, keepdims=True)
    out[...] = (grad[...] + inverse * scaled - value * (inverse**3 * inner)).astype(BF)


def input_call(grad, back_own, back_other, tokens, gain):
    rows = tokens.shape[0]
    wide = pl.BlockSpec((TILE, D), lambda i: (i, 0))
    return pl.pallas_call(
        input_kernel,
        out_shape=jax.ShapeDtypeStruct((rows, D), BF),
        grid=(rows // TILE,),
        in_specs=[wide, wide, wide, wide, pl.BlockSpec((1, D), lambda i: (0, 0))],
        out_specs=wide,
        compiler_params=params(VMEM),
        cost_estimate=cost(12 * rows * D, 12 * MIB),
        name="input_grad",
    )(grad, back_own, back_other, tokens, gain)


def choose(line, options):
    value = options[0]
    for here in range(1, len(options)):
        if options[here] is not options[0]:
            value = jnp.where(line == here, options[here], value)
    return value


def pair_kernel(keep, core, *outs):
    half = keep.shape[1] // 2
    for part in range(2):
        slots = slice(part * half, (part + 1) * half)
        for column in range(2):
            outs[2 * part + column][...] = (
                keep[column, slots].astype(F32) + core[column, slots].astype(F32)
            ).astype(BF)


def pair_add(keep, core):
    count, size, width = keep.shape[1:]
    return pl.pallas_call(
        pair_kernel,
        out_shape=(jax.ShapeDtypeStruct((count // 2, size, width), BF),) * 4,
        compiler_params=pltpu.CompilerParams(vmem_limit_bytes=VMEM * MIB),
        cost_estimate=cost(0, 0),
        name="pair_add",
    )(keep, core)


def split_kernel(left_one, right_one, left_two, right_two, *outs):
    width = left_one.shape[2]
    for index, out in enumerate(outs):
        out[:, :width] = (left_one[index].astype(F32) + right_one[index].astype(F32)).astype(BF)
        out[:, width:] = (left_two[index].astype(F32) + right_two[index].astype(F32)).astype(BF)


def split_add(one, two):
    count, size, width = one[0].shape
    total = width + two[0].shape[2]
    return pl.pallas_call(
        split_kernel,
        out_shape=(jax.ShapeDtypeStruct((size, total), BF),) * count,
        compiler_params=pltpu.CompilerParams(vmem_limit_bytes=VMEM * MIB),
        cost_estimate=cost(0, 0),
        name="split_add",
    )(*one, *two)


def low_kernel(left, right, out):
    out[...] = (left[...].astype(F32) + right[...].astype(F32)).astype(out.dtype)


def low_add(left, right):
    return pl.pallas_call(
        low_kernel,
        out_shape=jax.ShapeDtypeStruct(left.shape, BF),
        compiler_params=pltpu.CompilerParams(vmem_limit_bytes=VMEM * MIB),
        cost_estimate=cost(0, 0),
        name="low_add",
    )(left, right)


def chosen_kernel(flags, first, second, up_in, down_in, up, down):
    one, two = first[...].astype(F32), second[...].astype(F32)
    up[...] = (jnp.where(flags[0] > 0, one, two) + up_in[...].astype(F32)).astype(BF)
    down[...] = (jnp.where(flags[1] > 0, one, two) + down_in[...].astype(F32)).astype(BF)


def chosen_add(flags, first, second, up_in, down_in):
    shape = jax.ShapeDtypeStruct(first.shape, BF)
    vmem = pl.BlockSpec(memory_space=pltpu.VMEM)
    return pl.pallas_call(
        chosen_kernel,
        out_shape=(shape, shape),
        in_specs=[pl.BlockSpec(memory_space=pltpu.SMEM)] + [vmem] * 4,
        out_specs=(vmem, vmem),
        compiler_params=pltpu.CompilerParams(vmem_limit_bytes=VMEM * MIB),
        cost_estimate=cost(0, 0),
        name="chosen_add",
    )(flags, first, second, up_in, down_in)


def reduce_rows(paired, count, first_wait, last_wait):
    length = count // 4
    line = lax.axis_index("dp") // 4
    pairs = [(i, i ^ 2) for i in range(count)]
    over = lambda value: lax.ppermute(value, "dp", pairs)
    (mine_one, theirs_one, mine_two, theirs_two), (down_one, far_one, down_two, far_two) = paired
    others, first_wait = pin(((over(theirs_one), over(far_one)), first_wait))
    sums = list(split_add((mine_one, others[0]), (down_one, others[1])))
    others = (over(theirs_two), over(far_two))
    above = below = None
    for step in range(1, length):
        gap = length - step
        slots = lambda towards: [
            length - 1 - (here ^ (here + towards)) if 0 <= here + towards < length else None
            for here in range(length)
        ]
        ups, downs = slots(gap), slots(-gap)
        used = sorted({slot for slot in ups + downs if slot is not None})
        if len(used) == 1 and step == 1:
            up = down = sums[used[0]]
        elif len(used) == 1:
            one = sums[used[0]]
            up, down = chosen_add(jnp.ones((2,), jnp.int32), one, one, below, above)
        elif len(used) == 2:
            flags = jnp.stack(
                [
                    choose(line, [jnp.int32(slot == used[0]) for slot in side])
                    for side in (ups, downs)
                ]
            )
            up, down = chosen_add(flags, sums[used[0]], sums[used[1]], below, above)
        else:
            fill = lambda side: [sums[used[0] if slot is None else slot] for slot in side]
            up, down = choose(line, fill(ups)), choose(line, fill(downs))
            up, down = low_add(up, below), low_add(down, above)
        below = lax.ppermute(up, "dp", [(i, i + 4) for i in range(count - 4) if i // 4 + gap < length])
        above = lax.ppermute(down, "dp", [(i, i - 4) for i in range(4, count) if i // 4 >= gap])
        if step == length // 2 - 1:
            below, above, others = pin((below, above, others))
            sums += split_add((mine_two, others[0]), (down_two, others[1]))
    below, above, last_wait = pin((below, above, last_wait))
    return sums[-1], below, above, first_wait, last_wait


def interleave_kernel(info, *refs):
    pieces, out = refs[:4], refs[4]
    size = out.shape[0] // (4 * pieces[0].shape[0])
    length = pieces[0].shape[0]
    for index, piece in enumerate(pieces):
        side = info[3] if index % 2 == 0 else 1 - info[3]
        core = info[0] if index // 2 == 0 else 1 - info[0]
        for line in range(length):
            start = pl.multiple_of((line * 4 + side * 2 + core) * size, size)
            out[pl.ds(start, size), :] = piece[line]


def interleave(info, pieces, size):
    width = pieces[0].shape[1]
    pieces = [piece.reshape(-1, size, width) for piece in pieces]
    vmem = pl.BlockSpec(memory_space=pltpu.VMEM)
    return pl.pallas_call(
        interleave_kernel,
        out_shape=pltpu.VMEM((D, width), BF),
        in_specs=[pl.BlockSpec(memory_space=pltpu.SMEM)] + [vmem] * 4,
        out_specs=vmem,
        compiler_params=pltpu.CompilerParams(vmem_limit_bytes=VMEM * MIB),
        cost_estimate=cost(0, 0),
        name="interleave",
    )(info, *pieces)


def gain_kernel(own, other, gain, first, second, first_out, second_out, gain_out):
    low = gain[...].astype(BF).astype(F32)
    results = adamw(gain[...], (own[...] + other[...]) / low, first[...], second[...], 0.6)
    for out, result in zip((first_out, second_out, gain_out), results):
        out[...] = result


def gain_call(own, other, gain, first, second):
    shape = jax.ShapeDtypeStruct(gain.shape, F32)
    return pl.pallas_call(
        gain_kernel,
        out_shape=(shape, shape, shape),
        compiler_params=pltpu.CompilerParams(vmem_limit_bytes=VMEM * MIB),
        cost_estimate=cost(0, 0),
        name="gains",
    )(own, other, gain, first, second)


def shard_kernel(qkv, gains, out):
    width = qkv.shape[2]
    for part in range(3):
        out[:, part * width : (part + 1) * width] = qkv[part].astype(BF)
    rows = jnp.concatenate([gains[...], jnp.zeros((HEAD_DIM - 2, gains.shape[1]), F32)])
    out[:, 3 * width :] = rows.T.astype(BF)


def shard_call(qkv, gains):
    total = 3 * qkv.shape[2] + HEAD_DIM
    return pl.pallas_call(
        shard_kernel,
        out_shape=jax.ShapeDtypeStruct((qkv.shape[1], total), BF),
        compiler_params=pltpu.CompilerParams(vmem_limit_bytes=VMEM * MIB),
        cost_estimate=cost(0, 0),
        name="shard",
    )(qkv, gains)


def pin(values):
    return lax.optimization_barrier(values)


def body(
    tokens,
    cotangent,
    proj_qkv,
    proj_out,
    proj_gate_up,
    proj_down,
    norm_gains,
    first_qkv,
    first_out,
    first_gate_up,
    first_down,
    first_gains,
    second_qkv,
    second_out,
    second_gate_up,
    second_down,
    second_gains,
    cache,
    doc_segments,
    padding,
    retrieval,
):
    rows = tokens.shape[0]
    count = lax.axis_size("dp")
    device = lax.axis_index("dp")
    group = lax.axis_index("mp")
    rank = device % 2
    segment = device // 2
    shard = proj_qkv.shape[1]
    local = proj_qkv.shape[2]
    hidden_here = proj_gate_up.shape[2]
    core_pairs = [(i, i ^ 1) for i in range(count)]

    def across(value):
        return lax.ppermute(value, "mp", [(0, 1), (1, 0)])

    def beside(value):
        return lax.ppermute(value, "dp", core_pairs)

    shard_one = shard_call(proj_qkv, norm_gains)
    out_own = proj_out.astype(BF).T
    out_other = across(out_own)
    shard_two = jnp.concatenate(
        [
            proj_gate_up[0].astype(BF),
            proj_gate_up[1].astype(BF),
            proj_down.astype(BF).T,
            jnp.where(group == 0, out_own, out_other),
            jnp.where(group == 0, out_other, out_own),
        ],
        axis=1,
    )
    length = count // 4
    lines = [[i for i in range(count) if i % 4 == lane] for lane in range(4)]
    own_column = lax.all_gather(shard_one, "dp", axis=0, tiled=True, axis_index_groups=lines)
    next_column = lax.ppermute(own_column, "dp", [(i, i ^ 2) for i in range(count)])
    weights_two = lax.all_gather(shard_two, "dp", axis=0, tiled=True)

    places = jnp.arange(SEG, dtype=jnp.int32)
    starts = jnp.cumsum(doc_segments) - doc_segments
    memory_on = jnp.logical_not(jnp.any(starts == segment))
    side = (device // 2) % 2
    info = jnp.stack([rank, group, memory_on.astype(jnp.int32), side, device // 4]).astype(jnp.int32)
    cosines, sines = rope_tables(places)
    valid = lax.dynamic_slice_in_dim(padding, segment * SEG, SEG)
    lane = jnp.arange(HEAD_DIM, dtype=jnp.int32)[None, :]
    bias = jnp.where((valid[:, None] == 0) & (lane == 0), NEGATIVE, 0.0).astype(BF)
    fetched = cache[retrieval[0]].reshape(RETR, 2, 2, 2, HEAD_DIM).transpose(2, 1, 3, 0, 4)
    mem_own = lax.dynamic_index_in_dim(fetched, rank, keepdims=False)
    mem_other = beside(lax.dynamic_index_in_dim(fetched, 1 - rank, keepdims=False))
    next_column, mem_own, mem_other, bias, cosines, sines, info = pin(
        (next_column, mem_own, mem_other, bias, cosines, sines, info)
    )
    pieces = (own_column, next_column, beside(own_column), beside(next_column))
    weights_one = interleave(info, pieces, shard)

    send, normed_one, gains = project_first(info, tokens, weights_one, cosines, sines)
    gain_one, gain_two = gains[0:1], gains[1:2]
    other = beside(send)
    own = project_second(info, normed_one, weights_one, cosines, sines)
    out_keep, out_send, turned, logs = attend_forward(info, own, other, mem_own, mem_other, bias)
    out_recv = beside(out_send)
    pieces = (out_keep, out_recv, across(out_keep), across(out_recv))
    middle, normed_two, attended = middle_call(info, pieces, tokens, weights_two, gain_two)

    earlier, backs, backs_other = (), [], []
    for chunk, first in enumerate(range(0, rows, TILE)):
        if first + TILE == rows:
            earlier, backs_other[0] = pin((earlier, backs_other[0]))
        *earlier, back = feed_call(normed_two, cotangent, weights_two, first, TILE, earlier)
        backs.append(back)
        backs_other.append(across(back))
    hidden, grad_gate, grad_up, feed_part = earlier
    feed_grads, down_keep, down_send = feed_weight_call(
        info, normed_two, cotangent, hidden, grad_gate, grad_up, shard
    )
    feed_other = across(feed_part)
    backs[0], _ = pin((backs[0], feed_grads))
    earlier = ()
    for chunks in ((0, 1), (2,), (3,)):
        earlier = residual_call(
            info, middle, [backs[index] for index in chunks], [backs_other[index] for index in chunks],
            cotangent, gain_two, weights_two, chunks[0], earlier,
        )
    grad_middle, grad_low, grad_keep, *grad_sends = earlier
    grad_others = [beside(value) for value in grad_sends]

    d_keeps, d_others = [], []
    for head in range(2):
        d_keep, d_send, d_send_v = attend_backward(
            info, own, other, mem_own, mem_other, bias, grad_keep, grad_others[head], turned, logs,
            cosines, sines, head,
        )
        d_keeps.append(d_keep)
        d_others += [beside(d_send), beside(d_send_v)]
    moved = d_keeps + d_others
    back_one = back_call(info, moved, weights_one)
    moved[0], _ = pin((moved[0], back_one))
    attend_keep, attend_send = attend_weight_call(info, normed_one, grad_low, attended, moved, shard)
    back_one, feed_other = pin((back_one, feed_other))
    back_one_other = across(back_one)
    input_grad = input_call(grad_middle, back_one, back_one_other, tokens, gain_one)
    block_out = (
        middle + (feed_part.astype(F32) + feed_other.astype(F32))
    ).astype(BF)
    paired = [
        pair_add(keep, beside(send))
        for keep, send in ((attend_keep, attend_send), (down_keep, down_send))
    ]
    total, below, above, block_out, input_grad = reduce_rows(paired, count, block_out, input_grad)
    feed_sum = lax.psum_scatter(feed_grads, "dp", scatter_dimension=0, tiled=True).astype(F32)
    gate_up_sum = jnp.stack([feed_sum[:, :hidden_here], feed_sum[:, hidden_here : 2 * hidden_here]])
    gate_up_first, gate_up_second, gate_up_new = adamw(
        proj_gate_up, gate_up_sum, first_gate_up, second_gate_up, 0.5 / math.sqrt(D)
    )
    gate_up_new, total, below, above = pin((gate_up_new, total, below, above))
    attend_sum = total.astype(F32) + (below.astype(F32) + above.astype(F32))
    down_sum = jnp.concatenate([feed_sum[:, 2 * hidden_here :].T, attend_sum[:, 4 * local :].T])
    down_first, down_second, down_new = adamw(
        proj_down, down_sum, first_down, second_down, 0.5 / math.sqrt(FF)
    )
    qkv_sum = jnp.stack([attend_sum[:, part * local : (part + 1) * local] for part in range(3)])
    out_sum = attend_sum[:, 3 * local : 4 * local].T
    low_qkv, low_gate_up = proj_qkv.astype(BF).astype(F32), proj_gate_up.astype(BF).astype(F32)
    gains_sum = jnp.stack(
        [jnp.sum(low_qkv * qkv_sum, axis=(0, 2)), jnp.sum(low_gate_up * gate_up_sum, axis=(0, 2))]
    )
    gains_first, gains_second, gains_new = gain_call(
        gains_sum, across(gains_sum), norm_gains, first_gains, second_gains
    )

    qkv_first, qkv_second, qkv_new = adamw(
        proj_qkv, qkv_sum, first_qkv, second_qkv, 0.5 / math.sqrt(D)
    )
    out_first, out_second, out_new = adamw(
        proj_out, out_sum, first_out, second_out, 0.5 / math.sqrt(max(1, 4 * D // SEG))
    )
    return (
        block_out,
        input_grad,
        qkv_first,
        qkv_second,
        qkv_new,
        out_first,
        out_second,
        out_new,
        gate_up_first,
        gate_up_second,
        gate_up_new,
        down_first,
        down_second,
        down_new,
        gains_first,
        gains_second,
        gains_new,
    )


def solution(mesh):
    return jax.shard_map(
        body,
        mesh=mesh,
        in_specs=(
            P("dp", None),
            P("dp", None),
            P(None, "dp", "mp"),
            P("mp", "dp"),
            P(None, "dp", "mp"),
            P("mp", "dp"),
            P(None, "dp"),
            P(None, "dp", "mp"),
            P("mp", "dp"),
            P(None, "dp", "mp"),
            P("mp", "dp"),
            P(None, "dp"),
            P(None, "dp", "mp"),
            P("mp", "dp"),
            P(None, "dp", "mp"),
            P("mp", "dp"),
            P(None, "dp"),
            P("dp", None, "mp"),
            P(),
            P(),
            P("dp", None),
        ),
        out_specs=(
            P("dp", None),
            P("dp", None),
            P(None, "dp", "mp"),
            P(None, "dp", "mp"),
            P(None, "dp", "mp"),
            P("mp", "dp"),
            P("mp", "dp"),
            P("mp", "dp"),
            P(None, "dp", "mp"),
            P(None, "dp", "mp"),
            P(None, "dp", "mp"),
            P("mp", "dp"),
            P("mp", "dp"),
            P("mp", "dp"),
            P(None, "dp"),
            P(None, "dp"),
            P(None, "dp"),
        ),
        check_vma=False,
    )
```

```python
import functools
import math

import jax
import jax.numpy as jnp
from jax import lax
from jax.experimental import pallas as pl
from jax.experimental.pallas import tpu as pltpu
from jax.sharding import PartitionSpec as P

D = 1024
HEAD_DIM = 128
FF = 2816
SEG = 2048
RETR = 128
STEP = 10

EPS = 1e-05
BETA_ONE = 0.9
BETA_TWO = 0.95
ADAM_EPS = 1e-08
DECAY = 0.1
NEGATIVE = -1e30
SCALE = HEAD_DIM**-0.5
SCALE_TWO = SCALE * math.log2(math.e)

BF = jnp.bfloat16
F32 = jnp.float32
MIB = 1024 * 1024
TILE = 256
VMEM = 26
WEIGH = 1.0


def dot(left, right):
    return jnp.dot(left, right, preferred_element_type=F32)


def dot_nt(left, right):
    return lax.dot_general(left, right, (((1,), (1,)), ((), ())), preferred_element_type=F32)


def dot_tn(left, right):
    return lax.dot_general(left, right, (((0,), (0,)), ((), ())), preferred_element_type=F32)


def params(mib, axes=1):
    return pltpu.CompilerParams(
        dimension_semantics=("arbitrary",) * axes, vmem_limit_bytes=mib * MIB
    )


def cost(flops, moved, trans=0):
    return pl.CostEstimate(flops=int(flops * WEIGH), bytes_accessed=int(moved * WEIGH), transcendentals=int(trans))


def rope_tables(places):
    half_dim = HEAD_DIM // 2
    freqs = 10000.0 ** (-(jnp.arange(half_dim, dtype=F32) / half_dim))
    phase = places.astype(F32)[:, None] * freqs[None, :]
    cosines, sines = jnp.cos(phase), jnp.sin(phase)
    return jnp.concatenate([cosines, cosines], 1), jnp.concatenate([-sines, sines], 1)


def turn(value, cosines, sines):
    return value * cosines + pltpu.roll(value, HEAD_DIM // 2, 1) * sines


def adamw(weight, grad, first, second, rate):
    first_new = BETA_ONE * first + (1.0 - BETA_ONE) * grad
    second_new = BETA_TWO * second + (1.0 - BETA_TWO) * grad * grad
    first_hat = first_new / (1.0 - BETA_ONE**STEP)
    second_hat = second_new / (1.0 - BETA_TWO**STEP)
    updated = weight - rate * (first_hat / (jnp.sqrt(second_hat) + ADAM_EPS) + DECAY * weight)
    return (first_new, second_new, updated)


def rotate_out(result, part, cosines, sines, out):
    for head in range(2):
        value = result[:, head * HEAD_DIM : (head + 1) * HEAD_DIM]

        @pl.when(part < 2)
        def _():
            out[0, head] = turn(value, cosines[...], sines[...]).astype(BF)

        @pl.when(part == 2)
        def _():
            out[0, head] = value.astype(BF)


def first_kernel(info, tokens, gain_columns, weight, cosines, sines, out, normed, gains):
    part = pl.program_id(0)

    @pl.when(part == 0)
    def _():
        rows = gain_columns[...].astype(F32).T[:8, :]
        gains[...] = rows
        value = tokens[...].astype(F32)
        inverse = lax.rsqrt(jnp.mean(value * value, axis=1, keepdims=True) + EPS)
        normed[...] = (value * inverse * rows[0:1, :]).astype(BF)

    rotate_out(dot(normed[...], weight[...]), part, cosines, sines, out)


def second_kernel(info, normed, weight, cosines, sines, out):
    rotate_out(dot(normed[...], weight[...]), pl.program_id(0), cosines, sines, out)


def project_first(info, tokens, weights, cosines, sines):
    rows = tokens.shape[0]
    return pl.pallas_call(
        first_kernel,
        out_shape=(
            jax.ShapeDtypeStruct((3, 2, rows, HEAD_DIM), BF),
            jax.ShapeDtypeStruct((rows, D), BF),
            jax.ShapeDtypeStruct((8, D), F32),
        ),
        grid_spec=pltpu.PrefetchScalarGridSpec(
            num_scalar_prefetch=1,
            grid=(3,),
            in_specs=[
                pl.BlockSpec((rows, D), lambda j, info: (0, 0)),
                pl.BlockSpec((D, HEAD_DIM), lambda j, info: (0, 12)),
                pl.BlockSpec((D, 256), lambda j, info: (0, 2 * j + 1 - info[0])),
                pl.BlockSpec((rows, HEAD_DIM), lambda j, info: (info[0], 0)),
                pl.BlockSpec((rows, HEAD_DIM), lambda j, info: (info[0], 0)),
            ],
            out_specs=(
                pl.BlockSpec((1, 2, rows, HEAD_DIM), lambda j, info: (j, 0, 0, 0)),
                pl.BlockSpec((rows, D), lambda j, info: (0, 0)),
                pl.BlockSpec((8, D), lambda j, info: (0, 0)),
            ),
        ),
        compiler_params=params(VMEM),
        cost_estimate=cost(0, 0),
        name="project_first",
    )(info, tokens, weights, weights, cosines, sines)


def project_second(info, normed, weights, cosines, sines):
    rows = normed.shape[0]
    return pl.pallas_call(
        second_kernel,
        out_shape=pltpu.HBM((3, 2, rows, HEAD_DIM), BF),
        grid_spec=pltpu.PrefetchScalarGridSpec(
            num_scalar_prefetch=1,
            grid=(3,),
            in_specs=[
                pl.BlockSpec((rows, D), lambda j, info: (0, 0)),
                pl.BlockSpec((D, 256), lambda j, info: (0, 2 * j + info[0])),
                pl.BlockSpec((rows, HEAD_DIM), lambda j, info: (info[0], 0)),
                pl.BlockSpec((rows, HEAD_DIM), lambda j, info: (info[0], 0)),
            ],
            out_specs=pl.BlockSpec((1, 2, rows, HEAD_DIM), lambda j, info: (j, 0, 0, 0)),
        ),
        compiler_params=params(VMEM),
        cost_estimate=cost(0, 0),
        name="project_second",
    )(info, normed, weights, cosines, sines)


def place(scratch, own, other, rank, rows):
    scratch[pl.ds(pl.multiple_of(rank * rows, rows), rows), :] = own
    scratch[pl.ds(pl.multiple_of((1 - rank) * rows, rows), rows), :] = other


def chunks_of(tile, step):
    end = tile * TILE
    spans = [(start, min(step, end - start)) for start in range(0, end, step)]
    return spans + [(end, TILE)]


def causal(scores):
    rows = lax.broadcasted_iota(jnp.int32, scores.shape, 0)
    columns = lax.broadcasted_iota(jnp.int32, scores.shape, 1)
    return jnp.where(rows <= columns, scores, NEGATIVE)


def forward_kernel(
    info, own, other, mem_own, mem_other, bias, keep, send, turned, logs,
    q_s, k_s, v_s, vt_s, mem_s, s_s, out_s,
):
    rank = info[0]
    rows = own.shape[2]
    mem_bias = jnp.where(info[2] > 0, 0.0, NEGATIVE).astype(F32)
    place(q_s, own[0, 0], other[0, 0], rank, rows)
    place(k_s, own[1, 0], other[1, 0], rank, rows)
    place(v_s, own[2, 0], other[2, 0], rank, rows)
    mem_s[rank] = mem_own[:, 0]
    mem_s[1 - rank] = mem_other[:, 0]
    vt_s[...] = v_s[...].astype(F32).T.astype(BF)
    ones = (lax.broadcasted_iota(jnp.int32, (TILE, HEAD_DIM), 1) == 0).astype(BF)
    for tile in range(SEG // TILE):
        here = slice(tile * TILE, (tile + 1) * TILE)
        block = tile * TILE // rows
        query = q_s[here, :]
        wide = jnp.concatenate([query, ones], axis=1)
        spans = chunks_of(tile, 512)
        scores = dot_nt(mem_s[block, 0], query) + mem_bias
        s_s[SEG : SEG + RETR, :] = scores
        top = jnp.max(scores, axis=0, keepdims=True)
        for start, size in spans:
            span = slice(start, start + size)
            if start + size > SEG // 2:
                scores = dot_nt(jnp.concatenate([k_s[span, :], bias[span, :]], axis=1), wide)
            else:
                scores = dot_nt(k_s[span, :], query)
            if start == tile * TILE:
                scores = causal(scores)
            s_s[span, :] = scores
            top = jnp.maximum(top, jnp.max(scores, axis=0, keepdims=True))
        shift = top * SCALE_TWO
        exponent = jnp.exp2(s_s[SEG : SEG + RETR, :] * SCALE_TWO - shift)
        total = jnp.sum(exponent, axis=0, keepdims=True)
        result = dot(mem_s[block, 1].astype(F32).T.astype(BF), exponent.astype(BF))
        for start, size in spans:
            span = slice(start, start + size)
            exponent = jnp.exp2(s_s[span, :] * SCALE_TWO - shift)
            total = total + jnp.sum(exponent, axis=0, keepdims=True)
            result = result + dot(vt_s[:, span], exponent.astype(BF))
        result = result * (1.0 / total)
        turned[0, :, here] = result
        logs[0, :, here] = shift + jnp.log2(total)
        out_s[here, :] = result.T.astype(BF)
    keep[0] = out_s[pl.ds(pl.multiple_of(rank * rows, rows), rows), :]
    send[0] = out_s[pl.ds(pl.multiple_of((1 - rank) * rows, rows), rows), :]


def attend_forward(info, own, other, mem_own, mem_other, bias):
    rows = own.shape[2]
    part = pl.BlockSpec((3, 1, rows, HEAD_DIM), lambda h, info: (0, h, 0, 0))
    mem = pl.BlockSpec((2, 1, RETR, HEAD_DIM), lambda h, info: (0, h, 0, 0))
    half = pl.BlockSpec((1, rows, HEAD_DIM), lambda h, info: (h, 0, 0))
    return pl.pallas_call(
        forward_kernel,
        out_shape=(
            jax.ShapeDtypeStruct((2, rows, HEAD_DIM), BF),
            jax.ShapeDtypeStruct((2, rows, HEAD_DIM), BF),
            pltpu.HBM((2, HEAD_DIM, SEG), F32),
            jax.ShapeDtypeStruct((2, 1, SEG), F32),
        ),
        grid_spec=pltpu.PrefetchScalarGridSpec(
            num_scalar_prefetch=1,
            grid=(2,),
            in_specs=[
                part,
                part,
                mem,
                mem,
                pl.BlockSpec((SEG, HEAD_DIM), lambda h, info: (0, 0)),
            ],
            out_specs=(
                half,
                half,
                pl.BlockSpec((1, HEAD_DIM, SEG), lambda h, info: (h, 0, 0)),
                pl.BlockSpec((1, 1, SEG), lambda h, info: (h, 0, 0)),
            ),
            scratch_shapes=[
                pltpu.VMEM((SEG, HEAD_DIM), BF),
                pltpu.VMEM((SEG, HEAD_DIM), BF),
                pltpu.VMEM((SEG, HEAD_DIM), BF),
                pltpu.VMEM((HEAD_DIM, SEG), BF),
                pltpu.VMEM((2, 2, RETR, HEAD_DIM), BF),
                pltpu.VMEM((SEG + RETR, TILE), F32),
                pltpu.VMEM((SEG, HEAD_DIM), BF),
            ],
        ),
        compiler_params=params(VMEM),
        cost_estimate=cost(0, 0),
        name="attend_forward",
    )(info, own, other, mem_own, mem_other, bias)


def backward_kernel(
    info, own, other, mem_own, mem_other, bias, grad_own, grad_other, turned, logs, cosines, sines,
    keep, send, send_v,
    q_s, k_s, v_s, g_s, kt_s, mem_s, dots_s, dq_s, dk_s, dv_s,
):
    rank = info[0]
    rows = own.shape[2]
    mem_bias = jnp.where(info[2] > 0, 0.0, NEGATIVE).astype(F32)
    place(q_s, own[0, 0], other[0, 0], rank, rows)
    place(k_s, own[1, 0], other[1, 0], rank, rows)
    place(v_s, own[2, 0], other[2, 0], rank, rows)
    place(g_s, grad_own[0], grad_other[0], rank, rows)
    mem_s[rank] = mem_own[:, 0]
    mem_s[1 - rank] = mem_other[:, 0]
    kt_s[...] = k_s[...].astype(F32).T.astype(BF)
    dots_s[...] = jnp.sum(g_s[...].astype(F32).T * turned[0], axis=0, keepdims=True)
    dk_s[...] = jnp.zeros_like(dk_s)
    dv_s[...] = jnp.zeros_like(dv_s)
    ones = (lax.broadcasted_iota(jnp.int32, (TILE, HEAD_DIM), 1) == 0).astype(BF)
    for tile in range(SEG // TILE):
        here = slice(tile * TILE, (tile + 1) * TILE)
        block = tile * TILE // rows
        query = q_s[here, :]
        wide = jnp.concatenate([query, ones], axis=1)
        grad = g_s[here, :]
        log = logs[0, :, here]
        dots = dots_s[:, here]
        scores = dot_nt(mem_s[block, 0], query) + mem_bias
        probs = jnp.exp2(scores * SCALE_TWO - log)
        change = (probs * (dot_nt(mem_s[block, 1], grad) - dots)).astype(BF)
        result = dot(mem_s[block, 0].astype(F32).T.astype(BF), change)
        for start, size in chunks_of(tile, 512):
            span = slice(start, start + size)
            keys = k_s[span, :]
            if start + size > SEG // 2:
                scores = dot_nt(jnp.concatenate([keys, bias[span, :]], axis=1), wide)
            else:
                scores = dot_nt(keys, query)
            if start == tile * TILE:
                scores = causal(scores)
            probs = jnp.exp2(scores * SCALE_TWO - log)
            change = (probs * (dot_nt(v_s[span, :], grad) - dots)).astype(BF)
            dv_s[span, :] += dot(probs.astype(BF), grad)
            dk_s[span, :] += dot(change, query)
            result = result + dot(kt_s[:, span], change)
        dq_s[here, :] = turn(result.T * SCALE, cosines[here, :], -sines[here, :]).astype(BF)
    for outs, place_ in (((keep.at[0], keep.at[1], keep.at[2]), rank), ((send.at[0], send.at[1], send_v.at[0]), 1 - rank)):
        held = pl.ds(pl.multiple_of(place_ * rows, rows), rows)
        outs[0][0] = dq_s[held, :]
        outs[1][0] = turn(dk_s[held, :] * SCALE, cosines[held, :], -sines[held, :]).astype(BF)
        outs[2][0] = dv_s[held, :].astype(BF)


def attend_backward(
    info, own, other, mem_own, mem_other, bias, grad_own, grad_other, turned, logs, cosines, sines, head
):
    rows = own.shape[2]
    part = pl.BlockSpec((3, 1, rows, HEAD_DIM), lambda h, info: (0, head, 0, 0))
    mem = pl.BlockSpec((2, 1, RETR, HEAD_DIM), lambda h, info: (0, head, 0, 0))
    half = pl.BlockSpec((1, rows, HEAD_DIM), lambda h, info: (head, 0, 0))
    table = pl.BlockSpec((SEG, HEAD_DIM), lambda h, info: (0, 0))
    return pl.pallas_call(
        backward_kernel,
        out_shape=tuple(jax.ShapeDtypeStruct((parts, 1, rows, HEAD_DIM), BF) for parts in (3, 2, 1)),
        grid_spec=pltpu.PrefetchScalarGridSpec(
            num_scalar_prefetch=1,
            grid=(1,),
            in_specs=[
                part,
                part,
                mem,
                mem,
                table,
                half,
                pl.BlockSpec((1, rows, HEAD_DIM), lambda h, info: (0, 0, 0)),
                pl.BlockSpec((1, HEAD_DIM, SEG), lambda h, info: (head, 0, 0)),
                pl.BlockSpec((1, 1, SEG), lambda h, info: (head, 0, 0)),
                table,
                table,
            ],
            out_specs=tuple(
                pl.BlockSpec((parts, 1, rows, HEAD_DIM), lambda h, info: (0, 0, 0, 0)) for parts in (3, 2, 1)
            ),
            scratch_shapes=[pltpu.VMEM((SEG, HEAD_DIM), BF)] * 4
            + [
                pltpu.VMEM((HEAD_DIM, SEG), BF),
                pltpu.VMEM((2, 2, RETR, HEAD_DIM), BF),
                pltpu.VMEM((1, SEG), F32),
                pltpu.VMEM((SEG, HEAD_DIM), BF),
                pltpu.VMEM((SEG, HEAD_DIM), F32),
                pltpu.VMEM((SEG, HEAD_DIM), F32),
            ],
        ),
        compiler_params=params(VMEM),
        cost_estimate=cost(0, 0),
        name="attend_backward",
    )(
        info, own, other, mem_own, mem_other, bias, grad_own, grad_other, turned, logs, cosines, sines
    )


OUT_AT = 3 * FF // 2


def in_hbm(value):
    return pltpu.with_memory_space_constraint(value, pltpu.HBM)


def columns(width, start):
    return pl.BlockSpec(
        (pl.Element(D), pl.Element(width)), start, pipeline_mode=pl.Buffered(1)
    )


def middle_kernel(info, *refs):
    pieces, (tokens, weight, gain, middle, normed, attended, joined) = refs[:4], refs[4:]
    rank, group = info[0], info[1]
    for index, piece in enumerate(pieces):
        side = (group, 1 - group)[index // 2]
        pair = (rank, 1 - rank)[index % 2]
        for head in range(2):
            column = pl.multiple_of((side * 4 + pair * 2 + head) * HEAD_DIM, HEAD_DIM)
            joined[:, pl.ds(column, HEAD_DIM)] = piece[head]
    half = attended.shape[1]
    attended[...] = joined[:, pl.ds(pl.multiple_of(group * half, half), half)]
    value = tokens[...].astype(F32) + dot_nt(joined[...], weight[...])
    middle[...] = value
    inverse = lax.rsqrt(jnp.mean(value * value, axis=1, keepdims=True) + EPS)
    normed[...] = (value * inverse * gain[...]).astype(BF)


def middle_call(info, pieces, tokens, weights, gain):
    rows, half = tokens.shape[0], 4 * HEAD_DIM
    piece = pl.BlockSpec((2, TILE, HEAD_DIM), lambda i, info: (0, i, 0))
    wide = pl.BlockSpec((TILE, D), lambda i, info: (i, 0))
    return pl.pallas_call(
        middle_kernel,
        out_shape=(
            pltpu.HBM((rows, D), F32),
            jax.ShapeDtypeStruct((rows, D), BF),
            pltpu.HBM((rows, half), BF),
        ),
        grid_spec=pltpu.PrefetchScalarGridSpec(
            num_scalar_prefetch=1,
            grid=(rows // TILE,),
            in_specs=[piece] * 4
            + [
                wide,
                columns(D, lambda i, info: (0, OUT_AT)),
                pl.BlockSpec((1, D), lambda i, info: (0, 0)),
            ],
            out_specs=(wide, wide, pl.BlockSpec((TILE, half), lambda i, info: (i, 0))),
            scratch_shapes=[pltpu.VMEM((TILE, D), BF)],
        ),
        compiler_params=params(VMEM),
        cost_estimate=cost(0, 0),
        name="middle",
    )(info, *[in_hbm(piece) for piece in pieces], in_hbm(tokens), in_hbm(weights), gain)


def feed_kernel(normed, upstream, gate_w, up_w, down_w, *refs):
    hidden, gate_grad, up_grad, feed, back = refs[-5:]
    gate = dot(normed[...], gate_w[...])
    up_part = dot(normed[...], up_w[...])
    sigma = jax.nn.sigmoid(gate)
    silu = gate * sigma
    low = (silu * up_part).astype(BF)
    hidden[...] = low
    feed[...] = dot_nt(low, down_w[...]).astype(BF)
    grad = dot(upstream[...], down_w[...])
    grad_gate = (grad * up_part * sigma * (1.0 + gate * (1.0 - sigma))).astype(BF)
    grad_up = (grad * silu).astype(BF)
    gate_grad[...] = grad_gate
    up_grad[...] = grad_up
    back[...] = (dot_nt(grad_gate, gate_w[...]) + dot_nt(grad_up, up_w[...])).astype(BF)


def feed_call(normed, upstream, weights, first, count, earlier):
    rows = upstream.shape[0]
    width = FF // 2
    whole = lambda index: pl.BlockSpec((D, width), lambda i: (0, index), pipeline_mode=pl.Buffered(1))
    source = pl.BlockSpec((TILE, D), lambda i: (i + first // TILE, 0))
    narrow = pl.BlockSpec((TILE, width), lambda i: (i + first // TILE, 0))
    return pl.pallas_call(
        feed_kernel,
        out_shape=(pltpu.VMEM((rows, width), BF),) * 3
        + (jax.ShapeDtypeStruct((rows, D), BF), jax.ShapeDtypeStruct((count, D), BF)),
        grid=(count // TILE,),
        in_specs=[source, source, whole(0), whole(1), whole(2)]
        + [pl.BlockSpec(memory_space=pl.ANY)] * len(earlier),
        out_specs=(narrow, narrow, narrow, source, pl.BlockSpec((TILE, D), lambda i: (i, 0))),
        input_output_aliases={5 + index: index for index in range(len(earlier))},
        compiler_params=params(VMEM),
        cost_estimate=cost(5e7, 0),
        name="feed",
    )(normed, upstream, weights, weights, weights, *earlier)


DOWN_SPLIT = 1024


def scatter(info, out, keep, send):
    step, tile = pl.program_id(0), out.shape[0]
    count, size = keep.shape[1], keep.shape[2]
    for line in range(tile // (4 * size)):
        slot = count - 1 - ((step * (tile // (4 * size)) + line) ^ info[4])
        for column in range(2):
            for target, core in ((keep, info[0]), (send, 1 - info[0])):
                side = info[3] if column == 0 else 1 - info[3]
                start = pl.multiple_of((line * 4 + side * 2 + core) * size, size)
                target[column, slot] = out[pl.ds(start, size), :]


def feed_weight_kernel(info, normed, upstream, hidden, gate_grad, up_grad, out, keep, send, last):
    width = gate_grad.shape[1]
    left = normed[...].astype(F32).T.astype(BF)
    out[:, :width] = dot(left, gate_grad[...]).astype(BF)
    out[:, width : 2 * width] = dot(left, up_grad[...]).astype(BF)
    left = upstream[...].astype(F32).T.astype(BF)
    result = dot(left, hidden[...]).astype(BF)
    out[:, 2 * width :] = result[:, :DOWN_SPLIT]
    last[...] = result[:, DOWN_SPLIT:]
    scatter(info, last, keep, send)


def feed_weight_call(info, normed, upstream, hidden, gate_grad, up_grad, size):
    rows, width = gate_grad.shape
    total, rest, count = 2 * width + DOWN_SPLIT, width - DOWN_SPLIT, D // (4 * size)
    left = pl.BlockSpec((rows, TILE), lambda i, info: (0, i))
    whole = pl.BlockSpec((rows, width), lambda i, info: (0, 0), pipeline_mode=pl.Buffered(1))
    return pl.pallas_call(
        feed_weight_kernel,
        out_shape=(pltpu.HBM((D, total), BF),)
        + (jax.ShapeDtypeStruct((2, count, size, rest), BF),) * 2,
        grid_spec=pltpu.PrefetchScalarGridSpec(
            num_scalar_prefetch=1,
            grid=(D // TILE,),
            in_specs=[left, left, whole, whole, whole],
            out_specs=(pl.BlockSpec((TILE, total), lambda i, info: (i, 0)),)
            + (pl.BlockSpec((2, count, size, rest), lambda i, info: (0, 0, 0, 0)),) * 2,
            scratch_shapes=[pltpu.VMEM((TILE, rest), BF)],
        ),
        compiler_params=params(24),
        cost_estimate=cost(5e7, 0),
        name="feed_weights",
    )(info, normed, in_hbm(upstream), hidden, gate_grad, up_grad)


def residual_kernel(count, info, middle, upstream, gain, weight, *refs):
    grad, low, keep, send_one, send_two, back_s = refs[-6:]
    rank = info[0]
    for index in range(count):

        @pl.when(pl.program_id(0) == index)
        def _():
            back_s[...] = refs[index][...].astype(F32) + refs[count + index][...].astype(F32)

    value = middle[...]
    inverse = lax.rsqrt(jnp.mean(value * value, axis=1, keepdims=True) + EPS)
    scaled = gain[...] * back_s[...]
    inner = jnp.mean(scaled * value, axis=1, keepdims=True)
    total = upstream[...].astype(F32) + inverse * scaled - value * (inverse**3 * inner)
    grad[...] = total
    branch = total.astype(BF)
    low[...] = branch
    for outs, pair in (((keep.at[0], keep.at[1]), rank), ((send_one.at[0], send_two.at[0]), 1 - rank)):
        column = pl.multiple_of(pair * 2 * HEAD_DIM, 2 * HEAD_DIM)
        result = dot(branch, weight[:, pl.ds(column, 2 * HEAD_DIM)]).astype(BF)
        for head in range(2):
            outs[head][...] = result[:, head * HEAD_DIM : (head + 1) * HEAD_DIM]


def residual_call(info, middle, owns, others, upstream, gain, weights, first, earlier):
    rows, half, count = upstream.shape[0], 4 * HEAD_DIM, len(owns)
    wide = pl.BlockSpec((TILE, D), lambda i, info: (i + first, 0))
    part = pl.BlockSpec((TILE, D), lambda i, info: (0, 0), pipeline_mode=pl.Buffered(1))
    piece = pl.BlockSpec((2, TILE, HEAD_DIM), lambda i, info: (0, i + first, 0))
    single = pl.BlockSpec((1, TILE, HEAD_DIM), lambda i, info: (0, i + first, 0))
    return pl.pallas_call(
        functools.partial(residual_kernel, count),
        out_shape=(
            pltpu.HBM((rows, D), F32),
            jax.ShapeDtypeStruct((rows, D), BF),
            jax.ShapeDtypeStruct((2, rows, HEAD_DIM), BF),
            jax.ShapeDtypeStruct((1, rows, HEAD_DIM), BF),
            jax.ShapeDtypeStruct((1, rows, HEAD_DIM), BF),
        ),
        grid_spec=pltpu.PrefetchScalarGridSpec(
            num_scalar_prefetch=1,
            grid=(count,),
            in_specs=[
                wide,
                wide,
                pl.BlockSpec((1, D), lambda i, info: (0, 0)),
                columns(half, lambda i, info: (0, pl.multiple_of(OUT_AT + info[1] * half, HEAD_DIM))),
            ]
            + [part] * (2 * count)
            + [pl.BlockSpec(memory_space=pl.ANY)] * len(earlier),
            out_specs=(wide, wide, piece, single, single),
            scratch_shapes=[pltpu.VMEM((TILE, D), F32)],
        ),
        input_output_aliases={5 + 2 * count + index: index for index in range(len(earlier))},
        compiler_params=params(18),
        cost_estimate=cost(3e11 if first + count == rows // TILE else 5e7, 0),
        name="residual",
    )(info, in_hbm(middle), in_hbm(upstream), gain, in_hbm(weights), *owns, *others, *earlier)


def join(rank, pieces, joined):
    for head in range(2):
        own, other, other_v = pieces[head], pieces[2 + 2 * head], pieces[3 + 2 * head]
        for part in range(3):
            for value, pair in (
                (own[part, 0], rank),
                (other_v[0, 0] if part == 2 else other[part, 0], 1 - rank),
            ):
                column = pl.multiple_of((part * 4 + pair * 2 + head) * HEAD_DIM, HEAD_DIM)
                joined[:, pl.ds(column, HEAD_DIM)] = value


def back_kernel(info, *refs):
    pieces, (weight, out, joined) = refs[:6], refs[6:]
    join(info[0], pieces, joined)
    out[...] = dot_nt(joined[...], weight[...]).astype(BF)


def back_call(info, pieces, weights):
    rows = pieces[0].shape[2]
    width = 3 * 4 * HEAD_DIM
    piece = [
        pl.BlockSpec((parts, 1, TILE, HEAD_DIM), lambda i, info: (0, 0, i, 0))
        for parts in (3, 3, 2, 1, 2, 1)
    ]
    return pl.pallas_call(
        back_kernel,
        out_shape=jax.ShapeDtypeStruct((rows, D), BF),
        grid_spec=pltpu.PrefetchScalarGridSpec(
            num_scalar_prefetch=1,
            grid=(rows // TILE,),
            in_specs=piece + [pl.BlockSpec((D, width), lambda i, info: (0, 0))],
            out_specs=pl.BlockSpec((TILE, D), lambda i, info: (i, 0)),
            scratch_shapes=[pltpu.VMEM((TILE, width), BF)],
        ),
        compiler_params=params(VMEM),
        cost_estimate=cost(0, 0),
        name="back",
    )(info, *pieces, weights)


def attend_weight_kernel(info, normed, low, *refs):
    pieces, refs = refs[:6], refs[6:]
    attended, (keep, send, joined, out) = refs[:-4], refs[-4:]
    step = pl.program_id(0)

    @pl.when(step == 0)
    def _():
        join(info[0], pieces, joined)

    tile, width = normed.shape[1], joined.shape[1]
    left = normed[...].astype(F32).T.astype(BF)
    out[:, :width] = dot(left, joined[...]).astype(BF)
    left = low[...].astype(F32).T.astype(BF)
    out[:, width:] = dot(left, attended[0][...]).astype(BF)
    scatter(info, out, keep, send)


def attend_weight_call(info, normed, low, attended, pieces, size):
    rows, half = normed.shape[0], attended.shape[1]
    width = 3 * half
    total = width + half
    left = pl.BlockSpec((rows, TILE), lambda i, info: (0, i))
    piece = [
        pl.BlockSpec((parts, 1, rows, HEAD_DIM), lambda i, info: (0, 0, 0, 0))
        for parts in (3, 3, 2, 1, 2, 1)
    ]
    count = D // (4 * size)
    return pl.pallas_call(
        attend_weight_kernel,
        out_shape=(jax.ShapeDtypeStruct((2, count, size, total), BF),) * 2,
        grid_spec=pltpu.PrefetchScalarGridSpec(
            num_scalar_prefetch=1,
            grid=(D // TILE,),
            in_specs=[left, left]
            + piece
            + [pl.BlockSpec((rows, half), lambda i, info: (0, 0))],
            out_specs=(pl.BlockSpec((2, count, size, total), lambda i, info: (0, 0, 0, 0)),) * 2,
            scratch_shapes=[pltpu.VMEM((rows, width), BF), pltpu.VMEM((TILE, total), BF)],
        ),
        compiler_params=params(VMEM),
        cost_estimate=cost(0, 0),
        name="attend_weights",
    )(info, normed, low, *pieces, attended)


def input_kernel(grad, back_own, back_other, tokens, gain, out):
    value = tokens[...].astype(F32)
    back = back_own[...].astype(F32) + back_other[...].astype(F32)
    inverse = lax.rsqrt(jnp.mean(value * value, axis=1, keepdims=True) + EPS)
    scaled = gain[...] * back
    inner = jnp.mean(scaled * value, axis=1, keepdims=True)
    out[...] = (grad[...] + inverse * scaled - value * (inverse**3 * inner)).astype(BF)


def input_call(grad, back_own, back_other, tokens, gain):
    rows = tokens.shape[0]
    wide = pl.BlockSpec((TILE, D), lambda i: (i, 0))
    return pl.pallas_call(
        input_kernel,
        out_shape=jax.ShapeDtypeStruct((rows, D), BF),
        grid=(rows // TILE,),
        in_specs=[wide, wide, wide, wide, pl.BlockSpec((1, D), lambda i: (0, 0))],
        out_specs=wide,
        compiler_params=params(VMEM),
        cost_estimate=cost(12 * rows * D, 12 * MIB),
        name="input_grad",
    )(grad, back_own, back_other, tokens, gain)


def choose(line, options):
    value = options[0]
    for here in range(1, len(options)):
        if options[here] is not options[0]:
            value = jnp.where(line == here, options[here], value)
    return value


def pair_kernel(keep, core, *outs):
    half = keep.shape[1] // 2
    for part in range(2):
        slots = slice(part * half, (part + 1) * half)
        for column in range(2):
            outs[2 * part + column][...] = (
                keep[column, slots].astype(F32) + core[column, slots].astype(F32)
            ).astype(BF)


def pair_add(keep, core):
    count, size, width = keep.shape[1:]
    return pl.pallas_call(
        pair_kernel,
        out_shape=(jax.ShapeDtypeStruct((count // 2, size, width), BF),) * 4,
        compiler_params=pltpu.CompilerParams(vmem_limit_bytes=VMEM * MIB),
        cost_estimate=cost(0, 0),
        name="pair_add",
    )(keep, core)


def split_kernel(left_one, right_one, left_two, right_two, *outs):
    width = left_one.shape[2]
    for index, out in enumerate(outs):
        out[:, :width] = (left_one[index].astype(F32) + right_one[index].astype(F32)).astype(BF)
        out[:, width:] = (left_two[index].astype(F32) + right_two[index].astype(F32)).astype(BF)


def split_add(one, two):
    count, size, width = one[0].shape
    total = width + two[0].shape[2]
    return pl.pallas_call(
        split_kernel,
        out_shape=(jax.ShapeDtypeStruct((size, total), BF),) * count,
        compiler_params=pltpu.CompilerParams(vmem_limit_bytes=VMEM * MIB),
        cost_estimate=cost(0, 0),
        name="split_add",
    )(*one, *two)


def low_kernel(left, right, out):
    out[...] = (left[...].astype(F32) + right[...].astype(F32)).astype(out.dtype)


def low_add(left, right):
    return pl.pallas_call(
        low_kernel,
        out_shape=jax.ShapeDtypeStruct(left.shape, BF),
        compiler_params=pltpu.CompilerParams(vmem_limit_bytes=VMEM * MIB),
        cost_estimate=cost(0, 0),
        name="low_add",
    )(left, right)


def chosen_kernel(flags, first, second, up_in, down_in, up, down):
    one, two = first[...].astype(F32), second[...].astype(F32)
    up[...] = (jnp.where(flags[0] > 0, one, two) + up_in[...].astype(F32)).astype(BF)
    down[...] = (jnp.where(flags[1] > 0, one, two) + down_in[...].astype(F32)).astype(BF)


def chosen_add(flags, first, second, up_in, down_in):
    shape = jax.ShapeDtypeStruct(first.shape, BF)
    vmem = pl.BlockSpec(memory_space=pltpu.VMEM)
    return pl.pallas_call(
        chosen_kernel,
        out_shape=(shape, shape),
        in_specs=[pl.BlockSpec(memory_space=pltpu.SMEM)] + [vmem] * 4,
        out_specs=(vmem, vmem),
        compiler_params=pltpu.CompilerParams(vmem_limit_bytes=VMEM * MIB),
        cost_estimate=cost(0, 0),
        name="chosen_add",
    )(flags, first, second, up_in, down_in)


def reduce_rows(paired, count, first_wait, last_wait):
    length = count // 4
    line = lax.axis_index("dp") // 4
    pairs = [(i, i ^ 2) for i in range(count)]
    over = lambda value: lax.ppermute(value, "dp", pairs)
    (mine_one, theirs_one, mine_two, theirs_two), (down_one, far_one, down_two, far_two) = paired
    others, first_wait = pin(((over(theirs_one), over(far_one)), first_wait))
    sums = list(split_add((mine_one, others[0]), (down_one, others[1])))
    others = (over(theirs_two), over(far_two))
    above = below = None
    for step in range(1, length):
        gap = length - step
        slots = lambda towards: [
            length - 1 - (here ^ (here + towards)) if 0 <= here + towards < length else None
            for here in range(length)
        ]
        ups, downs = slots(gap), slots(-gap)
        used = sorted({slot for slot in ups + downs if slot is not None})
        if len(used) == 1 and step == 1:
            up = down = sums[used[0]]
        elif len(used) == 1:
            one = sums[used[0]]
            up, down = chosen_add(jnp.ones((2,), jnp.int32), one, one, below, above)
        elif len(used) == 2:
            flags = jnp.stack(
                [
                    choose(line, [jnp.int32(slot == used[0]) for slot in side])
                    for side in (ups, downs)
                ]
            )
            up, down = chosen_add(flags, sums[used[0]], sums[used[1]], below, above)
        else:
            fill = lambda side: [sums[used[0] if slot is None else slot] for slot in side]
            up, down = choose(line, fill(ups)), choose(line, fill(downs))
            up, down = low_add(up, below), low_add(down, above)
        if step == length - 1:
            up, down, last_wait = pin((up, down, last_wait))
        below = lax.ppermute(up, "dp", [(i, i + 4) for i in range(count - 4) if i // 4 + gap < length])
        above = lax.ppermute(down, "dp", [(i, i - 4) for i in range(4, count) if i // 4 >= gap])
        if step == length // 2 - 1:
            below, above, others = pin((below, above, others))
            sums += split_add((mine_two, others[0]), (down_two, others[1]))
    return sums[-1], below, above, first_wait, last_wait


def interleave_kernel(info, *refs):
    pieces, out = refs[:4], refs[4]
    size = out.shape[0] // (4 * pieces[0].shape[0])
    length = pieces[0].shape[0]
    for index, piece in enumerate(pieces):
        side = info[3] if index % 2 == 0 else 1 - info[3]
        core = info[0] if index // 2 == 0 else 1 - info[0]
        for line in range(length):
            start = pl.multiple_of((line * 4 + side * 2 + core) * size, size)
            out[pl.ds(start, size), :] = piece[line]


def interleave(info, pieces, size):
    width = pieces[0].shape[1]
    pieces = [piece.reshape(-1, size, width) for piece in pieces]
    vmem = pl.BlockSpec(memory_space=pltpu.VMEM)
    return pl.pallas_call(
        interleave_kernel,
        out_shape=pltpu.VMEM((D, width), BF),
        in_specs=[pl.BlockSpec(memory_space=pltpu.SMEM)] + [vmem] * 4,
        out_specs=vmem,
        compiler_params=pltpu.CompilerParams(vmem_limit_bytes=VMEM * MIB),
        cost_estimate=cost(0, 0),
        name="interleave",
    )(info, *pieces)


def gain_kernel(own, other, gain, first, second, first_out, second_out, gain_out):
    low = gain[...].astype(BF).astype(F32)
    results = adamw(gain[...], (own[...] + other[...]) / low, first[...], second[...], 0.6)
    for out, result in zip((first_out, second_out, gain_out), results):
        out[...] = result


def gain_call(own, other, gain, first, second):
    shape = jax.ShapeDtypeStruct(gain.shape, F32)
    return pl.pallas_call(
        gain_kernel,
        out_shape=(shape, shape, shape),
        compiler_params=pltpu.CompilerParams(vmem_limit_bytes=VMEM * MIB),
        cost_estimate=cost(0, 0),
        name="gains",
    )(own, other, gain, first, second)


def shard_kernel(qkv, gains, out):
    width = qkv.shape[2]
    for part in range(3):
        out[:, part * width : (part + 1) * width] = qkv[part].astype(BF)
    rows = jnp.concatenate([gains[...], jnp.zeros((HEAD_DIM - 2, gains.shape[1]), F32)])
    out[:, 3 * width :] = rows.T.astype(BF)


def shard_call(qkv, gains):
    total = 3 * qkv.shape[2] + HEAD_DIM
    return pl.pallas_call(
        shard_kernel,
        out_shape=jax.ShapeDtypeStruct((qkv.shape[1], total), BF),
        compiler_params=pltpu.CompilerParams(vmem_limit_bytes=VMEM * MIB),
        cost_estimate=cost(0, 0),
        name="shard",
    )(qkv, gains)


def pin(values):
    return lax.optimization_barrier(values)


def body(
    tokens,
    cotangent,
    proj_qkv,
    proj_out,
    proj_gate_up,
    proj_down,
    norm_gains,
    first_qkv,
    first_out,
    first_gate_up,
    first_down,
    first_gains,
    second_qkv,
    second_out,
    second_gate_up,
    second_down,
    second_gains,
    cache,
    doc_segments,
    padding,
    retrieval,
):
    rows = tokens.shape[0]
    count = lax.axis_size("dp")
    device = lax.axis_index("dp")
    group = lax.axis_index("mp")
    rank = device % 2
    segment = device // 2
    shard = proj_qkv.shape[1]
    local = proj_qkv.shape[2]
    hidden_here = proj_gate_up.shape[2]
    core_pairs = [(i, i ^ 1) for i in range(count)]

    def across(value):
        return lax.ppermute(value, "mp", [(0, 1), (1, 0)])

    def beside(value):
        return lax.ppermute(value, "dp", core_pairs)

    shard_one = shard_call(proj_qkv, norm_gains)
    out_own = proj_out.astype(BF).T
    out_other = across(out_own)
    shard_two = jnp.concatenate(
        [
            proj_gate_up[0].astype(BF),
            proj_gate_up[1].astype(BF),
            proj_down.astype(BF).T,
            jnp.where(group == 0, out_own, out_other),
            jnp.where(group == 0, out_other, out_own),
        ],
        axis=1,
    )
    length = count // 4
    lines = [[i for i in range(count) if i % 4 == lane] for lane in range(4)]
    own_column = lax.all_gather(shard_one, "dp", axis=0, tiled=True, axis_index_groups=lines)
    next_column = lax.ppermute(own_column, "dp", [(i, i ^ 2) for i in range(count)])
    weights_two = lax.all_gather(shard_two, "dp", axis=0, tiled=True)

    places = jnp.arange(SEG, dtype=jnp.int32)
    starts = jnp.cumsum(doc_segments) - doc_segments
    memory_on = jnp.logical_not(jnp.any(starts == segment))
    side = (device // 2) % 2
    info = jnp.stack([rank, group, memory_on.astype(jnp.int32), side, device // 4]).astype(jnp.int32)
    cosines, sines = rope_tables(places)
    valid = lax.dynamic_slice_in_dim(padding, segment * SEG, SEG)
    lane = jnp.arange(HEAD_DIM, dtype=jnp.int32)[None, :]
    bias = jnp.where((valid[:, None] == 0) & (lane == 0), NEGATIVE, 0.0).astype(BF)
    fetched = cache[retrieval[0]].reshape(RETR, 2, 2, 2, HEAD_DIM).transpose(2, 1, 3, 0, 4)
    mem_own = lax.dynamic_index_in_dim(fetched, rank, keepdims=False)
    mem_other = beside(lax.dynamic_index_in_dim(fetched, 1 - rank, keepdims=False))
    next_column, mem_own, mem_other, bias, cosines, sines, info = pin(
        (next_column, mem_own, mem_other, bias, cosines, sines, info)
    )
    pieces = (own_column, next_column, beside(own_column), beside(next_column))
    weights_one = interleave(info, pieces, shard)

    send, normed_one, gains = project_first(info, tokens, weights_one, cosines, sines)
    gain_one, gain_two = gains[0:1], gains[1:2]
    other = beside(send)
    own = project_second(info, normed_one, weights_one, cosines, sines)
    out_keep, out_send, turned, logs = attend_forward(info, own, other, mem_own, mem_other, bias)
    out_recv = beside(out_send)
    pieces = (out_keep, out_recv, across(out_keep), across(out_recv))
    middle, normed_two, attended = middle_call(info, pieces, tokens, weights_two, gain_two)

    earlier, backs, backs_other = (), [], []
    for chunk, first in enumerate(range(0, rows, TILE)):
        if first + TILE == rows:
            earlier, backs_other[0] = pin((earlier, backs_other[0]))
        *earlier, back = feed_call(normed_two, cotangent, weights_two, first, TILE, earlier)
        backs.append(back)
        backs_other.append(across(back))
    hidden, grad_gate, grad_up, feed_part = earlier
    feed_grads, down_keep, down_send = feed_weight_call(
        info, normed_two, cotangent, hidden, grad_gate, grad_up, shard
    )
    feed_other = across(feed_part)
    backs[0], _ = pin((backs[0], feed_grads))
    earlier = ()
    for chunks in ((0, 1), (2,), (3,)):
        earlier = residual_call(
            info, middle, [backs[index] for index in chunks], [backs_other[index] for index in chunks],
            cotangent, gain_two, weights_two, chunks[0], earlier,
        )
    grad_middle, grad_low, grad_keep, *grad_sends = earlier
    grad_others = [beside(value) for value in grad_sends]

    d_keeps, d_others = [], []
    for head in range(2):
        d_keep, d_send, d_send_v = attend_backward(
            info, own, other, mem_own, mem_other, bias, grad_keep, grad_others[head], turned, logs,
            cosines, sines, head,
        )
        d_keeps.append(d_keep)
        d_others += [beside(d_send), beside(d_send_v)]
    moved = d_keeps + d_others
    back_one = back_call(info, moved, weights_one)
    moved[0], _ = pin((moved[0], back_one))
    attend_keep, attend_send = attend_weight_call(info, normed_one, grad_low, attended, moved, shard)
    back_one, feed_other = pin((back_one, feed_other))
    back_one_other = across(back_one)
    input_grad = input_call(grad_middle, back_one, back_one_other, tokens, gain_one)
    block_out = (
        middle + (feed_part.astype(F32) + feed_other.astype(F32))
    ).astype(BF)
    paired = [
        pair_add(keep, beside(send))
        for keep, send in ((attend_keep, attend_send), (down_keep, down_send))
    ]
    total, below, above, block_out, input_grad = reduce_rows(paired, count, block_out, input_grad)
    feed_sum = lax.psum_scatter(feed_grads, "dp", scatter_dimension=0, tiled=True).astype(F32)
    gate_up_sum = jnp.stack([feed_sum[:, :hidden_here], feed_sum[:, hidden_here : 2 * hidden_here]])
    gate_up_first, gate_up_second, gate_up_new = adamw(
        proj_gate_up, gate_up_sum, first_gate_up, second_gate_up, 0.5 / math.sqrt(D)
    )
    gate_up_new, total, below, above = pin((gate_up_new, total, below, above))
    attend_sum = total.astype(F32) + (below.astype(F32) + above.astype(F32))
    down_sum = jnp.concatenate([feed_sum[:, 2 * hidden_here :].T, attend_sum[:, 4 * local :].T])
    down_first, down_second, down_new = adamw(
        proj_down, down_sum, first_down, second_down, 0.5 / math.sqrt(FF)
    )
    qkv_sum = jnp.stack([attend_sum[:, part * local : (part + 1) * local] for part in range(3)])
    out_sum = attend_sum[:, 3 * local : 4 * local].T
    low_qkv, low_gate_up = proj_qkv.astype(BF).astype(F32), proj_gate_up.astype(BF).astype(F32)
    gains_sum = jnp.stack(
        [jnp.sum(low_qkv * qkv_sum, axis=(0, 2)), jnp.sum(low_gate_up * gate_up_sum, axis=(0, 2))]
    )
    gains_first, gains_second, gains_new = gain_call(
        gains_sum, across(gains_sum), norm_gains, first_gains, second_gains
    )

    qkv_first, qkv_second, qkv_new = adamw(
        proj_qkv, qkv_sum, first_qkv, second_qkv, 0.5 / math.sqrt(D)
    )
    out_first, out_second, out_new = adamw(
        proj_out, out_sum, first_out, second_out, 0.5 / math.sqrt(max(1, 4 * D // SEG))
    )
    return (
        block_out,
        input_grad,
        qkv_first,
        qkv_second,
        qkv_new,
        out_first,
        out_second,
        out_new,
        gate_up_first,
        gate_up_second,
        gate_up_new,
        down_first,
        down_second,
        down_new,
        gains_first,
        gains_second,
        gains_new,
    )


def solution(mesh):
    return jax.shard_map(
        body,
        mesh=mesh,
        in_specs=(
            P("dp", None),
            P("dp", None),
            P(None, "dp", "mp"),
            P("mp", "dp"),
            P(None, "dp", "mp"),
            P("mp", "dp"),
            P(None, "dp"),
            P(None, "dp", "mp"),
            P("mp", "dp"),
            P(None, "dp", "mp"),
            P("mp", "dp"),
            P(None, "dp"),
            P(None, "dp", "mp"),
            P("mp", "dp"),
            P(None, "dp", "mp"),
            P("mp", "dp"),
            P(None, "dp"),
            P("dp", None, "mp"),
            P(),
            P(),
            P("dp", None),
        ),
        out_specs=(
            P("dp", None),
            P("dp", None),
            P(None, "dp", "mp"),
            P(None, "dp", "mp"),
            P(None, "dp", "mp"),
            P("mp", "dp"),
            P("mp", "dp"),
            P("mp", "dp"),
            P(None, "dp", "mp"),
            P(None, "dp", "mp"),
            P(None, "dp", "mp"),
            P("mp", "dp"),
            P("mp", "dp"),
            P("mp", "dp"),
            P(None, "dp"),
            P(None, "dp"),
            P(None, "dp"),
        ),
        check_vma=False,
    )
```
